32 devices in a mesh: dp: 8 (over z, y), tensor: 4 (over x, core).
Axes of the slice: x: 2, y: 2, z: 4, core: 2. Of those that a mesh axis runs over, the one named last changes fastest.
Arguments:
- inputs: bfloat16 [16, 1024, 1280], P('dp', 'tensor'), may hold values from -6 to 6
- cotangent: bfloat16 [16, 1024, 1280], P('dp', 'tensor'), may hold values from -6 to 6
- lengths: int32 [16], P('dp'), may hold values from 128 to 1024, as said below
- adapter_pick: int32 [16, 6], P('dp'), may hold values from 0 to 7
- first_gain: float32 [1280], replicated, may hold values from 0.5 to 1.5
- first_bias: float32 [1280], replicated, may hold values from -1.5 to 1.5
- query_weight: bfloat16 [1280, 1280], P(None, 'tensor'), may hold values from -0.15625 to 0.15625
- key_weight: bfloat16 [1280, 1280], P(None, 'tensor'), may hold values from -0.15625 to 0.15625
- value_weight: bfloat16 [1280, 1280], P(None, 'tensor'), may hold values from -0.15625 to 0.15625
- output_weight: bfloat16 [1280, 1280], P('tensor'), may hold values from -0.625 to 0.625
- second_gain: float32 [1280], replicated, may hold values from 0.5 to 1.5
- second_bias: float32 [1280], replicated, may hold values from -1.5 to 1.5
- widen_weight: bfloat16 [1280, 5120], P(None, 'tensor'), may hold values from -0.15625 to 0.15625
- narrow_weight: bfloat16 [5120, 1280], P('tensor'), may hold values from -0.078125 to 0.078125
- query_inner: bfloat16 [8, 1280, 16], replicated, may hold values from -0.15625 to 0.15625
- query_outer: bfloat16 [8, 16, 1280], P(None, None, 'tensor'), may hold values from -1.5 to 1.5
- key_inner: bfloat16 [8, 1280, 16], replicated, may hold values from -0.15625 to 0.15625
- key_outer: bfloat16 [8, 16, 1280], P(None, None, 'tensor'), may hold values from -1.5 to 1.5
- value_inner: bfloat16 [8, 1280, 16], replicated, may hold values from -0.15625 to 0.15625
- value_outer: bfloat16 [8, 16, 1280], P(None, None, 'tensor'), may hold values from -1.5 to 1.5
- output_inner: bfloat16 [8, 1280, 16], P(None, 'tensor'), may hold values from -0.625 to 0.625
- output_outer: bfloat16 [8, 16, 1280], replicated, may hold values from -1.5 to 1.5
- widen_inner: bfloat16 [8, 1280, 16], replicated, may hold values from -0.15625 to 0.15625
- widen_outer: bfloat16 [8, 16, 5120], P(None, None, 'tensor'), may hold values from -1.5 to 1.5
- narrow_inner: bfloat16 [8, 5120, 16], P(None, 'tensor'), may hold values from -0.078125 to 0.078125
- narrow_outer: bfloat16 [8, 16, 1280], replicated, may hold values from -1.5 to 1.5
Outputs:
- output: bfloat16 [16, 1024, 1280], P('dp', 'tensor')
- input_grad: float32 [16, 1024, 1280], P('dp', 'tensor')
- query_inner_gradient: float32 [8, 1280, 16], replicated
- query_outer_gradient: float32 [8, 16, 1280], P(None, None, 'tensor')
- key_inner_gradient: float32 [8, 1280, 16], replicated
- key_outer_gradient: float32 [8, 16, 1280], P(None, None, 'tensor')
- value_inner_gradient: float32 [8, 1280, 16], replicated
- value_outer_gradient: float32 [8, 16, 1280], P(None, None, 'tensor')
- output_inner_gradient: float32 [8, 1280, 16], P(None, 'tensor')
- output_outer_gradient: float32 [8, 16, 1280], replicated
- widen_inner_gradient: float32 [8, 1280, 16], replicated
- widen_outer_gradient: float32 [8, 16, 5120], P(None, None, 'tensor')
- narrow_inner_gradient: float32 [8, 5120, 16], P(None, 'tensor')
- narrow_outer_gradient: float32 [8, 16, 1280], replicated
The draws below stay inside these ranges and needn't reach their ends.
Inputs may be any that keep to these rules, and one draw needn't show every extreme that they name: `lengths`: of the 2 clips that share an index of dp, one has all 1024 tokens; some clip has 128 tokens.
All inputs are finite; a program needn't handle non-finite values.
Results may differ from the reference program's by a relative error of at most 0.015.
The reference program's roundings to bfloat16 on the way count: a program that leaves them out, or rounds other values in their place, can miss the bound.
Values may be sent and summed in bfloat16 or wider, within the bound.
No kernel may reach another device: no remote copies, remote signals or barrier semaphores. Data moves between devices by JAX's collectives and lax.ppermute only.
A program may use at most 192 MiB of HBM per device.

```python
import math
import jax
import jax.numpy as jnp
from jax import lax

D = 1280
HEADS = 16
HEAD_DIM = 80
FF = 5120
RANK = 16
NADAPT = 8
SLOT = 1024
CLIP_DEV = 2
CLIPS = 16


def draw_lengths(key, part):
    key = jax.random.fold_in(key, 7)
    draw_base, draw_full, draw_short = jax.random.split(key, 3)
    groups = CLIPS // CLIP_DEV
    clip_lengths = jax.random.randint(draw_base, (CLIPS,), SLOT // 8, SLOT + 1, dtype=jnp.int32)
    offsets = jax.random.randint(draw_full, (groups,), 0, CLIP_DEV, dtype=jnp.int32)
    full_spots = jnp.arange(groups, dtype=jnp.int32) * CLIP_DEV + offsets
    clip_lengths = clip_lengths.at[full_spots].set(SLOT)
    chosen_group = jax.random.randint(draw_short, (), 0, groups, dtype=jnp.int32)
    short_spot = chosen_group * CLIP_DEV + (offsets[chosen_group] + 1) % CLIP_DEV
    return clip_lengths.at[short_spot].set(SLOT // 8).astype(jnp.int32)


def place_ends(entries, rng, low, top_value):
    index_at = [jax.random.randint(jax.random.fold_in(rng, axis), (), 0, length) for axis, length in enumerate(entries.shape)]
    widest = entries.shape.index(max(entries.shape))
    beside = index_at[:widest] + [(index_at[widest] + 1) % entries.shape[widest]] + index_at[widest + 1:]
    return entries.at[tuple(index_at)].set(low).at[tuple(beside)].set(top_value)


def shard_levels(rng, dims, cuts, least, largest):
    factor_of = 1.0
    for axis_at, blocks in cuts:
        steps = jax.random.uniform(jax.random.fold_in(jax.random.fold_in(rng, 6), axis_at), (blocks,), jnp.float32, least / len(cuts), largest / len(cuts))
        factor_of = factor_of * jnp.repeat(jnp.exp(steps), dims[axis_at] // blocks).reshape((-1,) + (1,) * (len(dims) - 1 - axis_at))
    return factor_of


def bell_draw(rng, extent, width, bound, cuts=(), kind=jnp.bfloat16):
    gain = shard_levels(rng, extent, cuts, -0.22, 0.18) if cuts else 1.0
    entries = jax.random.normal(rng, extent, jnp.float32) * width * gain
    return jnp.minimum(jnp.maximum(entries, -bound), bound).astype(kind)


def setup_inputs(seed: int = 0) -> dict:
    streams_of = jax.random.split(jax.random.key(seed), 27)
    inputs = bell_draw(streams_of[0], (CLIPS, SLOT, D), 1.0, 6.0, ((0, 8), (1, 4)))
    cotangent = bell_draw(streams_of[1], (CLIPS, SLOT, D), 1.0, 6.0, ((0, 8), (1, 4)))
    lengths = draw_lengths(jax.random.fold_in(streams_of[26], 71), 0)
    adapter_pick = place_ends(jax.random.randint(streams_of[3], (CLIPS, 6), 0, NADAPT), jax.random.fold_in(streams_of[3], 1), 0, NADAPT - 1).astype(jnp.int32)
    first_gain = jnp.clip(1.0 + 0.1 * jax.random.normal(streams_of[4], (D,), jnp.float32), 0.5, 1.5)
    first_bias = bell_draw(streams_of[5], (D,), 0.3, 1.5, (), jnp.float32)
    query_weight = bell_draw(streams_of[6], (D, HEADS * HEAD_DIM), D ** -0.5, 0.15625, ((1, 4),))
    key_weight = bell_draw(streams_of[7], (D, HEADS * HEAD_DIM), D ** -0.5, 0.15625, ((1, 4),))
    value_weight = bell_draw(streams_of[8], (D, HEADS * HEAD_DIM), D ** -0.5, 0.15625, ((1, 4),))
    output_weight = bell_draw(streams_of[9], (HEADS * HEAD_DIM, D), (HEADS * HEAD_DIM // 16) ** -0.5, 0.625, ((0, 4),))
    second_gain = jnp.clip(1.0 + 0.1 * jax.random.normal(streams_of[10], (D,), jnp.float32), 0.5, 1.5)
    second_bias = bell_draw(streams_of[11], (D,), 0.3, 1.5, (), jnp.float32)
    widen_weight = bell_draw(streams_of[12], (D, FF), D ** -0.5, 0.15625, ((1, 4),))
    narrow_weight = bell_draw(streams_of[13], (FF, D), FF ** -0.5, 0.078125, ((0, 4),))
    query_inner = bell_draw(streams_of[14], (NADAPT, D, RANK), D ** -0.5, 0.15625)
    query_outer = bell_draw(streams_of[15], (NADAPT, RANK, HEADS * HEAD_DIM), RANK ** -0.5, 1.5, ((2, 4),))
    key_inner = bell_draw(streams_of[16], (NADAPT, D, RANK), D ** -0.5, 0.15625)
    key_outer = bell_draw(streams_of[17], (NADAPT, RANK, HEADS * HEAD_DIM), RANK ** -0.5, 1.5, ((2, 4),))
    value_inner = bell_draw(streams_of[18], (NADAPT, D, RANK), D ** -0.5, 0.15625)
    value_outer = bell_draw(streams_of[19], (NADAPT, RANK, HEADS * HEAD_DIM), RANK ** -0.5, 1.5, ((2, 4),))
    output_inner = bell_draw(streams_of[20], (NADAPT, HEADS * HEAD_DIM, RANK), (HEADS * HEAD_DIM // 16) ** -0.5, 0.625, ((1, 4),))
    output_outer = bell_draw(streams_of[21], (NADAPT, RANK, D), RANK ** -0.5, 1.5)
    widen_inner = bell_draw(streams_of[22], (NADAPT, D, RANK), D ** -0.5, 0.15625)
    widen_outer = bell_draw(streams_of[23], (NADAPT, RANK, FF), RANK ** -0.5, 1.5, ((2, 4),))
    narrow_inner = bell_draw(streams_of[24], (NADAPT, FF, RANK), FF ** -0.5, 0.078125, ((1, 4),))
    narrow_outer = bell_draw(streams_of[25], (NADAPT, RANK, D), RANK ** -0.5, 1.5)
    return dict(inputs=inputs, cotangent=cotangent, lengths=lengths, adapter_pick=adapter_pick, first_gain=first_gain, first_bias=first_bias, query_weight=query_weight, key_weight=key_weight, value_weight=value_weight, output_weight=output_weight, second_gain=second_gain, second_bias=second_bias, widen_weight=widen_weight, narrow_weight=narrow_weight, query_inner=query_inner, query_outer=query_outer, key_inner=key_inner, key_outer=key_outer, value_inner=value_inner, value_outer=value_outer, output_inner=output_inner, output_outer=output_outer, widen_inner=widen_inner, widen_outer=widen_outer, narrow_inner=narrow_inner, narrow_outer=narrow_outer)


@jax.custom_vjp
def low(v):
    return lax.optimization_barrier(v.astype(jnp.bfloat16)).astype(jnp.float32)

@jax.custom_vjp
def low_back(v):
    return v

def low_keep(v):
    return (low(v), None)

def low_pass(kept, grad):
    return (grad,)

def back_keep(v):
    return (v, None)

def back_low(kept, grad):
    return (low(grad),)
low.defvjp(low_keep, low_pass)
low_back.defvjp(back_keep, back_low)
highest = lax.Precision.HIGHEST

def normalize(states, norm_gain, norm_shift):
    centre = states - lax.optimization_barrier(jnp.mean(states, axis=-1, keepdims=True))
    return centre * lax.rsqrt(lax.optimization_barrier(jnp.mean(centre * centre, axis=-1, keepdims=True)) + 1e-05) * norm_gain + norm_shift

def project(source, weight, inner_factor, outer_factor):
    lowrank = jnp.dot(source, inner_factor, precision=highest)
    return jnp.dot(source, weight, precision=highest) + jnp.dot(lowrank, outer_factor, precision=highest)

def clip_layer(states, length, picked, frozen, adapters):
    first_gain, first_bias, query_weight, key_weight, value_weight, output_weight, second_gain, second_bias, widen_weight, narrow_weight = frozen
    picked_hot = (picked[:, None] == jnp.arange(NADAPT)).astype(jnp.float32)
    chosen = [jnp.tensordot(picked_hot[number // 2], adapters[number], axes=1, precision=highest) for number in range(12)]
    clip_slots = states.shape[0]
    key_live = jnp.arange(clip_slots) < length
    row_mask = key_live.astype(jnp.float32)[:, None]
    first_rows = low(normalize(states, first_gain, first_bias))
    queries = low(low_back(project(first_rows, query_weight, chosen[0], chosen[1])))
    key_rows = low(low_back(project(first_rows, key_weight, chosen[2], chosen[3])))
    values = low(low_back(project(first_rows, value_weight, chosen[4], chosen[5])))
    head_shape = (clip_slots, HEADS, HEAD_DIM)
    scores = jnp.einsum('qhd,khd->hqk', queries.reshape(head_shape), key_rows.reshape(head_shape), precision=highest) * (1.0 / math.sqrt(HEAD_DIM))
    scores = low_back(jnp.where(key_live[None, None, :], scores, -1000000000.0))
    row_top = lax.optimization_barrier(jnp.max(scores, axis=-1, keepdims=True))
    log_total = jnp.log(lax.optimization_barrier(jnp.sum(jnp.exp(scores - row_top), axis=-1, keepdims=True))) + row_top
    soft_weights = low(jnp.exp(scores - log_total))
    context = jnp.einsum('hqk,khd->qhd', soft_weights, values.reshape(head_shape), precision=highest).reshape(clip_slots, HEADS * HEAD_DIM)
    context = low(low_back(context))
    attended = low_back(project(context, output_weight, chosen[6], chosen[7]))
    hidden = states + row_mask * attended
    second_rows = low(normalize(hidden, second_gain, second_bias))
    widened = low_back(project(second_rows, widen_weight, chosen[8], chosen[9]))
    activated = low(jax.nn.gelu(widened))
    branch = low_back(project(activated, narrow_weight, chosen[10], chosen[11]))
    return hidden + row_mask * branch

def reference(inputs, cotangent, lengths, adapter_pick, first_gain, first_bias, query_weight, key_weight, value_weight, output_weight, second_gain, second_bias, widen_weight, narrow_weight, query_inner, query_outer, key_inner, key_outer, value_inner, value_outer, output_inner, output_outer, widen_inner, widen_outer, narrow_inner, narrow_outer):
    frozen = tuple((weight.astype(jnp.float32) for weight in (first_gain, first_bias, query_weight, key_weight, value_weight, output_weight, second_gain, second_bias, widen_weight, narrow_weight)))
    adapters = tuple((weight.astype(jnp.float32) for weight in (query_inner, query_outer, key_inner, key_outer, value_inner, value_outer, output_inner, output_outer, widen_inner, widen_outer, narrow_inner, narrow_outer)))

    def forward(states, factors):
        clip_run = jax.checkpoint(lambda clip_states, length, picked: clip_layer(clip_states, length, picked, frozen, factors))
        return lax.map(lambda clip_items: clip_run(*clip_items), (states, lengths, adapter_pick))
    output, pullback = jax.vjp(forward, inputs.astype(jnp.float32), adapters)
    input_grad, factor_grads = pullback(cotangent.astype(jnp.float32))
    return (output.astype(jnp.bfloat16), input_grad, factor_grads[0], factor_grads[1], factor_grads[2], factor_grads[3], factor_grads[4], factor_grads[5], factor_grads[6], factor_grads[7], factor_grads[8], factor_grads[9], factor_grads[10], factor_grads[11])
```

```python
import functools
import math

import jax
import jax.numpy as jnp
from jax import lax
from jax.experimental import pallas as pl
from jax.experimental.pallas import tpu as pltpu
from jax.sharding import PartitionSpec as P

HEAD_DIM = 80
f32 = jnp.float32
bf16 = jnp.bfloat16
neg_fill = -1000000000.0
score_scale = 1.0 / math.sqrt(HEAD_DIM)
log2_e = math.log2(math.e)


def swap(array, axis, bits, size):
    return lax.ppermute(array, axis, [(i, i ^ bits) for i in range(size)])


def nn(a, b):
    return jnp.dot(a, b, preferred_element_type=f32)


def nt(a, b):
    return lax.dot_general(a, b, (((1,), (1,)), ((), ())), preferred_element_type=f32)


def tn(a, b):
    return lax.dot_general(a, b, (((0,), (0,)), ((), ())), preferred_element_type=f32)


def halves(low):
    top = low.astype(bf16)
    return jnp.concatenate([top, (low - top.astype(f32)).astype(bf16)], axis=0)


def twice(factor):
    return jnp.concatenate([factor, factor], axis=0)


def folded(pair):
    count = pair.shape[0] // 2
    return pair[:count] + pair[count:]


def normalize(states, gain, shift):
    centre = states - jnp.mean(states, axis=-1, keepdims=True)
    scaled = lax.rsqrt(jnp.mean(centre * centre, axis=-1, keepdims=True) + 1e-05)
    unit = centre * scaled
    return unit * gain + shift, unit, scaled


def normalize_back(grad_rows, unit, scaled, gain):
    grad_unit = grad_rows * gain
    return scaled * (
        grad_unit
        - jnp.mean(grad_unit, axis=-1, keepdims=True)
        - unit * jnp.mean(grad_unit * unit, axis=-1, keepdims=True)
    )


def live_column(spot_ref, length_ref, rows, bits):
    iota = lax.broadcasted_iota(jnp.int32, (2 * rows, 1), 0)
    place = spot_ref[3]
    first, second = place ^ bits[0], place ^ bits[1]
    position = jnp.where(iota < rows, first * rows + iota, second * rows + iota - rows)
    return position < length_ref[spot_ref[0]]


def whole(shape):
    return pl.BlockSpec(shape, lambda *_: (0,) * len(shape), pipeline_mode=pl.Buffered(1))


def placed_block(shape, index):
    return pl.BlockSpec(shape, index, pipeline_mode=pl.Buffered(1))


def call(body, scalars, operands, specs, outs, out_specs, grid=(1,), scratch=(), cost=(0, 0, 0), limit=58):
    return pl.pallas_call(
        body,
        grid_spec=pltpu.PrefetchScalarGridSpec(
            num_scalar_prefetch=len(scalars),
            grid=grid,
            in_specs=specs,
            out_specs=out_specs,
            scratch_shapes=list(scratch),
        ),
        out_shape=outs,
        cost_estimate=pl.CostEstimate(
            flops=int(cost[0]), bytes_accessed=int(cost[1]), transcendentals=int(cost[2])
        ),
        compiler_params=pltpu.CompilerParams(vmem_limit_bytes=limit * 2**20),
    )(*scalars, *operands)


def shaped(shape, dtype):
    return jax.ShapeDtypeStruct(shape, dtype)


def of_mine(number):
    return lambda i, spot, pick, *_: (pick[spot[0], number], 0, 0)


def of_other(number):
    return lambda i, spot, pick, *_: (pick[spot[1], number], 0, 0)


def stage(spot, pick, inputs, factors):
    rows, features = inputs.shape[1:]
    rank = factors[0].shape[1]

    def body(spot_ref, pick_ref, inputs_ref, *refs):
        send_ref, pack_ref = refs[12:]
        send_ref[:rows] = inputs_ref[0]
        for group, ref, base in ((refs[:6], pack_ref, 0), (refs[6:12], send_ref, rows)):
            ref[base : base + rank] = jnp.concatenate([r[0] for r in group[:4]], axis=1)
            ref[base + rank : base + 2 * rank] = group[4][0]
            ref[base + 2 * rank : base + 3 * rank] = group[5][0]

    specs = [placed_block((1, rows, features), lambda i, spot, *_: (spot[1], 0, 0))]
    for of in (of_mine, of_other):
        specs += [placed_block((1,) + f.shape[1:], of(n)) for n, f in enumerate(factors)]
    outs = [shaped((rows + 3 * rank, features), bf16), shaped((3 * rank, features), bf16)]
    return call(
        body, (spot, pick), [inputs] + factors * 2, specs, outs, [whole(o.shape) for o in outs],
        cost=(0, 4e6, 0),
    )


def stage_weights(spot, pick, heads, dense, cotangent):
    features = heads[0].shape[1]
    head_rows = heads[0].shape[0] // 4
    dense_rows = dense[0].shape[0] // 4
    rows = cotangent.shape[1]

    def body(spot_ref, pick_ref, *refs):
        ins, (heads_ref, wide_ref, thin_ref, cot_ref) = refs[:7], refs[7:]
        for n in range(4):
            heads_ref[n] = ins[n][...]
        wide_ref[...] = ins[4][...]
        thin_ref[...] = ins[5][...]
        cot_ref[...] = ins[6][0]

    part = lambda i, spot, *_: (spot[2], 0)
    specs = [placed_block((head_rows, features), part)] * 4
    specs += [placed_block((dense_rows, features), part)] * 2
    specs += [placed_block((1, rows, features), lambda i, spot, *_: (spot[1], 0, 0))]
    outs = [
        shaped((4, head_rows, features), bf16),
        shaped((dense_rows, features), bf16),
        shaped((dense_rows, features), bf16),
        shaped((rows, features), bf16),
    ]
    return call(
        body, (spot, pick), heads + dense + [cotangent], specs, outs, [whole(o.shape) for o in outs],
        cost=(0, 6e6, 0),
    )


def project_rows(weight, rows_in, outer, low):
    return (nt(weight, rows_in) + tn(twice(outer), halves(low))).astype(bf16)


def project_near(spot, pick, inputs, received, gain, shift, inners, pack, side, weights):
    rows, features = inputs.shape[1:]
    tokens = 2 * rows
    width = weights[0].shape[0]
    rank = inners[0].shape[1]

    def body(spot_ref, pick_ref, xa, xb, gain_ref, shift_ref, iq, ik, iv, pack_ref, side_ref, *refs):
        ws, (z_ref, low_ref, q_ref, kv_ref) = refs[:6], refs[6:]
        states = jnp.concatenate([xa[0], xb[...]], axis=0).astype(f32)
        z = normalize(states, gain_ref[...], shift_ref[...])[0].astype(bf16)
        z_ref[...] = z
        low = nt(jnp.concatenate([iq[0], ik[0], iv[0]], axis=0), z)
        low_ref[...] = low
        for i, packs in enumerate((pack_ref, side_ref)):
            for n in range(3):
                outer = packs[:rank, n * width : (n + 1) * width]
                y = project_rows(
                    ws[3 * i + n][...], z_ref[...], outer, low[n * rank : (n + 1) * rank]
                )
                if n == 0:
                    q_ref[i] = y
                else:
                    kv_ref[i, n - 1] = y

    specs = [
        placed_block((1, rows, features), lambda i, spot, *_: (spot[0], 0, 0)),
        whole((rows, features)),
        whole((1, features)),
        whole((1, features)),
    ]
    specs += [placed_block((1, rank, features), of_mine(n)) for n in range(3)]
    specs += [whole(pack.shape), whole(side.shape)] + [whole((width, features))] * 6
    outs = [
        shaped((tokens, features), bf16),
        shaped((3 * rank, tokens), f32),
        shaped((2, width, tokens), bf16),
        shaped((2, 2, width, tokens), bf16),
    ]
    return call(
        body,
        (spot, pick),
        [inputs, received, gain, shift] + inners + [pack, side] + weights,
        specs,
        outs,
        [whole(o.shape) for o in outs],
        cost=(2 * tokens * features * width * 6, 1e7, tokens),
    )


def project_far(spot, pick, z, low, received, side, parts):
    tokens, features = z.shape
    head_rows = parts[0][0].shape[1]
    width = 4 * head_rows
    rank = low.shape[0] // 3
    base = received.shape[0] - 3 * rank
    flat = [p for group in parts for p in group]

    def body(spot_ref, pick_ref, z_ref, low_ref, received_ref, side_ref, *refs):
        ins, (weight_ref, q_ref, kv_ref) = refs[:10], refs[10:]
        for i in range(2):
            group = ins[5 * i : 5 * i + 5]
            for n in range(4):
                for r in range(4):
                    at = pl.ds(pl.multiple_of((spot_ref[2] ^ r) * head_rows, 16), head_rows)
                    if r < 3:
                        weight_ref[i, n, at] = group[r][n]
                    else:
                        weight_ref[i, n, at] = group[3 + n // 2][n % 2]
        for i in range(2):
            for n in range(3):
                lanes = slice(n * width, (n + 1) * width)
                if i == 0:
                    outer = received_ref[base : base + rank, lanes]
                else:
                    outer = side_ref[3 * rank : 4 * rank, lanes]
                y = project_rows(
                    weight_ref[i, n], z_ref[...], outer, low_ref[n * rank : (n + 1) * rank]
                )
                if n == 0:
                    q_ref[i] = y
                else:
                    kv_ref[i, n - 1] = y

    operands = [z, low, received, side] + flat
    outs = [
        shaped((2, 4, width, features), bf16),
        shaped((2, width, tokens), bf16),
        shaped((2, 2, width, tokens), bf16),
    ]
    return call(
        body,
        (spot, pick),
        operands,
        [whole(o.shape) for o in operands],
        outs,
        [whole(o.shape) for o in outs],
        cost=(2 * tokens * features * width * 6, 2e7, 0),
    )


def attend(spot, lengths, q, kv, kv_side):
    _, width, tokens = q.shape
    rows = tokens // 2
    pair = 2 * HEAD_DIM
    steps = width // pair

    def body(spot_ref, length_ref, q_ref, k1, k2, v1, v2, ctx_ref, total_ref):
        bias1 = jnp.where(live_column(spot_ref, length_ref, rows, (0, 2)), 0.0, neg_fill * log2_e)
        bias2 = jnp.where(live_column(spot_ref, length_ref, rows, (1, 3)), 0.0, neg_fill * log2_e)
        for h in range(2):
            at = slice(h * HEAD_DIM, (h + 1) * HEAD_DIM)
            query = q_ref[0, at]
            s1 = tn(k1[0, 0, at], query) * (score_scale * log2_e) + bias1
            s2 = tn(k2[0, 0, at], query) * (score_scale * log2_e) + bias2
            top = jnp.maximum(jnp.max(s1, axis=0, keepdims=True), jnp.max(s2, axis=0, keepdims=True))
            p1 = jnp.exp2(s1 - top)
            p2 = jnp.exp2(s2 - top)
            total = jnp.sum(p1, axis=0, keepdims=True) + jnp.sum(p2, axis=0, keepdims=True)
            context = nn(v1[0, 0, at], p1.astype(bf16)) + nn(v2[0, 0, at], p2.astype(bf16))
            ctx_ref[0, at] = (context * (1.0 / total)).astype(bf16)
            total_ref[h] = top + jnp.log2(total)

    def own(n):
        return pl.BlockSpec((1, 1, pair, tokens), lambda h, *_: (h // steps, n, h % steps, 0))

    def beside(n):
        return pl.BlockSpec((1, 1, pair, tokens), lambda h, *_: (1 - h // steps, n, h % steps, 0))

    rows_spec = pl.BlockSpec((1, pair, tokens), lambda h, *_: (h // steps, h % steps, 0))
    return call(
        body,
        (spot, lengths),
        [q, kv, kv_side, kv, kv_side],
        [rows_spec, own(0), beside(0), own(1), beside(1)],
        [shaped(q.shape, bf16), shaped((4 * steps, 1, tokens), f32)],
        [rows_spec, pl.BlockSpec((2, 1, tokens), lambda h, *_: (h, 0, 0))],
        grid=(2 * steps,),
        cost=(2 * 2 * 2 * width * 256 // HEAD_DIM * tokens * 2 * tokens, 6e6, 0),
    )


def attend_back(spot, lengths, q, kv, kv_side, grad_context, totals, deltas, which):
    _, width, tokens = q.shape
    rows = tokens // 2
    pair = 2 * HEAD_DIM
    steps = width // pair

    def body(spot_ref, length_ref, q_ref, k1, k2, v1, v2, g_ref, total_ref, delta_ref, gq, own_ref, other_ref):
        bias1 = jnp.where(live_column(spot_ref, length_ref, rows, (0, 2)), 0.0, neg_fill * log2_e)
        bias2 = jnp.where(live_column(spot_ref, length_ref, rows, (1, 3)), 0.0, neg_fill * log2_e)
        for h in range(2):
            at = slice(h * HEAD_DIM, (h + 1) * HEAD_DIM)
            query = q_ref[0, at]
            grad = g_ref[0, at]
            grad_query = None
            for k, v, bias, out in ((k1, v1, bias1, own_ref), (k2, v2, bias2, other_ref)):
                s = tn(k[0, 0, at], query) * (score_scale * log2_e) + bias
                soft = jnp.exp2(s - total_ref[h])
                grad_soft = tn(v[0, 0, at], grad)
                grad_scores = (soft * (grad_soft - delta_ref[h])).astype(bf16)
                part = nn(k[0, 0, at], grad_scores)
                grad_query = part if grad_query is None else grad_query + part
                out[0, 0, at] = nt(query, grad_scores) * score_scale
                out[0, 1, at] = nt(grad, soft.astype(bf16))
            gq[0, at] = (grad_query * score_scale).astype(bf16)

    def own(n):
        return pl.BlockSpec((1, 1, pair, tokens), lambda h, *_: (h // steps, n, h % steps, 0))

    def beside(n):
        return pl.BlockSpec((1, 1, pair, tokens), lambda h, *_: (1 - h // steps, n, h % steps, 0))

    rows_spec = pl.BlockSpec((1, pair, tokens), lambda h, *_: (h // steps, h % steps, 0))
    grads_spec = pl.BlockSpec((1, pair, tokens), lambda h, *_: (2 * which + h // steps, h % steps, 0))
    line = pl.BlockSpec((2, 1, tokens), lambda h, *_: (h, 0, 0))
    line_at = pl.BlockSpec((2, 1, tokens), lambda h, *_: (2 * steps * which + h, 0, 0))
    both = pl.BlockSpec((1, 2, pair, tokens), lambda h, *_: (h // steps, 0, h % steps, 0))
    return call(
        body,
        (spot, lengths),
        [q, kv, kv_side, kv, kv_side, grad_context, totals, deltas],
        [rows_spec, own(0), beside(0), own(1), beside(1), grads_spec, line, line_at],
        [shaped(q.shape, bf16), shaped(kv.shape, f32), shaped(kv.shape, f32)],
        [rows_spec, both, both],
        grid=(2 * steps,),
        cost=(5 * 2 * 2 * width * 256 // HEAD_DIM * tokens * 2 * tokens, 2e7, 0),
    )


cubic = 0.044715
root = math.sqrt(2.0 / math.pi)


def feed_quarter(z_ref, gy_ref, wide_ref, thin_ref, outer_ref, inner_ref, rows_at, low_w, low_n, act_ref, grad_ref):
    features = wide_ref.shape[0]
    units = wide_ref.shape[1]
    block = 256
    outer_at, inner_at, rank = rows_at
    low_w2, low_n2 = halves(low_w), halves(low_n)

    def step(b, carry):
        at = pl.ds(pl.multiple_of(b * block, block), block)
        widened = nn(z_ref[...], wide_ref[:, at]) + tn(low_w2, twice(outer_ref[pl.ds(outer_at, rank), at]))
        grad = nt(gy_ref[...], thin_ref[at, :]) + tn(low_n2, twice(inner_ref[pl.ds(inner_at, rank), at]))
        square = widened * widened
        bend = jnp.tanh(root * widened * (1.0 + cubic * square))
        up = 0.5 * (1.0 + bend)
        act_ref[:, at] = (widened * up).astype(bf16)
        slope = up + widened * (0.5 * root) * (1.0 - bend * bend) * (1.0 + 3.0 * cubic * square)
        grad_ref[:, at] = (grad * slope).astype(bf16)
        return carry

    lax.fori_loop(0, units // block, step, 0)


def feed_sums(wide_ref, thin_ref, outer, inner, low_w, low_n, act_ref, grad_ref, sums_ref):
    branch = nn(act_ref[...], thin_ref[...])
    grad_second = nt(grad_ref[...], wide_ref[...])
    low_next = nt(inner, act_ref[...])
    grad_low = nt(outer, grad_ref[...])
    rank = outer.shape[0]
    sums_ref[:rank] = folded(nn(halves(low_w), grad_ref[...]))
    sums_ref[rank:] = folded(nn(halves(low_n), act_ref[...]))
    return branch, grad_second, low_next, grad_low


def feed_near(spot, pick, lengths, contexts, outs_w, far, packs, tables, inputs, received, cotangent, cot_side, gain, shift, dense):
    rows, features = inputs.shape[1:]
    tokens = 2 * rows
    width = contexts[0].shape[1]
    rank = tables[0].shape[1]
    pack, side = packs
    base = received.shape[0] - 3 * rank
    units = dense[0].shape[1]

    def body(spot_ref, pick_ref, length_ref, c01, c23, wo0, wo1, far_ref, pack_ref, side_ref, received_ref, oo, wi, no, xa, ca, cb, gain_ref, shift_ref, *refs):
        hbm, (hidden_ref, z_ref, gy_ref, branch_ref, second_ref, lows_ref, sums_ref) = refs[:4], refs[4:11]
        wide0, thin0, wide1, thin1, act_ref, grad_ref, sems = refs[11:]
        local = (wide0, thin0, wide1, thin1)
        copies = [pltpu.make_async_copy(hbm[n], local[n], sems.at[n]) for n in range(4)]
        for c in copies:
            c.start()
        states = jnp.concatenate([xa[0], received_ref[:rows]], axis=0).astype(f32)
        mask = live_column(spot_ref, length_ref, rows, (0, 2)).astype(f32)
        low_o = jnp.zeros((rank, tokens), f32)
        attended = jnp.zeros((tokens, features), f32)
        inner_lanes = slice(3 * width, 4 * width)
        inner_o = [
            pack_ref[:rank, inner_lanes],
            side_ref[:rank, inner_lanes],
            received_ref[base : base + rank, inner_lanes],
            side_ref[3 * rank : 4 * rank, inner_lanes],
        ]
        contexts_all = [c01[0], c01[1], c23[0], c23[1]]
        weights_all = [wo0[...], wo1[...], far_ref[0, 0], far_ref[1, 0]]
        attended = tn(jnp.concatenate(contexts_all, axis=0), jnp.concatenate(weights_all, axis=0))
        for i in range(4):
            low_o = low_o + nn(inner_o[i], contexts_all[i])
        attended = attended + tn(halves(low_o), twice(oo[0]))
        hidden = states + mask * attended
        hidden_ref[...] = hidden
        z_ref[...] = normalize(hidden, gain_ref[...], shift_ref[...])[0].astype(bf16)
        grad_in = jnp.concatenate([ca[0], cb[...]], axis=0).astype(f32)
        gy_ref[...] = (mask * grad_in).astype(bf16)
        low_w = nt(wi[0], z_ref[...])
        low_n = nt(no[0], gy_ref[...])
        lows_ref[:rank] = low_o
        lows_ref[rank : 2 * rank] = low_w
        lows_ref[2 * rank : 3 * rank] = low_n
        for i, ref in enumerate((pack_ref, side_ref)):
            wide, thin = local[2 * i], local[2 * i + 1]
            copies[2 * i].wait()
            copies[2 * i + 1].wait()
            feed_quarter(z_ref, gy_ref, wide, thin, ref, ref, (rank, 2 * rank, rank), low_w, low_n, act_ref, grad_ref)
            sums = feed_sums(
                wide, thin, ref[rank : 2 * rank], ref[2 * rank : 3 * rank], low_w, low_n, act_ref, grad_ref, sums_ref.at[i]
            )
            if i == 0:
                branch_ref[...], second_ref[...], low_next, grad_low = sums
            else:
                branch_ref[...] += sums[0]
                second_ref[...] += sums[1]
                low_next += sums[2]
                grad_low += sums[3]
        lows_ref[3 * rank : 4 * rank] = low_next
        lows_ref[4 * rank :] = grad_low

    operands = contexts + outs_w + [far, pack, side, received] + tables
    specs = [whole(c.shape) for c in contexts] + [whole(w.shape) for w in outs_w]
    specs += [placed_block((2, 1, width, features), lambda *_: (0, 3, 0, 0))]
    specs += [whole(pack.shape), whole(side.shape), whole(received.shape)]
    specs += [placed_block((1, rank, features), of_mine(n)) for n in (3, 4, 5)]
    operands += [inputs, cotangent, cot_side, gain, shift] + dense
    specs += [placed_block((1, rows, features), lambda i, spot, *_: (spot[0], 0, 0))] * 2
    specs += [whole(cot_side.shape), whole(gain.shape), whole(shift.shape)]
    specs += [pl.BlockSpec(memory_space=pl.ANY)] * 4
    outs = [
        shaped((tokens, features), f32),
        shaped((tokens, features), bf16),
        shaped((tokens, features), bf16),
        shaped((tokens, features), f32),
        shaped((tokens, features), f32),
        shaped((5 * rank, tokens), f32),
        shaped((2, 2 * rank, units), f32),
    ]
    scratch = [pltpu.VMEM(d.shape, bf16) for d in dense]
    scratch += [pltpu.VMEM((tokens, units), bf16)] * 2 + [pltpu.SemaphoreType.DMA((4,))]
    return call(
        body,
        (spot, pick, lengths),
        operands,
        specs,
        outs,
        [whole(o.shape) for o in outs],
        scratch=scratch,
        cost=(2 * tokens * features * (4 * width + 8 * units), 4e7, tokens * units * 2),
    )


def feed_far(spot, pick, lengths, near, contexts, outs_w, far, packs, tables, received, cotangent, cot_side, gain, parts):
    hidden, z, gy, branch, second, lows = near
    tokens, features = hidden.shape
    rows = tokens // 2
    width = contexts[0].shape[1]
    rank = tables[0].shape[1]
    pack, side = packs
    base = received.shape[0] - 3 * rank
    part_rows = parts[0][0].shape[0]
    units = features
    flat = [p for group in parts for p in group]
    heads = width // HEAD_DIM

    def body(spot_ref, pick_ref, length_ref, hidden_ref, z_ref, gy_ref, branch_in, second_in, lows_ref, c01, c23, wo0, wo1, far_ref, pack_ref, side_ref, received_ref, oo, wi, no, ca, cb, gain_ref, *refs):
        hbm = refs[:16]
        outa_ref, outb_ref, gh_ref, gc_ref, delta_ref, sums_ref, shared_ref, inner_ref = refs[16:24]
        wide0, thin0, wide1, thin1, act_ref, grad_ref, sems = refs[24:]
        local = (wide0, thin0, wide1, thin1)
        copies = []
        for n in range(4):
            for r in range(4):
                at = pl.ds(pl.multiple_of((spot_ref[2] ^ r) * part_rows, 16), part_rows)
                copies.append(pltpu.make_async_copy(hbm[4 * n + r], local[n].at[at], sems.at[4 * n + r]))
        for c in copies:
            c.start()
        low_w = lows_ref[rank : 2 * rank]
        low_n = lows_ref[2 * rank : 3 * rank]
        low_next = lows_ref[3 * rank : 4 * rank]
        grad_low = lows_ref[4 * rank :]
        branch, grad_second = branch_in[...], second_in[...]
        places = ((received_ref, base), (side_ref, 3 * rank))
        for i, (ref, start) in enumerate(places):
            wide, thin = local[2 * i], local[2 * i + 1]
            for c in copies[8 * i : 8 * i + 8]:
                c.wait()
            at = (start + rank, start + 2 * rank, rank)
            feed_quarter(z_ref, gy_ref, wide, thin, ref, ref, at, low_w, low_n, act_ref, grad_ref)
            sums = feed_sums(
                wide, thin, ref[start + rank : start + 2 * rank], ref[start + 2 * rank : start + 3 * rank],
                low_w, low_n, act_ref, grad_ref, sums_ref.at[i],
            )
            branch = branch + sums[0]
            grad_second = grad_second + sums[1]
            low_next = low_next + sums[2]
            grad_low = grad_low + sums[3]
        mask = live_column(spot_ref, length_ref, rows, (0, 2)).astype(f32)
        branch = branch + tn(halves(low_next), twice(no[0]))
        grad_second = grad_second + tn(halves(grad_low), twice(wi[0]))
        hidden_now = hidden_ref[...]
        output = (hidden_now + mask * branch).astype(bf16)
        outa_ref[...] = output[:rows]
        outb_ref[...] = output[rows:]
        _, unit, scaled = normalize(hidden_now, gain_ref[...], gain_ref[...])
        grad_in = jnp.concatenate([ca[0], cb[...]], axis=0).astype(f32)
        grad_hidden = grad_in + normalize_back(grad_second, unit, scaled, gain_ref[...])
        gh_ref[...] = grad_hidden
        grad_attended = (mask * grad_hidden).astype(bf16)
        act_ref[...] = grad_attended
        grad_low_o = nt(oo[0], act_ref[...])
        shared_ref[:rank] = folded(nn(halves(grad_low), z_ref[...]))
        shared_ref[rank : 2 * rank] = folded(nn(halves(lows_ref[:rank]), act_ref[...]))
        shared_ref[2 * rank :] = folded(nn(halves(low_next), gy_ref[...]))
        inner_lanes = slice(3 * width, 4 * width)
        inner_o = [
            pack_ref[:rank, inner_lanes],
            side_ref[:rank, inner_lanes],
            received_ref[base : base + rank, inner_lanes],
            side_ref[3 * rank : 4 * rank, inner_lanes],
        ]
        contexts_all = [c01[0], c01[1], c23[0], c23[1]]
        weights_all = [wo0, wo1, far_ref.at[0, 0], far_ref.at[1, 0]]
        low_o2 = halves(grad_low_o)
        for i in range(4):
            grad = (nt(weights_all[i][...], act_ref[...]) + tn(twice(inner_o[i]), low_o2)).astype(bf16)
            gc_ref[i] = grad
            product = grad.astype(f32) * contexts_all[i].astype(f32)
            for h in range(heads):
                delta_ref[heads * i + h] = jnp.sum(
                    product[h * HEAD_DIM : (h + 1) * HEAD_DIM], axis=0, keepdims=True
                )
            inner_ref[i] = folded(nt(low_o2, contexts_all[i]))

    operands = [hidden, z, gy, branch, second, lows] + contexts + outs_w + [far, pack, side, received] + tables
    specs = [whole(o.shape) for o in operands[:10]]
    specs += [placed_block((2, 1, width, features), lambda *_: (0, 3, 0, 0))]
    specs += [whole(pack.shape), whole(side.shape), whole(received.shape)]
    specs += [placed_block((1, rank, features), of_mine(n)) for n in (3, 4, 5)]
    operands += [cotangent, cot_side, gain] + flat
    specs += [placed_block((1, rows, features), lambda i, spot, *_: (spot[0], 0, 0))]
    specs += [whole(cot_side.shape), whole(gain.shape)]
    specs += [pl.BlockSpec(memory_space=pl.ANY)] * 16
    outs = [
        shaped((rows, features), bf16),
        shaped((rows, features), bf16),
        shaped((tokens, features), f32),
        shaped((4, width, tokens), bf16),
        shaped((4 * heads, 1, tokens), f32),
        shaped((2, 2 * rank, units), f32),
        shaped((3 * rank, features), f32),
        shaped((4, rank, width), f32),
    ]
    scratch = [pltpu.VMEM((features, units), bf16), pltpu.VMEM((units, features), bf16)] * 2
    scratch += [pltpu.VMEM((tokens, units), bf16)] * 2 + [pltpu.SemaphoreType.DMA((16,))]
    return call(
        body,
        (spot, pick, lengths),
        operands,
        specs,
        outs,
        [whole(o.shape) for o in outs],
        scratch=scratch,
        cost=(2 * tokens * features * (4 * width + 8 * units), 5e7, tokens * units * 2),
    )


def gather_grads(near, far, z, low, packs, received):
    tokens, features = z.shape
    rank = low.shape[0] // 3
    width = near[0].shape[1]
    pack, side = packs
    base = received.shape[0] - 3 * rank

    def body(q01, own01, side01, q23, own23, side23, z_ref, low_ref, pack_ref, side_ref, received_ref, g_ref, gl_ref, outer_ref, inner_ref):
        groups = ((q01, own01, side01), (q23, own23, side23))
        places = ((pack_ref, 0), (side_ref, 0), (received_ref, base), (side_ref, 3 * rank))
        lows = [halves(low_ref[n * rank : (n + 1) * rank]) for n in range(3)]
        total = [jnp.zeros((rank, tokens), f32) for _ in range(3)]
        for i in range(4):
            q, own, other = groups[i // 2]
            ref, start = places[i]
            for n in range(3):
                if n == 0:
                    g = q[i % 2]
                else:
                    g = (own[i % 2, n - 1] + other[1 - i % 2, n - 1]).astype(bf16)
                g_ref[i, n] = g
                lanes = slice(n * width, (n + 1) * width)
                total[n] = total[n] + nn(ref[start : start + rank, lanes], g)
                outer_ref[i, n] = folded(nt(lows[n], g))
        for n in range(3):
            gl_ref[n * rank : (n + 1) * rank] = total[n]
            inner_ref[n * rank : (n + 1) * rank] = folded(nn(halves(total[n]), z_ref[...]))

    operands = list(near) + list(far) + [z, low, pack, side, received]
    outs = [
        shaped((4, 3, width, tokens), bf16),
        shaped((3 * rank, tokens), f32),
        shaped((4, 3, rank, width), f32),
        shaped((3 * rank, features), f32),
    ]
    return call(
        body, (), operands, [whole(o.shape) for o in operands], outs, [whole(o.shape) for o in outs],
        cost=(2 * tokens * features * 3 * 256, 2e7, 0),
    )


def finish(spot, pick, g, gl, inners, weights, far, inputs, received, grad_hidden, gain):
    rows, features = inputs.shape[1:]
    tokens = 2 * rows
    width = g.shape[2]
    rank = gl.shape[0] // 3

    def body(spot_ref, pick_ref, g_ref, gl_ref, iq, ik, iv, *refs):
        ws, (far_ref, xa, xb, gh_ref, gain_ref, grada_ref, gradb_ref) = refs[:6], refs[6:]
        low = [halves(gl_ref[n * rank : (n + 1) * rank]) for n in range(3)]
        total = tn(
            jnp.concatenate(low, axis=0),
            jnp.concatenate([twice(iq[0]), twice(ik[0]), twice(iv[0])], axis=0),
        )
        for i in range(4):
            for n in range(3):
                weight = ws[3 * i + n][...] if i < 2 else far_ref[i - 2, n]
                total = total + tn(g_ref[i, n], weight)
        states = jnp.concatenate([xa[0], xb[...]], axis=0).astype(f32)
        _, unit, scaled = normalize(states, gain_ref[...], gain_ref[...])
        grad = gh_ref[...] + normalize_back(total, unit, scaled, gain_ref[...])
        grada_ref[...] = grad[:rows]
        gradb_ref[...] = grad[rows:].astype(bf16)

    operands = [g, gl] + inners + weights + [far, inputs, received, grad_hidden, gain]
    specs = [whole(g.shape), whole(gl.shape)]
    specs += [placed_block((1, rank, features), of_mine(n)) for n in range(3)]
    specs += [whole(w.shape) for w in weights]
    specs += [placed_block((2, 3, width, features), lambda *_: (0, 0, 0, 0))]
    specs += [placed_block((1, rows, features), lambda i, spot, *_: (spot[0], 0, 0))]
    specs += [whole((rows, features)), whole(grad_hidden.shape), whole(gain.shape)]
    outs = [shaped((rows, features), f32), shaped((rows, features), bf16)]
    return call(
        body, (spot, pick), operands, specs, outs, [whole(o.shape) for o in outs],
        cost=(2 * tokens * features * 12 * width, 3e7, tokens),
    )


def make_body(dp_size, tensor_size):
    def across(array):
        return swap(array, "tensor", 2, tensor_size)

    def beside(array):
        return swap(array, "tensor", 1, tensor_size)

    def along(array, bits):
        return swap(array, "dp", bits, dp_size)

    def body(
        inputs,
        cotangent,
        lengths,
        adapter_pick,
        first_gain,
        first_bias,
        query_weight,
        key_weight,
        value_weight,
        output_weight,
        second_gain,
        second_bias,
        widen_weight,
        narrow_weight,
        query_inner,
        query_outer,
        key_inner,
        key_outer,
        value_inner,
        value_outer,
        output_inner,
        output_outer,
        widen_inner,
        widen_outer,
        narrow_inner,
        narrow_outer,
    ):
        rows, features = inputs.shape[1:]
        place = lax.axis_index("tensor")
        quad = lax.axis_index("dp") & 3
        mine = place >> 1
        spot = jnp.stack([mine, 1 - mine, quad, place]).astype(jnp.int32)
        pick = adapter_pick

        def flip(array):
            return jnp.swapaxes(array, 1, 2)

        small = [query_outer, key_outer, value_outer, flip(output_inner), widen_outer, flip(narrow_inner)]
        inners = [flip(query_inner), flip(key_inner), flip(value_inner)]
        tables = [output_outer, flip(widen_inner), narrow_outer]
        gains = [v.reshape(1, -1) for v in (first_gain, first_bias, second_gain, second_bias)]
        rank = query_outer.shape[1]
        heads = [query_weight.T, key_weight.T, value_weight.T, output_weight]
        dense = [widen_weight, narrow_weight]

        send, pack = stage(spot, pick, inputs, small)
        received = across(send)
        part_heads, part_wide, part_thin, cot_send = stage_weights(spot, pick, heads, dense, cotangent)
        near_heads = [beside(w) for w in heads]
        side = beside(jnp.concatenate([pack, received[rows:]], axis=0))
        near_dense = [beside(w) for w in dense]

        far_heads = [across(part_heads)]
        far_heads += [along(far_heads[0], 1), along(far_heads[0], 2)]
        far_heads += [along(far_heads[2][:2], 1), along(far_heads[1][2:], 2)]
        far_wide = [across(part_wide)]
        far_thin = [across(part_thin)]
        cot_side = across(cot_send)
        for far, bits in ((far_wide, 1), (far_thin, 2)):
            far += [along(far[0], 1), along(far[0], 2)]
            far += [along(far[3 - bits], bits)]
        side_heads = [beside(p) for p in far_heads]
        side_wide = [beside(p) for p in far_wide]
        side_thin = [beside(p) for p in far_thin]

        z, low, q01, kv01 = project_near(
            spot, pick, inputs, received, gains[0], gains[1], inners, pack, side, heads[:3] + near_heads[:3]
        )
        kv01_side = beside(kv01)
        c01, total01 = attend(spot, lengths, q01, kv01, kv01_side)
        far, q23, kv23 = project_far(spot, pick, z, low, received, side, [far_heads, side_heads])
        kv23_side = beside(kv23)
        c23, total23 = attend(spot, lengths, q23, kv23, kv23_side)
        *near, near_sums = feed_near(
            spot, pick, lengths, [c01, c23], [heads[3], near_heads[3]], far, [pack, side], tables,
            inputs, received, cotangent, cot_side, gains[2], gains[3], dense + near_dense,
        )
        outa, outb, grad_hidden, grad_context, deltas, far_sums, shared_early, inner_sums = feed_far(
            spot, pick, lengths, near, [c01, c23], [heads[3], near_heads[3]], far, [pack, side], tables,
            received, cotangent, cot_side, gains[2], [far_wide, far_thin, side_wide, side_thin],
        )
        out_side = across(outb)
        gq01, own01, other01 = attend_back(
            spot, lengths, q01, kv01, kv01_side, grad_context, total01, deltas, 0
        )
        side01 = beside(other01)
        gq23, own23, other23 = attend_back(
            spot, lengths, q23, kv23, kv23_side, grad_context, total23, deltas, 1
        )
        side23 = beside(other23)
        g, gl, outer_sums, shared_late = gather_grads(
            (gq01, own01, side01), (gq23, own23, side23), z, low, (pack, side), received
        )
        grada, gradb = finish(
            spot, pick, g, gl, inners, heads[:3] + near_heads[:3], far, inputs, received, grad_hidden, gains[0]
        )
        grad_side = across(gradb)

        def pair_up(first, second):
            pair = jnp.stack([first, second.astype(first.dtype)])
            return jnp.where(mine == 0, pair, pair[::-1])

        output = pair_up(outa, out_side)
        input_grad = pair_up(grada, grad_side)

        core = place & 1
        half = features // 2
        picks = jnp.zeros((8, features), f32).at[0, :6].set(pick[mine].astype(f32))

        def reduce(quarters, shared):
            count = quarters[0].shape[0]
            keep = lax.dynamic_slice_in_dim(shared, core * half, half, 1)
            give = lax.dynamic_slice_in_dim(shared, (1 - core) * half, half, 1)

            def packed(a, b, s):
                s = jnp.concatenate([s[: s.shape[0] // 2], s[s.shape[0] // 2 :]], axis=1)
                return jnp.concatenate([a, b, s], axis=0)

            moved = beside(packed(quarters[1], quarters[3], give))
            kept = packed(quarters[0], quarters[2], keep) + moved
            here = jnp.concatenate([kept[:count], kept[2 * count :], picks], axis=0).astype(bf16)
            there = jnp.concatenate([kept[count:], picks], axis=0).astype(bf16)
            every = jnp.stack([here, across(there)])
            bits = 1
            while bits < min(dp_size, 8):
                every = jnp.concatenate([every, along(every, bits)], axis=0)
                bits *= 2
            hot = (
                every[:, -8, :6, None].astype(jnp.int32) == jnp.arange(query_inner.shape[0])
            ).astype(bf16)
            s = every[:, count:-8]
            return every[:, :count], jnp.concatenate([s[..., :half], s[..., half:]], axis=1), hot

        def spread(hot, number, values):
            table = jnp.einsum("ce,crw->erw", hot[:, number], values, preferred_element_type=f32)
            bits = 8
            while bits < dp_size:
                table = table + along(table, bits)
                bits *= 2
            return table

        sums = [near_sums[0], near_sums[1], far_sums[0], far_sums[1]]
        wide, shared, hot = reduce(sums, shared_early)
        widen_outer_grad = spread(hot, 4, wide[:, :rank])
        narrow_inner_grad = spread(hot, 5, wide[:, rank:])
        early = [
            spread(hot, 4, shared[:, :rank]),
            spread(hot, 3, shared[:, rank : 2 * rank]),
            spread(hot, 5, shared[:, 2 * rank :]),
        ]
        quarters = [
            jnp.concatenate([outer_sums[i, 0], outer_sums[i, 1], outer_sums[i, 2], inner_sums[i]], axis=1)
            for i in range(4)
        ]
        thin, shared, hot = reduce(quarters, shared_late)
        width = query_outer.shape[2]
        heads_grads = [spread(hot, n, thin[:, :, n * width : (n + 1) * width]) for n in range(4)]
        late = [spread(hot, n, shared[:, n * rank : (n + 1) * rank]) for n in range(3)]

        def complete(group):
            group = jnp.stack(group)
            moved = beside(group)
            first = jnp.where(core == 0, group, moved)
            second = jnp.where(core == 0, moved, group)
            return jnp.concatenate([first, second], axis=-1)

        early = complete(early)
        late = complete(late)
        return (
            output,
            input_grad,
            flip(late[0]),
            heads_grads[0],
            flip(late[1]),
            heads_grads[1],
            flip(late[2]),
            heads_grads[2],
            flip(heads_grads[3]),
            early[1],
            flip(early[0]),
            widen_outer_grad,
            flip(narrow_inner_grad),
            early[2],
        )

    return body


def solution(mesh):
    placed = (
        P("dp", "tensor", None),
        P("dp", "tensor", None),
        P("dp"),
        P("dp", None),
        P(),
        P(),
        P(None, "tensor"),
        P(None, "tensor"),
        P(None, "tensor"),
        P("tensor", None),
        P(),
        P(),
        P(None, "tensor"),
        P("tensor", None),
        P(),
        P(None, None, "tensor"),
        P(),
        P(None, None, "tensor"),
        P(),
        P(None, None, "tensor"),
        P(None, "tensor", None),
        P(),
        P(),
        P(None, None, "tensor"),
        P(None, "tensor", None),
        P(),
    )
    return jax.shard_map(
        make_body(mesh.shape["dp"], mesh.shape["tensor"]),
        mesh=mesh,
        in_specs=placed,
        out_specs=(
            P("dp", "tensor", None),
            P("dp", "tensor", None),
            P(),
            P(None, None, "tensor"),
            P(),
            P(None, None, "tensor"),
            P(),
            P(None, None, "tensor"),
            P(None, "tensor", None),
            P(),
            P(),
            P(None, None, "tensor"),
            P(None, "tensor", None),
            P(),
        ),
        check_vma=False,
    )
```

```python
import functools
import math

import jax
import jax.numpy as jnp
from jax import lax
from jax.experimental import pallas as pl
from jax.experimental.pallas import tpu as pltpu
from jax.sharding import PartitionSpec as P

HEAD_DIM = 80
f32 = jnp.float32
bf16 = jnp.bfloat16
neg_fill = -1000000000.0
score_scale = 1.0 / math.sqrt(HEAD_DIM)
log2_e = math.log2(math.e)
LIMIT = 26
KEEP = pl.BlockSpec(memory_space=pltpu.VMEM)
remain = pl.BlockSpec(memory_space=pl.ANY)


def swap(array, axis, bits, size):
    return lax.ppermute(array, axis, [(i, i ^ bits) for i in range(size)])


def nn(a, b):
    return jnp.dot(a, b, preferred_element_type=f32)


def nt(a, b):
    return lax.dot_general(a, b, (((1,), (1,)), ((), ())), preferred_element_type=f32)


def tn(a, b):
    return lax.dot_general(a, b, (((0,), (0,)), ((), ())), preferred_element_type=f32)


def halves(low):
    top = low.astype(bf16)
    return jnp.concatenate([top, (low - top.astype(f32)).astype(bf16)], axis=0)


def twice(factor):
    return jnp.concatenate([factor, factor], axis=0)


def folded(pair):
    count = pair.shape[0] // 2
    return pair[:count] + pair[count:]


def normalize(states, gain, shift):
    centre = states - jnp.mean(states, axis=-1, keepdims=True)
    scaled = lax.rsqrt(jnp.mean(centre * centre, axis=-1, keepdims=True) + 1e-05)
    unit = centre * scaled
    return unit * gain + shift, unit, scaled


def normalize_back(grad_rows, unit, scaled, gain):
    grad_unit = grad_rows * gain
    return scaled * (
        grad_unit
        - jnp.mean(grad_unit, axis=-1, keepdims=True)
        - unit * jnp.mean(grad_unit * unit, axis=-1, keepdims=True)
    )


def live_column(spot_ref, length_ref, rows, bits):
    iota = lax.broadcasted_iota(jnp.int32, (2 * rows, 1), 0)
    place = spot_ref[3]
    first, second = place ^ bits[0], place ^ bits[1]
    position = jnp.where(iota < rows, first * rows + iota, second * rows + iota - rows)
    return position < length_ref[spot_ref[0]]


def whole(shape):
    return KEEP


def placed_block(shape, index):
    return pl.BlockSpec(shape, index, pipeline_mode=pl.Buffered(1))


def call(body, scalars, operands, specs, outs, out_specs, grid=(1,), scratch=(), limit=LIMIT, aliases=None, weight=100):
    return pl.pallas_call(
        body,
        grid_spec=pltpu.PrefetchScalarGridSpec(
            num_scalar_prefetch=len(scalars),
            grid=grid,
            in_specs=specs,
            out_specs=out_specs,
            scratch_shapes=list(scratch),
        ),
        out_shape=outs,
        cost_estimate=pl.CostEstimate(flops=weight * 10**9, bytes_accessed=100000, transcendentals=0),
        input_output_aliases=aliases or {},
        compiler_params=pltpu.CompilerParams(vmem_limit_bytes=limit * 2**20),
    )(*scalars, *operands)


def shaped(shape, dtype):
    return jax.ShapeDtypeStruct(shape, dtype)


def of_mine(number):
    return lambda i, spot, pick, *_: (pick[spot[0], number], 0, 0)


def of_other(number):
    return lambda i, spot, pick, *_: (pick[spot[1], number], 0, 0)


def after(values, *others):
    return lax.optimization_barrier((values, others))[0]


def shuffled(array, quad):
    count = array.shape[1] // 4
    blocks = [array[:, n * count : (n + 1) * count] for n in range(4)]
    for bits in (1, 2):
        on = ((quad >> (bits - 1)) & 1) == 1
        blocks = [jnp.where(on, blocks[n ^ bits], blocks[n]) for n in range(4)]
    return jnp.concatenate(blocks, axis=1)


def stage(spot, pick, inputs, factors):
    rows, features = inputs.shape[1:]
    rank = factors[0].shape[1]

    def body(spot_ref, pick_ref, inputs_ref, *refs):
        send_ref, pack_ref = refs[12:]
        send_ref[:rows] = inputs_ref[0]
        quad = spot_ref[2]
        for group, ref, base in ((refs[:6], pack_ref, 0), (refs[6:12], send_ref, rows)):
            ref[base : base + rank] = jnp.concatenate([r[0] for r in group[:4]], axis=1)
            wide, thin = group[4][0], group[5][0]
            if base:
                wide, thin = shuffled(wide, quad), shuffled(thin, quad)
            ref[base + rank : base + 2 * rank] = wide
            ref[base + 2 * rank : base + 3 * rank] = thin

    specs = [placed_block((1, rows, features), lambda i, spot, *_: (spot[1], 0, 0))]
    for of in (of_mine, of_other):
        specs += [placed_block((1,) + f.shape[1:], of(n)) for n, f in enumerate(factors)]
    outs = [shaped((rows + 3 * rank, features), bf16), shaped((3 * rank, features), bf16)]
    return call(body, (spot, pick), [inputs] + factors * 2, specs, outs, [whole(o.shape) for o in outs])


def stage_heads(spot, heads):
    features = heads[0].shape[1]
    head_rows = heads[0].shape[0] // 4

    def body(spot_ref, *refs):
        out, sems = refs[4:]
        at = pl.ds(pl.multiple_of(spot_ref[2] * head_rows, 16), head_rows)
        copies = [pltpu.make_async_copy(refs[n].at[at], out.at[n], sems.at[n]) for n in range(4)]
        for c in copies:
            c.start()
        for c in copies:
            c.wait()

    out = shaped((4, head_rows, features), bf16)
    return call(body, (spot,), heads, [remain] * 4, out, KEEP, scratch=[pltpu.SemaphoreType.DMA((4,))])


def stage_dense(spot, wide, thin, cotangent):
    features, units = wide.shape
    part = units // 4
    rows = cotangent.shape[1]

    def body(spot_ref, wide_ref, thin_ref, cot_ref, wide_out, thin_out, cot_out):
        for r in range(4):

            @pl.when(spot_ref[2] == r)
            def _():
                wide_out[...] = wide_ref[:, r * part : (r + 1) * part].T

        thin_out[...] = thin_ref[...]
        cot_out[...] = cot_ref[0]

    specs = [
        whole(wide.shape),
        placed_block((part, features), lambda i, spot: (spot[2], 0)),
        placed_block((1, rows, features), lambda i, spot: (spot[1], 0, 0)),
    ]
    outs = [shaped((part, features), bf16), shaped((part, features), bf16), shaped((rows, features), bf16)]
    return call(body, (spot,), [wide, thin, cotangent], specs, outs, [whole(o.shape) for o in outs])


def project_rows(weight, rows_in, outer, low):
    return (nt(weight, rows_in) + tn(twice(outer), halves(low))).astype(bf16)


def project_near(spot, pick, inputs, received, gain, shift, inners, pack, side, weights):
    rows, features = inputs.shape[1:]
    tokens = 2 * rows
    width = weights[0].shape[0]
    rank = inners[0].shape[1]

    def body(spot_ref, pick_ref, xa, xb, gain_ref, shift_ref, iq, ik, iv, pack_ref, side_ref, *refs):
        ws, (z_ref, low_ref, kv_ref) = refs[:4], refs[4:]
        states = jnp.concatenate([xa[0], xb[...]], axis=0).astype(f32)
        z_ref[...] = normalize(states, gain_ref[...], shift_ref[...])[0].astype(bf16)
        low = nt(jnp.concatenate([iq[0], ik[0], iv[0]], axis=0), z_ref[...])
        low_ref[...] = low
        for i, packs in enumerate((pack_ref, side_ref)):
            for n in (1, 2):
                outer = packs[:rank, n * width : (n + 1) * width]
                kv_ref[i, n - 1] = project_rows(
                    ws[2 * i + n - 1][...], z_ref[...], outer, low[n * rank : (n + 1) * rank]
                )

    specs = [
        placed_block((1, rows, features), lambda i, spot, *_: (spot[0], 0, 0)),
        placed_block((rows, features), lambda *_: (0, 0)),
        whole((1, features)),
        whole((1, features)),
    ]
    specs += [placed_block((1, rank, features), of_mine(n)) for n in range(3)]
    specs += [whole(pack.shape), whole(side.shape)] + [whole((width, features))] * 4
    outs = [
        shaped((tokens, features), bf16),
        shaped((3 * rank, tokens), f32),
        shaped((2, 2, width, tokens), bf16),
    ]
    return call(
        body,
        (spot, pick),
        [inputs, received, gain, shift] + inners + [pack, side] + weights,
        specs,
        outs,
        [whole(o.shape) for o in outs],
    )


def queries_near(z, low, pack, side, weights):
    tokens, features = z.shape
    width = weights[0].shape[0]
    rank = low.shape[0] // 3

    def body(z_ref, low_ref, pack_ref, side_ref, w0, w1, q_ref):
        for i, (packs, w) in enumerate(((pack_ref, w0), (side_ref, w1))):
            q_ref[i] = project_rows(w[...], z_ref[...], packs[:rank, :width], low_ref[:rank])

    operands = [z, low, pack, side] + weights
    out = shaped((2, width, tokens), bf16)
    return call(body, (), operands, [whole(o.shape) for o in operands], out, whole(out.shape))


def project_far(spot, z, low, received, side, parts):
    tokens, features = z.shape
    head_rows = parts[0][0].shape[1]
    width = 4 * head_rows
    rank = low.shape[0] // 3
    base = received.shape[0] - 3 * rank
    flat = [p for group in parts for p in group]

    def body(spot_ref, z_ref, low_ref, received_ref, side_ref, *refs):
        ins, (weight_ref, kv_ref) = refs[:10], refs[10:]
        for i in range(2):
            group = ins[5 * i : 5 * i + 5]
            for n in range(4):
                for r in range(4):
                    at = pl.ds(pl.multiple_of((spot_ref[0] ^ r) * head_rows, 16), head_rows)
                    if r < 3:
                        weight_ref[i, n, at] = group[r][n]
                    else:
                        weight_ref[i, n, at] = group[3 + n // 2][n % 2]
        for i, (ref, start) in enumerate(((received_ref, base), (side_ref, 0))):
            for n in (1, 2):
                outer = ref[start : start + rank, n * width : (n + 1) * width]
                kv_ref[i, n - 1] = project_rows(
                    weight_ref[i, n], z_ref[...], outer, low_ref[n * rank : (n + 1) * rank]
                )

    operands = [z, low, received, side] + flat
    outs = [shaped((2, 4, width, features), bf16), shaped((2, 2, width, tokens), bf16)]
    return call(
        body, (spot[2:3],), operands, [whole(o.shape) for o in operands], outs, [whole(o.shape) for o in outs]
    )


def queries_far(z, low, received, side, far):
    tokens, features = z.shape
    width = far.shape[2]
    rank = low.shape[0] // 3
    base = received.shape[0] - 3 * rank

    def body(z_ref, low_ref, received_ref, side_ref, far_ref, q_ref):
        for i, (ref, start) in enumerate(((received_ref, base), (side_ref, 0))):
            outer = ref[start : start + rank, :width]
            q_ref[i] = project_rows(far_ref[i, 0], z_ref[...], outer, low_ref[:rank])

    operands = [z, low, received, side, far]
    specs = [whole(o.shape) for o in operands[:4]] + [placed_block((2, 1, width, features), lambda *_: (0, 0, 0, 0))]
    out = shaped((2, width, tokens), bf16)
    return call(body, (), operands, specs, out, whole(out.shape))


def attend(spot, lengths, q, kv, kv_side):
    _, width, tokens = q.shape
    rows = tokens // 2
    pair = 2 * HEAD_DIM
    steps = width // pair

    def body(spot_ref, length_ref, q_ref, k1, k2, v1, v2, ctx_ref, total_ref):
        bias1 = jnp.where(live_column(spot_ref, length_ref, rows, (0, 2)), 0.0, neg_fill * log2_e)
        bias2 = jnp.where(live_column(spot_ref, length_ref, rows, (1, 3)), 0.0, neg_fill * log2_e)
        for h in range(2):
            at = slice(h * HEAD_DIM, (h + 1) * HEAD_DIM)
            query = q_ref[0, at]
            s1 = tn(k1[0, 0, at], query) * (score_scale * log2_e) + bias1
            s2 = tn(k2[0, 0, at], query) * (score_scale * log2_e) + bias2
            top = jnp.maximum(jnp.max(s1, axis=0, keepdims=True), jnp.max(s2, axis=0, keepdims=True))
            p1 = jnp.exp2(s1 - top)
            p2 = jnp.exp2(s2 - top)
            total = jnp.sum(p1, axis=0, keepdims=True) + jnp.sum(p2, axis=0, keepdims=True)
            context = nn(v1[0, 0, at], p1.astype(bf16)) + nn(v2[0, 0, at], p2.astype(bf16))
            ctx_ref[0, at] = (context * (1.0 / total)).astype(bf16)
            total_ref[h] = top + jnp.log2(total)

    def own(n):
        return pl.BlockSpec((1, 1, pair, tokens), lambda h, *_: (h // steps, n, h % steps, 0))

    def beside(n):
        return pl.BlockSpec((1, 1, pair, tokens), lambda h, *_: (1 - h // steps, n, h % steps, 0))

    rows_spec = pl.BlockSpec((1, pair, tokens), lambda h, *_: (h // steps, h % steps, 0))
    return call(
        body,
        (spot, lengths),
        [q, kv, kv_side, kv, kv_side],
        [rows_spec, own(0), beside(0), own(1), beside(1)],
        [shaped(q.shape, bf16), shaped((4 * steps, 1, tokens), f32)],
        [rows_spec, pl.BlockSpec((2, 1, tokens), lambda h, *_: (h, 0, 0))],
        grid=(2 * steps,),
    )


def attend_back(spot, lengths, q, kv, kv_side, grad_context, totals, deltas, which):
    _, width, tokens = q.shape
    rows = tokens // 2
    pair = 2 * HEAD_DIM
    steps = width // pair

    def body(spot_ref, length_ref, q_ref, k1, k2, v1, v2, g_ref, total_ref, delta_ref, gq, own_ref, other_ref):
        bias1 = jnp.where(live_column(spot_ref, length_ref, rows, (0, 2)), 0.0, neg_fill * log2_e)
        bias2 = jnp.where(live_column(spot_ref, length_ref, rows, (1, 3)), 0.0, neg_fill * log2_e)
        for h in range(2):
            at = slice(h * HEAD_DIM, (h + 1) * HEAD_DIM)
            query = q_ref[0, at]
            grad = g_ref[0, at]
            grad_query = None
            for k, v, bias, out in ((k1, v1, bias1, own_ref), (k2, v2, bias2, other_ref)):
                s = tn(k[0, 0, at], query) * (score_scale * log2_e) + bias
                soft = jnp.exp2(s - total_ref[h])
                grad_soft = tn(v[0, 0, at], grad)
                grad_scores = (soft * (grad_soft - delta_ref[h])).astype(bf16)
                part = nn(k[0, 0, at], grad_scores)
                grad_query = part if grad_query is None else grad_query + part
                out[0, 0, at] = nt(query, grad_scores) * score_scale
                out[0, 1, at] = nt(grad, soft.astype(bf16))
            gq[0, at] = (grad_query * score_scale).astype(bf16)

    def own(n):
        return pl.BlockSpec((1, 1, pair, tokens), lambda h, *_: (h // steps, n, h % steps, 0))

    def beside(n):
        return pl.BlockSpec((1, 1, pair, tokens), lambda h, *_: (1 - h // steps, n, h % steps, 0))

    rows_spec = pl.BlockSpec((1, pair, tokens), lambda h, *_: (h // steps, h % steps, 0))
    grads_spec = pl.BlockSpec((1, pair, tokens), lambda h, *_: (2 * which + h // steps, h % steps, 0))
    line = pl.BlockSpec((2, 1, tokens), lambda h, *_: (h, 0, 0))
    line_at = pl.BlockSpec((2, 1, tokens), lambda h, *_: (2 * steps * which + h, 0, 0))
    both = pl.BlockSpec((1, 2, pair, tokens), lambda h, *_: (h // steps, 0, h % steps, 0))
    return call(
        body,
        (spot, lengths),
        [q, kv, kv_side, kv, kv_side, grad_context, totals, deltas],
        [rows_spec, own(0), beside(0), own(1), beside(1), grads_spec, line, line_at],
        [shaped(q.shape, bf16), shaped(kv.shape, f32), shaped(kv.shape, f32)],
        [rows_spec, both, both],
        grid=(2 * steps,),
    )


cubic = 0.044715
root = math.sqrt(2.0 / math.pi)


def bend_of(widened, grad):
    square = widened * widened
    bend = jnp.tanh(root * widened * (1.0 + cubic * square))
    up = 0.5 * (1.0 + bend)
    slope = up + widened * (0.5 * root) * (1.0 - bend * bend) * (1.0 + 3.0 * cubic * square)
    return (widened * up).astype(bf16), (grad * slope).astype(bf16)


def feed_quarter(z_ref, gy_ref, wide_ref, thin_ref, pack_ref, rank, low_w, low_n, act_ref, grad_ref, sums_ref):
    units = wide_ref.shape[1]
    block = 256
    low_w2, low_n2 = halves(low_w), halves(low_n)

    def step(b, carry):
        at = pl.ds(pl.multiple_of(b * block, block), block)
        widened = nn(z_ref[...], wide_ref[:, at]) + tn(low_w2, twice(pack_ref[rank : 2 * rank, at]))
        grad = nt(gy_ref[...], thin_ref[at, :]) + tn(low_n2, twice(pack_ref[2 * rank : 3 * rank, at]))
        act_ref[:, at], grad_ref[:, at] = bend_of(widened, grad)
        return carry

    lax.fori_loop(0, units // block, step, 0)
    sums_ref[:rank] = folded(nn(low_w2, grad_ref[...]))
    sums_ref[rank:] = folded(nn(low_n2, act_ref[...]))
    return (
        nn(act_ref[...], thin_ref[...]),
        nt(grad_ref[...], wide_ref[...]),
        nt(pack_ref[2 * rank : 3 * rank], act_ref[...]),
        nt(pack_ref[rank : 2 * rank], grad_ref[...]),
    )


def feed_units(z_ref, gy_ref, wide_ref, thin_ref, outer, inner, low_w, low_n, act_ref, grad_ref):
    units = wide_ref.shape[0]
    block = 256
    low_w2, low_n2 = halves(low_w), halves(low_n)
    for start in range(0, units, block):
        at = slice(start, min(start + block, units))
        widened = nt(z_ref[...], wide_ref[at]) + tn(low_w2, twice(outer[:, at]))
        grad = nt(gy_ref[...], thin_ref[at]) + tn(low_n2, twice(inner[:, at]))
        act_ref[:, at], grad_ref[:, at] = bend_of(widened, grad)
    sums = jnp.concatenate(
        [folded(nn(low_w2, grad_ref[...])), folded(nn(low_n2, act_ref[...]))], axis=0
    )
    return (
        nn(act_ref[...], thin_ref[...]),
        nn(grad_ref[...], wide_ref[...]),
        nt(inner, act_ref[...]),
        nt(outer, grad_ref[...]),
        sums,
    )


def output_inner_rows(pack_ref, side_ref, received_ref, far_side_ref, rank, base, width):
    lanes = slice(3 * width, 4 * width)
    return [
        pack_ref[:rank, lanes],
        side_ref[:rank, lanes],
        received_ref[base : base + rank, lanes],
        far_side_ref[:rank, lanes],
    ]


def feed_open(spot, pick, lengths, contexts, outs_w, far, packs, tables, inputs, received, gain, shift):
    rows, features = inputs.shape[1:]
    tokens = 2 * rows
    width = contexts[0].shape[1]
    rank = tables[0].shape[1]
    pack, side, far_side = packs
    base = received.shape[0] - 3 * rank

    def body(spot_ref, pick_ref, length_ref, c01, c23, wo0, wo1, far_ref, pack_ref, side_ref, far_side_ref, received_ref, oo, wi, xa, gain_ref, shift_ref, hidden_ref, z_ref, lows_ref):
        states = jnp.concatenate([xa[0], received_ref[:rows]], axis=0).astype(f32)
        mask = live_column(spot_ref, length_ref, rows, (0, 2)).astype(f32)
        inner_o = output_inner_rows(pack_ref, side_ref, received_ref, far_side_ref, rank, base, width)
        contexts_all = [c01[0], c01[1], c23[0], c23[1]]
        weights_all = [wo0[...], wo1[...], far_ref[0, 0], far_ref[1, 0]]
        joined = jnp.concatenate(contexts_all, axis=0)
        attended = tn(joined, jnp.concatenate(weights_all, axis=0))
        low_o = nn(jnp.concatenate(inner_o, axis=1), joined)
        attended = attended + tn(halves(low_o), twice(oo[0]))
        hidden = states + mask * attended
        hidden_ref[...] = hidden
        z_ref[...] = normalize(hidden, gain_ref[...], shift_ref[...])[0].astype(bf16)
        lows_ref[:rank] = low_o
        lows_ref[rank:] = nt(wi[0], z_ref[...])

    operands = contexts + outs_w + [far, pack, side, far_side, received] + tables[:2]
    specs = [whole(c.shape) for c in contexts] + [whole(w.shape) for w in outs_w]
    specs += [placed_block((2, 1, width, features), lambda *_: (0, 3, 0, 0))]
    specs += [whole(p.shape) for p in packs] + [whole(received.shape)]
    specs += [placed_block((1, rank, features), of_mine(n)) for n in (3, 4)]
    operands += [inputs, gain, shift]
    specs += [placed_block((1, rows, features), lambda i, spot, *_: (spot[0], 0, 0))]
    specs += [whole(gain.shape), whole(shift.shape)]
    outs = [shaped((tokens, features), f32), shaped((tokens, features), bf16), shaped((2 * rank, tokens), f32)]
    return call(body, (spot, pick, lengths), operands, specs, outs, [KEEP] * 3)


def feed_first(spot, pick, lengths, z, lows, table, cotangent, cot_side, pack, dense):
    tokens, features = z.shape
    rows = tokens // 2
    rank = table.shape[1]
    units = dense[0].shape[1]

    def body(spot_ref, pick_ref, length_ref, z_ref, lows_in, no, ca, cb, pack_ref, wide, thin, gy_ref, branch_ref, second_ref, lows_ref, sums_ref, act_ref, grad_ref):
        mask = live_column(spot_ref, length_ref, rows, (0, 2)).astype(f32)
        grad_in = jnp.concatenate([ca[0], cb[...]], axis=0).astype(f32)
        gy_ref[...] = (mask * grad_in).astype(bf16)
        low_n = nt(no[0], gy_ref[...])
        lows_ref[: 2 * rank] = lows_in[...]
        lows_ref[2 * rank : 3 * rank] = low_n
        branch_ref[...], second_ref[...], lows_ref[3 * rank : 4 * rank], lows_ref[4 * rank :] = feed_quarter(
            z_ref, gy_ref, wide, thin, pack_ref, rank, lows_in[rank:], low_n, act_ref, grad_ref, sums_ref
        )

    operands = [z, lows, table, cotangent, cot_side, pack] + dense
    specs = [KEEP, KEEP, placed_block((1, rank, features), of_mine(5))]
    specs += [placed_block((1, rows, features), lambda i, spot, *_: (spot[0], 0, 0))] + [KEEP] * 4
    outs = [
        shaped((tokens, features), bf16),
        shaped((tokens, features), f32),
        shaped((tokens, features), f32),
        shaped((5 * rank, tokens), f32),
        shaped((2 * rank, units), f32),
    ]
    scratch = [pltpu.VMEM((tokens, units), bf16)] * 2
    return call(body, (spot, pick, lengths), operands, specs, outs, [KEEP] * 5, scratch=scratch)


def feed_near(z, gy, branch, second, lows, pack, dense):
    tokens, features = z.shape
    units = dense[0].shape[1]
    rank = lows.shape[0] // 5

    def body(z_ref, gy_ref, branch_in, second_in, lows_in, pack_ref, wide, thin, branch_ref, second_ref, lows_ref, sums_ref, act_ref, grad_ref):
        sums = feed_quarter(
            z_ref, gy_ref, wide, thin, pack_ref, rank, lows_in[rank : 2 * rank], lows_in[2 * rank : 3 * rank],
            act_ref, grad_ref, sums_ref,
        )
        branch_ref[...] = branch_in[...] + sums[0]
        second_ref[...] = second_in[...] + sums[1]
        lows_ref[: 3 * rank] = lows_in[: 3 * rank]
        lows_ref[3 * rank : 4 * rank] = lows_in[3 * rank : 4 * rank] + sums[2]
        lows_ref[4 * rank :] = lows_in[4 * rank :] + sums[3]

    operands = [z, gy, branch, second, lows, pack] + dense
    outs = [shaped(branch.shape, f32), shaped(second.shape, f32), shaped(lows.shape, f32), shaped((2 * rank, units), f32)]
    scratch = [pltpu.VMEM((tokens, units), bf16)] * 2
    return call(body, (), operands, [KEEP] * len(operands), outs, [KEEP] * 4, scratch=scratch, aliases={2: 0, 3: 1})


def far_parts(parts, z_ref, gy_ref, ins, wide, thin, received_ref, far_side_ref, rank, base, low_w, low_n, act_ref, grad_ref, sums_ref):
    count = wide.shape[0] // 2
    total = None
    for n, r in enumerate(parts):
        lanes = slice(r * count, (r + 1) * count)
        outer = jnp.concatenate(
            [received_ref[base + rank : base + 2 * rank, lanes], far_side_ref[rank : 2 * rank, lanes]], axis=1
        )
        inner = jnp.concatenate(
            [received_ref[base + 2 * rank : base + 3 * rank, lanes], far_side_ref[2 * rank : 3 * rank, lanes]], axis=1
        )
        for q in range(2):
            at = slice(q * count, (q + 1) * count)
            wide[at] = ins[4 * n + q][...]
            thin[at] = ins[4 * n + 2 + q][...]
        found = feed_units(z_ref, gy_ref, wide, thin, outer, inner, low_w, low_n, act_ref, grad_ref)
        sums_ref[n] = found[4]
        total = found[:4] if total is None else [a + b for a, b in zip(total, found[:4])]
    return total


def far_scratch(part, features, tokens):
    return [pltpu.VMEM((2 * part, features), bf16)] * 2 + [pltpu.VMEM((tokens, 2 * part), bf16)] * 2


def feed_far(parts, z, gy, branch, second, lows, received, far_side, weights):
    tokens, features = z.shape
    part = weights[0].shape[0]
    rank = lows.shape[0] // 5
    base = received.shape[0] - 3 * rank
    count = len(weights)

    def body(z_ref, gy_ref, branch_in, second_in, lows_in, received_ref, far_side_ref, *refs):
        ins, (branch_ref, second_ref, lows_ref, sums_ref) = refs[:count], refs[count : count + 4]
        wide, thin, act_ref, grad_ref = refs[count + 4 :]
        total = far_parts(
            parts, z_ref, gy_ref, ins, wide, thin, received_ref, far_side_ref, rank, base,
            lows_in[rank : 2 * rank], lows_in[2 * rank : 3 * rank], act_ref, grad_ref, sums_ref,
        )
        branch_ref[...] = branch_in[...] + total[0]
        second_ref[...] = second_in[...] + total[1]
        lows_ref[: 3 * rank] = lows_in[: 3 * rank]
        lows_ref[3 * rank : 4 * rank] = lows_in[3 * rank : 4 * rank] + total[2]
        lows_ref[4 * rank :] = lows_in[4 * rank :] + total[3]

    operands = [z, gy, branch, second, lows, received, far_side] + weights
    outs = [
        shaped(branch.shape, f32),
        shaped(second.shape, f32),
        shaped(lows.shape, f32),
        shaped((len(parts), 2 * rank, 2 * part), f32),
    ]
    return call(
        body, (), operands, [KEEP] * len(operands), outs, [KEEP] * 4,
        scratch=far_scratch(part, features, tokens), aliases={2: 0, 3: 1},
    )


def shares(array, core):
    half = array.shape[1] // 2
    low, high = array[:, :half], array[:, half:]
    return jnp.where(core == 0, low, high), jnp.where(core == 0, high, low)


def padded(array, count):
    return jnp.concatenate([array, jnp.zeros((array.shape[0], count - array.shape[1]), array.dtype)], axis=1)


def lanes_up(count):
    return (count + 127) // 128 * 128


def feed_close(parts, spot, pick, lengths, hidden, z, gy, branch, second, lows, near_sums, far_sums, contexts, outs_w, far, packs, tables, received, cotangent, cot_side, gain, weights):
    tokens, features = hidden.shape
    rows = tokens // 2
    width = contexts[0].shape[1]
    rank = tables[0].shape[1]
    pack, side, far_side = packs
    base = received.shape[0] - 3 * rank
    part = weights[0].shape[0]
    units = 4 * part
    heads = width // HEAD_DIM
    half = features // 2
    tail = lanes_up(width)
    total_lanes = 3 * half + 2 * (2 * units + tail)

    def body(spot_ref, pick_ref, length_ref, hidden_ref, z_ref, gy_ref, branch_in, second_in, lows_ref, near0, near1, far0, far12, c01, c23, wo0, wo1, far_ref, pack_ref, side_ref, far_side_ref, received_ref, oo, wi, no, ca, cb, gain_ref, *refs):
        hbm, (outa_ref, outb_ref, gh_ref, gc_ref, delta_ref, keep_ref, give_ref) = refs[:4], refs[4:11]
        wide, thin, act_ref, grad_ref, far3, ga_ref = refs[11:]
        low_w = lows_ref[rank : 2 * rank]
        low_n = lows_ref[2 * rank : 3 * rank]
        found = far_parts(
            parts, z_ref, gy_ref, hbm, wide, thin, received_ref, far_side_ref, rank, base,
            low_w, low_n, act_ref, grad_ref, far3,
        )
        branch = branch_in[...] + found[0]
        grad_second = second_in[...] + found[1]
        low_next = lows_ref[3 * rank : 4 * rank] + found[2]
        grad_low = lows_ref[4 * rank :] + found[3]
        mask = live_column(spot_ref, length_ref, rows, (0, 2)).astype(f32)
        branch = branch + tn(halves(low_next), twice(no[0]))
        grad_second = grad_second + tn(halves(grad_low), twice(wi[0]))
        hidden_now = hidden_ref[...]
        output = (hidden_now + mask * branch).astype(bf16)
        outa_ref[...] = output[:rows]
        outb_ref[...] = output[rows:]
        _, unit, scaled = normalize(hidden_now, gain_ref[...], gain_ref[...])
        grad_in = jnp.concatenate([ca[0], cb[...]], axis=0).astype(f32)
        grad_hidden = grad_in + normalize_back(grad_second, unit, scaled, gain_ref[...])
        gh_ref[...] = grad_hidden
        ga_ref[...] = (mask * grad_hidden).astype(bf16)
        grad_low_o = nt(oo[0], ga_ref[...])
        low_o2 = halves(grad_low_o)
        inner_o = output_inner_rows(pack_ref, side_ref, received_ref, far_side_ref, rank, base, width)
        contexts_all = [c01[0], c01[1], c23[0], c23[1]]
        weights_all = [wo0, wo1, far_ref.at[0, 0], far_ref.at[1, 0]]
        inner_sums = []
        for i in range(4):
            grad = (nt(weights_all[i][...], ga_ref[...]) + tn(twice(inner_o[i]), low_o2)).astype(bf16)
            gc_ref[i] = grad
            product = grad.astype(f32) * contexts_all[i].astype(f32)
            for h in range(heads):
                delta_ref[heads * i + h] = jnp.sum(
                    product[h * HEAD_DIM : (h + 1) * HEAD_DIM], axis=0, keepdims=True
                )
            inner_sums.append(folded(nt(low_o2, contexts_all[i])))
        core = spot_ref[3] & 1
        quad = spot_ref[2]
        shared = (
            folded(nn(halves(grad_low), z_ref[...])),
            folded(nn(halves(lows_ref[:rank]), ga_ref[...])),
            folded(nn(halves(low_next), gy_ref[...])),
        )
        for n in range(3):
            keep_ref[:, n * half : (n + 1) * half], give_ref[:, n * half : (n + 1) * half] = shares(shared[n], core)
        quarters = []
        for near in (near0, near1):
            quarters.append((near[:rank], near[rank:]))
        for q in range(2):
            lanes = slice(q * part, (q + 1) * part)
            pieces = [far0[0, :, lanes], far12[0, :, lanes], far12[1, :, lanes], far3[0, :, lanes]]
            joined = shuffled(jnp.concatenate(pieces, axis=1), quad)
            quarters.append((joined[:rank], joined[rank:]))
        for i in range(4):
            ref = (keep_ref, give_ref)[i % 2]
            at = 3 * half + (i // 2) * (2 * units + tail)
            ref[:, at : at + units] = quarters[i][0]
            ref[:, at + units : at + 2 * units] = quarters[i][1]
            ref[:, at + 2 * units : at + 2 * units + tail] = padded(inner_sums[i], tail)

    operands = [hidden, z, gy, branch, second, lows] + near_sums + far_sums + contexts + outs_w
    specs = [whole(hidden.shape), KEEP, KEEP, KEEP, KEEP] + [whole(o.shape) for o in operands[5:]]
    operands += [far, pack, side, far_side, received] + tables
    specs += [placed_block((2, 1, width, features), lambda *_: (0, 3, 0, 0))]
    specs += [whole(p.shape) for p in packs] + [whole(received.shape)]
    specs += [placed_block((1, rank, features), of_mine(n)) for n in (3, 4, 5)]
    operands += [cotangent, cot_side, gain] + weights
    specs += [placed_block((1, rows, features), lambda i, spot, *_: (spot[0], 0, 0))]
    specs += [whole(cot_side.shape), whole(gain.shape)] + [KEEP] * 4
    outs = [
        shaped((rows, features), bf16),
        shaped((rows, features), bf16),
        shaped((tokens, features), f32),
        shaped((4, width, tokens), bf16),
        shaped((4 * heads, 1, tokens), f32),
        shaped((rank, total_lanes), f32),
        shaped((rank, total_lanes), f32),
    ]
    scratch = far_scratch(part, features, tokens)
    scratch += [pltpu.VMEM((1, 2 * rank, 2 * part), f32), pltpu.VMEM((tokens, features), bf16)]
    return call(
        body, (spot, pick, lengths), operands, specs, outs, [whole(o.shape) for o in outs], scratch=scratch
    )


def gather_grads(spot, near, far, z, low, packs, received):
    tokens, features = z.shape
    rank = low.shape[0] // 3
    width = near[0].shape[1]
    pack, side, far_side = packs
    base = received.shape[0] - 3 * rank
    half = features // 2
    tail = lanes_up(3 * width)
    total_lanes = 3 * half + 2 * tail

    def body(spot_ref, q01, own01, side01, q23, own23, side23, z_ref, low_ref, pack_ref, side_ref, far_side_ref, received_ref, g_ref, gl_ref, keep_ref, give_ref):
        groups = ((q01, own01, side01), (q23, own23, side23))
        places = ((pack_ref, 0), (side_ref, 0), (received_ref, base), (far_side_ref, 0))
        lows = [halves(low_ref[n * rank : (n + 1) * rank]) for n in range(3)]
        total = [jnp.zeros((rank, tokens), f32) for _ in range(3)]
        core = spot_ref[3] & 1
        for i in range(4):
            q, own, other = groups[i // 2]
            ref, start = places[i]
            outers = []
            for n in range(3):
                if n == 0:
                    g = q[i % 2]
                else:
                    g = (own[i % 2, n - 1] + other[1 - i % 2, n - 1]).astype(bf16)
                g_ref[i, n] = g
                lanes = slice(n * width, (n + 1) * width)
                total[n] = total[n] + nn(ref[start : start + rank, lanes], g)
                outers.append(folded(nt(lows[n], g)))
            at = 3 * half + (i // 2) * tail
            (keep_ref, give_ref)[i % 2][:, at : at + tail] = padded(jnp.concatenate(outers, axis=1), tail)
        for n in range(3):
            gl_ref[n * rank : (n + 1) * rank] = total[n]
            inner = folded(nn(halves(total[n]), z_ref[...]))
            keep_ref[:, n * half : (n + 1) * half], give_ref[:, n * half : (n + 1) * half] = shares(inner, core)

    operands = list(near) + list(far) + [z, low] + list(packs) + [received]
    outs = [
        shaped((4, 3, width, tokens), bf16),
        shaped((3 * rank, tokens), f32),
        shaped((rank, total_lanes), f32),
        shaped((rank, total_lanes), f32),
    ]
    return call(
        body, (spot,), operands, [whole(o.shape) for o in operands], outs, [whole(o.shape) for o in outs]
    )


def settle(spot, pick, keep, moved, common, with_picks):
    rank, lanes = keep.shape
    own = (lanes - common) // 2
    extra = 128 if with_picks else 0

    def body(spot_ref, pick_ref, keep_ref, moved_ref, here_ref, there_ref):
        total = (keep_ref[...] + moved_ref[...]).astype(bf16)
        here_ref[:, : common + own] = total[:, : common + own]
        there_ref[:, :common] = total[:, :common]
        there_ref[:, common : common + own] = total[:, common + own :]
        if with_picks:
            iota = lax.broadcasted_iota(jnp.int32, (rank, 128), 1)
            line = jnp.zeros((rank, 128), f32)
            for n in range(6):
                line = jnp.where(iota == n, pick_ref[spot_ref[0], n].astype(f32), line)
            here_ref[:, common + own :] = line.astype(bf16)
            there_ref[:, common + own :] = line.astype(bf16)

    out = shaped((rank, common + own + extra), bf16)
    return call(body, (spot, pick), [keep, moved], [whole(keep.shape)] * 2, [out, out], [whole(out.shape)] * 2)


def combine(picks, arrays, groups, rows_of_table):
    per, rank = arrays[0].shape[:2]

    def body(pick_ref, *refs):
        ins, outs = refs[: len(arrays)], refs[len(arrays) :]
        outs = [outs[0].at[n] for n in range(3)] + list(outs[1:])
        for out in outs:
            out[...] = jnp.zeros(out.shape, f32)
        for a, ref in enumerate(ins):
            for c in range(per):
                for (start, count, number), out in zip(groups, outs):
                    row = pick_ref[a * per + c, number]
                    out[row] += ref[c, :, start : start + count].astype(f32)

    outs = [shaped((3, rows_of_table, rank, groups[0][1]), f32)]
    outs += [shaped((rows_of_table, rank, count), f32) for _, count, _ in groups[3:]]
    return call(body, (picks,), list(arrays), [whole(a.shape) for a in arrays], outs, [whole(o.shape) for o in outs])


def complete(spot, own, moved):
    _, count, rank, half = own.shape

    def body(spot_ref, own_ref, moved_ref, *outs):
        core = spot_ref[3] & 1
        for n in range(3):
            mine, theirs = own_ref[n], moved_ref[n]
            outs[n][:, :, :half] = jnp.where(core == 0, mine, theirs)
            outs[n][:, :, half:] = jnp.where(core == 0, theirs, mine)

    out = shaped((count, rank, 2 * half), f32)
    return call(body, (spot,), [own, moved], [whole(own.shape)] * 2, [out] * 3, [whole(out.shape)] * 3)


def pair_up(spot, first, second):
    rows, features = first.shape

    def body(spot_ref, first_ref, second_ref, out_ref):
        out_ref[spot_ref[0]] = first_ref[...]
        out_ref[spot_ref[1]] = second_ref[...].astype(first.dtype)

    out = shaped((2, rows, features), first.dtype)
    return call(body, (spot,), [first, second], [whole(first.shape)] * 2, out, whole(out.shape))


def finish(spot, pick, g, gl, inners, weights, far, inputs, received, grad_hidden, gain):
    rows, features = inputs.shape[1:]
    tokens = 2 * rows
    width = g.shape[2]
    rank = gl.shape[0] // 3

    def body(spot_ref, pick_ref, g_ref, gl_ref, iq, ik, iv, *refs):
        ws, (far_ref, xa, xb, gh_ref, gain_ref, grada_ref, gradb_ref) = refs[:6], refs[6:]
        low = [halves(gl_ref[n * rank : (n + 1) * rank]) for n in range(3)]
        total = tn(
            jnp.concatenate(low, axis=0),
            jnp.concatenate([twice(iq[0]), twice(ik[0]), twice(iv[0])], axis=0),
        )
        for i in range(4):
            for n in range(3):
                weight = ws[3 * i + n][...] if i < 2 else far_ref[i - 2, n]
                total = total + tn(g_ref[i, n], weight)
        states = jnp.concatenate([xa[0], xb[...]], axis=0).astype(f32)
        _, unit, scaled = normalize(states, gain_ref[...], gain_ref[...])
        grad = gh_ref[...] + normalize_back(total, unit, scaled, gain_ref[...])
        grada_ref[...] = grad[:rows]
        gradb_ref[...] = grad[rows:].astype(bf16)

    operands = [g, gl] + inners + weights + [far, inputs, received, grad_hidden, gain]
    specs = [whole(g.shape), whole(gl.shape)]
    specs += [placed_block((1, rank, features), of_mine(n)) for n in range(3)]
    specs += [whole(w.shape) for w in weights]
    specs += [placed_block((2, 3, width, features), lambda *_: (0, 0, 0, 0))]
    specs += [placed_block((1, rows, features), lambda i, spot, *_: (spot[0], 0, 0))]
    specs += [placed_block((rows, features), lambda *_: (0, 0)), whole(grad_hidden.shape), whole(gain.shape)]
    outs = [shaped((rows, features), f32), shaped((rows, features), bf16)]
    return call(
        body, (spot, pick), operands, specs, outs, [whole(o.shape) for o in outs],
    )


def make_body(dp_size, tensor_size):
    def across(array):
        return swap(array, "tensor", 2, tensor_size)

    def beside(array):
        return swap(array, "tensor", 1, tensor_size)

    def along(array, bits):
        return swap(array, "dp", bits, dp_size)

    def body(
        inputs,
        cotangent,
        lengths,
        adapter_pick,
        first_gain,
        first_bias,
        query_weight,
        key_weight,
        value_weight,
        output_weight,
        second_gain,
        second_bias,
        widen_weight,
        narrow_weight,
        query_inner,
        query_outer,
        key_inner,
        key_outer,
        value_inner,
        value_outer,
        output_inner,
        output_outer,
        widen_inner,
        widen_outer,
        narrow_inner,
        narrow_outer,
    ):
        rows, features = inputs.shape[1:]
        place = lax.axis_index("tensor")
        quad = lax.axis_index("dp") & 3
        mine = place >> 1
        spot = jnp.stack([mine, 1 - mine, quad, place]).astype(jnp.int32)
        pick = adapter_pick

        def flip(array):
            return jnp.swapaxes(array, 1, 2)

        small = [query_outer, key_outer, value_outer, flip(output_inner), widen_outer, flip(narrow_inner)]
        inners = [flip(query_inner), flip(key_inner), flip(value_inner)]
        tables = [output_outer, flip(widen_inner), narrow_outer]
        gains = [v.reshape(1, -1) for v in (first_gain, first_bias, second_gain, second_bias)]
        heads = [query_weight.T, key_weight.T, value_weight.T, output_weight]
        dense = [widen_weight, narrow_weight]
        width = query_outer.shape[2]
        half = features // 2

        part_heads = stage_heads(spot, heads)
        far0 = across(part_heads)
        near_heads = [beside(w) for w in after(heads, part_heads)]
        send, pack = stage(after(spot, part_heads), pick, inputs, small)
        side = beside(pack)
        part_wide, part_thin, cot_send = stage_dense(after(spot, pack), widen_weight, narrow_weight, cotangent)
        near_dense = [beside(w) for w in after(dense, near_heads)]
        received = across(after(send, far0))
        far1, far2 = along(far0, 1), along(far0, 2)
        side0 = beside(after(far0, side, near_dense, part_wide))
        wide0 = across(after(part_wide, received))
        far3, far4 = along(far2[:2], 1), along(far1[2:], 2)
        side1 = beside(far1)
        z, low, kv01 = project_near(
            after(spot, part_wide, far1, far2, side0), pick, inputs, received, gains[0], gains[1], inners, pack, side,
            [heads[1], heads[2], near_heads[1], near_heads[2]],
        )
        kv01_side = beside(kv01)
        side2 = beside(after(far2, kv01, side1))
        q01 = queries_near(after(z, kv01), low, pack, side, [heads[0], near_heads[0]])
        far_side = beside(after(received[rows:], q01))
        side3, side4 = beside(after(far3, q01, side2)), beside(after(far4, q01, side2))
        c01, total01 = attend(after(spot, side2), lengths, q01, kv01, kv01_side)
        wide1, wide2 = along(after(wide0, c01), 1), along(after(wide0, c01), 2)
        cot_side = across(after(cot_send, c01, wide0))
        far, kv23 = project_far(
            after(spot, c01, wide0), z, low, received, far_side,
            [[far0, far1, far2, far3, far4], [side0, side1, side2, side3, side4]],
        )
        kv23_side = beside(kv23)
        q23 = queries_far(after(z, kv23), low, received, far_side, far)
        c23, total23 = attend(spot, lengths, q23, kv23, kv23_side)
        thin0 = across(after(part_thin, c23))
        packs = [pack, side, far_side]
        outs_w = [heads[3], near_heads[3]]
        hidden, z2, lows = feed_open(
            spot, pick, lengths, [c01, c23], outs_w, far, packs, tables, inputs, received, gains[2], gains[3]
        )
        wide3 = along(after(wide2, lows), 1)
        wide_sides = [beside(after(w, lows, wide1, wide2)) for w in (wide0, wide1, wide2)]
        gy, branch, second, lows, sums0 = feed_first(
            spot, pick, lengths, z2, lows, tables[2], cotangent, cot_side, pack, dense
        )
        wide_sides.append(beside(after(wide3, lows)))
        thin1, thin2 = along(after(thin0, lows), 1), along(after(thin0, lows), 2)
        thin_sides = [beside(after(thin0, lows))]
        branch, second, lows, sums1 = feed_near(
            z2, gy, branch, second, after(lows, wide_sides[:3], thin0, wide3), side, near_dense
        )
        thin3 = along(after(thin1, sums1), 2)
        thin_sides += [beside(after(t, sums1)) for t in (thin1, thin2)]
        branch, second, lows, sums2 = feed_far(
            (0,), z2, gy, branch, second, after(lows, thin1, thin2), received, far_side,
            [wide0, wide_sides[0], thin0, thin_sides[0]],
        )
        thin_sides.append(beside(after(thin3, sums2)))
        branch, second, lows, sums3 = feed_far(
            (1, 2), z2, gy, branch, second, after(lows, thin3), received, far_side,
            [wide1, wide_sides[1], thin1, thin_sides[1], wide2, wide_sides[2], thin2, thin_sides[2]],
        )
        outa, outb, grad_hidden, grad_context, deltas, keep, give = feed_close(
            (3,), spot, pick, lengths, hidden, z2, gy, branch, second, lows, [sums0, sums1], [sums2, sums3],
            [c01, c23], outs_w, far, packs, tables, received, cotangent, cot_side, gains[2],
            [wide3, wide_sides[3], thin3, thin_sides[3]],
        )

        def crossing(here, other):
            both = jnp.stack([here, other])
            return along(both, 4)

        def first_turn(here, other, crossed):
            one = jnp.stack([here, crossed[0]])
            two = jnp.stack([other, crossed[1]])
            return [(one, along(one, 1)), (two, along(two, 2))]

        def second_turn(turns):
            one, two = [jnp.concatenate(t) for t in turns]
            return [one, along(one, 2), two, along(two, 1)]

        def whole_sum(table):
            bits = 8
            while bits < dp_size:
                table = table + along(table, bits)
                bits *= 2
            return table

        moved = beside(give)
        here, there = settle(spot, pick, keep, moved, 3 * half, True)
        other = across(there)
        gq01, own01, other01 = attend_back(
            after(spot, here), lengths, q01, kv01, kv01_side, grad_context, total01, deltas, 0
        )
        side01 = beside(other01)
        crossed = crossing(here, after(other, gq01))
        out_side = across(after(outb, other, gq01))
        gq23, own23, other23 = attend_back(
            after(spot, gq01, other), lengths, q23, kv23, kv23_side, grad_context, total23, deltas, 1
        )
        side23 = beside(other23)
        turns = first_turn(here, other, after(crossed, gq23))
        output = pair_up(after(spot, gq23), outa, out_side)
        g, gl, keep, give = gather_grads(
            after(spot, output), (gq01, own01, side01), (gq23, own23, side23), z, low, packs, received
        )
        moved = beside(give)
        early = second_turn(after(turns, g))
        here, there = settle(spot, pick, keep, moved, 3 * half, False)
        other = across(there)
        crossed = crossing(here, other)
        grada, gradb = finish(
            after(spot, other), pick, g, gl, inners, heads[:3] + near_heads[:3], far, inputs, received, grad_hidden,
            gains[0],
        )
        grad_side = across(after(gradb, crossed))
        turns = first_turn(here, other, after(crossed, grada))
        picks = jnp.concatenate([a[:, 0, -128:-122] for a in early]).astype(jnp.int32)
        adapters = query_inner.shape[0]
        units = widen_weight.shape[1]
        base = 3 * half
        early = combine(
            after(picks, grada),
            early,
            [
                (0, half, 4),
                (half, half, 3),
                (2 * half, half, 5),
                (base, units, 4),
                (base + units, units, 5),
                (base + 2 * units, width, 3),
            ],
            adapters,
        )
        early = [whole_sum(t) for t in early]
        early_shared = complete(spot, early[0], beside(early[0]))
        late = second_turn(turns)
        input_grad = pair_up(spot, grada, grad_side)
        late = combine(
            picks,
            late,
            [(n * half, half, n) for n in range(3)] + [(base + n * width, width, n) for n in range(3)],
            adapters,
        )
        late = [whole_sum(t) for t in late]
        late_shared = complete(spot, late[0], beside(late[0]))
        return (
            output,
            input_grad,
            flip(late_shared[0]),
            late[1],
            flip(late_shared[1]),
            late[2],
            flip(late_shared[2]),
            late[3],
            flip(early[3]),
            early_shared[1],
            flip(early_shared[0]),
            early[1],
            flip(early[2]),
            early_shared[2],
        )

    return body


def solution(mesh):
    placed = (
        P("dp", "tensor", None),
        P("dp", "tensor", None),
        P("dp"),
        P("dp", None),
        P(),
        P(),
        P(None, "tensor"),
        P(None, "tensor"),
        P(None, "tensor"),
        P("tensor", None),
        P(),
        P(),
        P(None, "tensor"),
        P("tensor", None),
        P(),
        P(None, None, "tensor"),
        P(),
        P(None, None, "tensor"),
        P(),
        P(None, None, "tensor"),
        P(None, "tensor", None),
        P(),
        P(),
        P(None, None, "tensor"),
        P(None, "tensor", None),
        P(),
    )
    return jax.shard_map(
        make_body(mesh.shape["dp"], mesh.shape["tensor"]),
        mesh=mesh,
        in_specs=placed,
        out_specs=(
            P("dp", "tensor", None),
            P("dp", "tensor", None),
            P(),
            P(None, None, "tensor"),
            P(),
            P(None, None, "tensor"),
            P(),
            P(None, None, "tensor"),
            P(None, "tensor", None),
            P(),
            P(),
            P(None, None, "tensor"),
            P(None, "tensor", None),
            P(),
        ),
        check_vma=False,
    )
```

```python
import functools
import math

import jax
import jax.numpy as jnp
from jax import lax
from jax.experimental import pallas as pl
from jax.experimental.pallas import tpu as pltpu
from jax.sharding import PartitionSpec as P

HEAD_DIM = 80
f32 = jnp.float32
bf16 = jnp.bfloat16
neg_fill = -1000000000.0
score_scale = 1.0 / math.sqrt(HEAD_DIM)
log2_e = math.log2(math.e)
LIMIT = 16
KEEP = pl.BlockSpec(memory_space=pltpu.VMEM)
remain = pl.BlockSpec(memory_space=pl.ANY)


def swap(array, axis, bits, size):
    return lax.ppermute(array, axis, [(i, i ^ bits) for i in range(size)])


def nn(a, b):
    return jnp.dot(a, b, preferred_element_type=f32)


def nt(a, b):
    return lax.dot_general(a, b, (((1,), (1,)), ((), ())), preferred_element_type=f32)


def tn(a, b):
    return lax.dot_general(a, b, (((0,), (0,)), ((), ())), preferred_element_type=f32)


def halves(low):
    top = low.astype(bf16)
    return jnp.concatenate([top, (low - top.astype(f32)).astype(bf16)], axis=0)


def twice(factor):
    return jnp.concatenate([factor, factor], axis=0)


def folded(pair):
    count = pair.shape[0] // 2
    return pair[:count] + pair[count:]


def normalize(states, gain, shift):
    centre = states - jnp.mean(states, axis=-1, keepdims=True)
    scaled = lax.rsqrt(jnp.mean(centre * centre, axis=-1, keepdims=True) + 1e-05)
    unit = centre * scaled
    return unit * gain + shift, unit, scaled


def normalize_back(grad_rows, unit, scaled, gain):
    grad_unit = grad_rows * gain
    return scaled * (
        grad_unit
        - jnp.mean(grad_unit, axis=-1, keepdims=True)
        - unit * jnp.mean(grad_unit * unit, axis=-1, keepdims=True)
    )


def live_column(spot_ref, length_ref, rows, bits):
    iota = lax.broadcasted_iota(jnp.int32, (2 * rows, 1), 0)
    place = spot_ref[3]
    first, second = place ^ bits[0], place ^ bits[1]
    position = jnp.where(iota < rows, first * rows + iota, second * rows + iota - rows)
    return position < length_ref[spot_ref[0]]


def whole(shape):
    return KEEP


def placed_block(shape, index):
    return pl.BlockSpec(shape, index, pipeline_mode=pl.Buffered(1))


def call(body, scalars, operands, specs, outs, out_specs, grid=(1,), scratch=(), limit=LIMIT, aliases=None, weight=100):
    return pl.pallas_call(
        body,
        grid_spec=pltpu.PrefetchScalarGridSpec(
            num_scalar_prefetch=len(scalars),
            grid=grid,
            in_specs=specs,
            out_specs=out_specs,
            scratch_shapes=list(scratch),
        ),
        out_shape=outs,
        cost_estimate=pl.CostEstimate(flops=weight * 10**9, bytes_accessed=100000, transcendentals=0),
        input_output_aliases=aliases or {},
        compiler_params=pltpu.CompilerParams(vmem_limit_bytes=limit * 2**20),
    )(*scalars, *operands)


def shaped(shape, dtype):
    return jax.ShapeDtypeStruct(shape, dtype)


def of_mine(number):
    return lambda i, spot, pick, *_: (pick[spot[0], number], 0, 0)


def of_other(number):
    return lambda i, spot, pick, *_: (pick[spot[1], number], 0, 0)


def after(values, *others):
    return lax.optimization_barrier((values, others))[0]


def shuffled(array, quad):
    count = array.shape[1] // 4
    blocks = [array[:, n * count : (n + 1) * count] for n in range(4)]
    for bits in (1, 2):
        on = ((quad >> (bits - 1)) & 1) == 1
        blocks = [jnp.where(on, blocks[n ^ bits], blocks[n]) for n in range(4)]
    return jnp.concatenate(blocks, axis=1)


def stage(spot, pick, inputs, factors):
    rows, features = inputs.shape[1:]
    rank = factors[0].shape[1]

    def body(spot_ref, pick_ref, inputs_ref, *refs):
        send_ref, pack_ref = refs[12:]
        send_ref[:rows] = inputs_ref[0]
        quad = spot_ref[2]
        for group, ref, base in ((refs[:6], pack_ref, 0), (refs[6:12], send_ref, rows)):
            ref[base : base + rank] = jnp.concatenate([r[0] for r in group[:4]], axis=1)
            wide, thin = group[4][0], group[5][0]
            if base:
                wide, thin = shuffled(wide, quad), shuffled(thin, quad)
            ref[base + rank : base + 2 * rank] = wide
            ref[base + 2 * rank : base + 3 * rank] = thin

    specs = [placed_block((1, rows, features), lambda i, spot, *_: (spot[1], 0, 0))]
    for of in (of_mine, of_other):
        specs += [placed_block((1,) + f.shape[1:], of(n)) for n, f in enumerate(factors)]
    outs = [shaped((rows + 3 * rank, features), bf16), shaped((3 * rank, features), bf16)]
    return call(body, (spot, pick), [inputs] + factors * 2, specs, outs, [whole(o.shape) for o in outs])


def stage_heads(spot, heads):
    features = heads[0].shape[1]
    head_rows = heads[0].shape[0] // 4

    def body(spot_ref, *refs):
        out, sems = refs[4:]
        at = pl.ds(pl.multiple_of(spot_ref[2] * head_rows, 16), head_rows)
        copies = [pltpu.make_async_copy(refs[n].at[at], out.at[n], sems.at[n]) for n in range(4)]
        for c in copies:
            c.start()
        for c in copies:
            c.wait()

    out = shaped((4, head_rows, features), bf16)
    return call(body, (spot,), heads, [remain] * 4, out, KEEP, scratch=[pltpu.SemaphoreType.DMA((4,))])


def stage_dense(spot, wide, thin, cotangent):
    features, units = wide.shape
    part = units // 4
    rows = cotangent.shape[1]

    def body(spot_ref, wide_ref, thin_ref, last_ref, cot_ref, wide_out, thin_out, last_out, cot_out):
        for r in range(4):

            @pl.when(spot_ref[2] == r)
            def _():
                wide_out[...] = wide_ref[:, r * part : (r + 1) * part].T

        thin_out[...] = thin_ref[...]
        last_out[...] = last_ref[...]
        cot_out[...] = cot_ref[0]

    specs = [
        whole(wide.shape),
        placed_block((part, features), lambda i, spot: (spot[2], 0)),
        placed_block((part, features), lambda i, spot: (spot[2] ^ 3, 0)),
        placed_block((1, rows, features), lambda i, spot: (spot[1], 0, 0)),
    ]
    outs = [shaped((part, features), bf16)] * 3 + [shaped((rows, features), bf16)]
    return call(body, (spot,), [wide, thin, thin, cotangent], specs, outs, [whole(o.shape) for o in outs])


def project_rows(weight, rows_in, outer, low):
    return (nt(weight, rows_in) + tn(twice(outer), halves(low))).astype(bf16)


def project_near(spot, pick, inputs, received, gain, shift, inners, pack, side, weights):
    rows, features = inputs.shape[1:]
    tokens = 2 * rows
    width = weights[0].shape[0]
    rank = inners[0].shape[1]

    def body(spot_ref, pick_ref, xa, xb, gain_ref, shift_ref, iq, ik, iv, pack_ref, side_ref, *refs):
        ws, (z_ref, low_ref, kv_ref) = refs[:4], refs[4:]
        states = jnp.concatenate([xa[0], xb[...]], axis=0).astype(f32)
        z_ref[...] = normalize(states, gain_ref[...], shift_ref[...])[0].astype(bf16)
        low = nt(jnp.concatenate([iq[0], ik[0], iv[0]], axis=0), z_ref[...])
        low_ref[...] = low
        for i, packs in enumerate((pack_ref, side_ref)):
            for n in (1, 2):
                outer = packs[:rank, n * width : (n + 1) * width]
                kv_ref[i, n - 1] = project_rows(
                    ws[2 * i + n - 1][...], z_ref[...], outer, low[n * rank : (n + 1) * rank]
                )

    specs = [
        placed_block((1, rows, features), lambda i, spot, *_: (spot[0], 0, 0)),
        placed_block((rows, features), lambda *_: (0, 0)),
        whole((1, features)),
        whole((1, features)),
    ]
    specs += [placed_block((1, rank, features), of_mine(n)) for n in range(3)]
    specs += [whole(pack.shape), whole(side.shape)] + [whole((width, features))] * 4
    outs = [
        shaped((tokens, features), bf16),
        shaped((3 * rank, tokens), f32),
        shaped((2, 2, width, tokens), bf16),
    ]
    return call(
        body,
        (spot, pick),
        [inputs, received, gain, shift] + inners + [pack, side] + weights,
        specs,
        outs,
        [whole(o.shape) for o in outs],
    )


def queries_near(z, low, pack, side, weights):
    tokens, features = z.shape
    width = weights[0].shape[0]
    rank = low.shape[0] // 3

    def body(z_ref, low_ref, pack_ref, side_ref, w0, w1, q_ref):
        for i, (packs, w) in enumerate(((pack_ref, w0), (side_ref, w1))):
            q_ref[i] = project_rows(w[...], z_ref[...], packs[:rank, :width], low_ref[:rank])

    operands = [z, low, pack, side] + weights
    out = shaped((2, width, tokens), bf16)
    return call(body, (), operands, [whole(o.shape) for o in operands], out, whole(out.shape))


def project_far(spot, z, low, received, side, parts):
    tokens, features = z.shape
    head_rows = parts[0][0].shape[1]
    width = 4 * head_rows
    rank = low.shape[0] // 3
    base = received.shape[0] - 3 * rank
    flat = [p for group in parts for p in group]

    def body(spot_ref, z_ref, low_ref, received_ref, side_ref, *refs):
        ins, (out_ref, kv_ref, weight_ref, sems) = refs[:10], refs[10:]
        for i in range(2):
            group = ins[5 * i : 5 * i + 5]
            for n in range(4):
                for r in range(4):
                    at = pl.ds(pl.multiple_of((spot_ref[0] ^ r) * head_rows, 16), head_rows)
                    if r < 3:
                        weight_ref[i, n, at] = group[r][n]
                    else:
                        weight_ref[i, n, at] = group[3 + n // 2][n % 2]
        copies = [pltpu.make_async_copy(weight_ref.at[i], out_ref.at[i], sems.at[i]) for i in range(2)]
        for c in copies:
            c.start()
        for i, (ref, start) in enumerate(((received_ref, base), (side_ref, 0))):
            for n in (1, 2):
                outer = ref[start : start + rank, n * width : (n + 1) * width]
                kv_ref[i, n - 1] = project_rows(
                    weight_ref[i, n], z_ref[...], outer, low_ref[n * rank : (n + 1) * rank]
                )
        for c in copies:
            c.wait()

    operands = [z, low, received, side] + flat
    outs = [shaped((2, 4, width, features), bf16), shaped((2, 2, width, tokens), bf16)]
    return call(
        body, (spot[2:3],), operands, [KEEP] * len(operands), outs, [remain, KEEP],
        scratch=[pltpu.VMEM((2, 4, width, features), bf16), pltpu.SemaphoreType.DMA((2,))],
    )


def queries_far(z, low, received, side, far):
    tokens, features = z.shape
    width = far.shape[2]
    rank = low.shape[0] // 3
    base = received.shape[0] - 3 * rank

    def body(z_ref, low_ref, received_ref, side_ref, far_ref, q_ref):
        for i, (ref, start) in enumerate(((received_ref, base), (side_ref, 0))):
            outer = ref[start : start + rank, :width]
            q_ref[i] = project_rows(far_ref[i, 0], z_ref[...], outer, low_ref[:rank])

    operands = [z, low, received, side, far]
    specs = [whole(o.shape) for o in operands[:4]] + [placed_block((2, 1, width, features), lambda *_: (0, 0, 0, 0))]
    out = shaped((2, width, tokens), bf16)
    return call(body, (), operands, specs, out, whole(out.shape))


def attend(spot, lengths, q, kv, kv_side):
    _, width, tokens = q.shape
    rows = tokens // 2
    pair = 2 * HEAD_DIM
    steps = width // pair

    def body(spot_ref, length_ref, q_ref, k1, k2, v1, v2, ctx_ref, total_ref):
        bias1 = jnp.where(live_column(spot_ref, length_ref, rows, (0, 2)), 0.0, neg_fill * log2_e)
        bias2 = jnp.where(live_column(spot_ref, length_ref, rows, (1, 3)), 0.0, neg_fill * log2_e)
        for h in range(2):
            at = slice(h * HEAD_DIM, (h + 1) * HEAD_DIM)
            query = q_ref[0, at]
            s1 = tn(k1[0, 0, at], query) * (score_scale * log2_e) + bias1
            s2 = tn(k2[0, 0, at], query) * (score_scale * log2_e) + bias2
            top = jnp.maximum(jnp.max(s1, axis=0, keepdims=True), jnp.max(s2, axis=0, keepdims=True))
            p1 = jnp.exp2(s1 - top)
            p2 = jnp.exp2(s2 - top)
            total = jnp.sum(p1, axis=0, keepdims=True) + jnp.sum(p2, axis=0, keepdims=True)
            context = nn(v1[0, 0, at], p1.astype(bf16)) + nn(v2[0, 0, at], p2.astype(bf16))
            ctx_ref[0, at] = (context * (1.0 / total)).astype(bf16)
            total_ref[h] = top + jnp.log2(total)

    def own(n):
        return pl.BlockSpec((1, 1, pair, tokens), lambda h, *_: (h // steps, n, h % steps, 0))

    def beside(n):
        return pl.BlockSpec((1, 1, pair, tokens), lambda h, *_: (1 - h // steps, n, h % steps, 0))

    rows_spec = pl.BlockSpec((1, pair, tokens), lambda h, *_: (h // steps, h % steps, 0))
    return call(
        body,
        (spot, lengths),
        [q, kv, kv_side, kv, kv_side],
        [rows_spec, own(0), beside(0), own(1), beside(1)],
        [shaped(q.shape, bf16), shaped((4 * steps, 1, tokens), f32)],
        [rows_spec, pl.BlockSpec((2, 1, tokens), lambda h, *_: (h, 0, 0))],
        grid=(2 * steps,),
    )


def attend_back(spot, lengths, q, kv, kv_side, grad_context, totals, deltas, number):
    _, width, tokens = q.shape
    rows = tokens // 2
    pair = 2 * HEAD_DIM
    steps = width // pair
    at_hand = number % 2

    def body(spot_ref, length_ref, q_ref, k1, k2, v1, v2, g_ref, total_ref, delta_ref, gq, own_ref, other_ref):
        bias1 = jnp.where(live_column(spot_ref, length_ref, rows, (0, 2)), 0.0, neg_fill * log2_e)
        bias2 = jnp.where(live_column(spot_ref, length_ref, rows, (1, 3)), 0.0, neg_fill * log2_e)
        for h in range(2):
            at = slice(h * HEAD_DIM, (h + 1) * HEAD_DIM)
            query = q_ref[0, at]
            grad = g_ref[0, at]
            grad_query = None
            for k, v, bias, out in ((k1, v1, bias1, own_ref), (k2, v2, bias2, other_ref)):
                s = tn(k[0, 0, at], query) * (score_scale * log2_e) + bias
                soft = jnp.exp2(s - total_ref[h])
                grad_soft = tn(v[0, 0, at], grad)
                grad_scores = (soft * (grad_soft - delta_ref[h])).astype(bf16)
                part = nn(k[0, 0, at], grad_scores)
                grad_query = part if grad_query is None else grad_query + part
                out[0, at] = (nt(query, grad_scores) * score_scale).astype(out.dtype)
                out[1, at] = nt(grad, soft.astype(bf16)).astype(out.dtype)
            gq[at] = (grad_query * score_scale).astype(bf16)

    def own(n):
        return pl.BlockSpec((1, 1, pair, tokens), lambda h, *_: (at_hand, n, h, 0))

    def beside(n):
        return pl.BlockSpec((1, 1, pair, tokens), lambda h, *_: (1 - at_hand, n, h, 0))

    rows_spec = pl.BlockSpec((1, pair, tokens), lambda h, *_: (at_hand, h, 0))
    grads_spec = pl.BlockSpec((1, pair, tokens), lambda h, *_: (number, h, 0))
    line = pl.BlockSpec((2, 1, tokens), lambda h, *_: (steps * at_hand + h, 0, 0))
    line_at = pl.BlockSpec((2, 1, tokens), lambda h, *_: (steps * number + h, 0, 0))
    both = pl.BlockSpec((2, pair, tokens), lambda h, *_: (0, h, 0))
    return call(
        body,
        (spot, lengths),
        [q, kv, kv_side, kv, kv_side, grad_context, totals, deltas],
        [rows_spec, own(0), beside(0), own(1), beside(1), grads_spec, line, line_at],
        [shaped(q.shape[1:], bf16), shaped(kv.shape[1:], f32), shaped(kv.shape[1:], bf16)],
        [pl.BlockSpec((pair, tokens), lambda h, *_: (h, 0)), both, both],
        grid=(steps,), weight=8)


cubic = 0.044715
root = math.sqrt(2.0 / math.pi)


def bend_of(widened, grad):
    square = widened * widened
    bend = jnp.tanh(root * widened * (1.0 + cubic * square))
    up = 0.5 * (1.0 + bend)
    slope = up + widened * (0.5 * root) * (1.0 - bend * bend) * (1.0 + 3.0 * cubic * square)
    return (widened * up).astype(bf16), (grad * slope).astype(bf16)


def feed_quarter(z_ref, gy_ref, wide_ref, thin_ref, pack_ref, rank, low_w, low_n, act_ref, grad_ref, sums_ref, ready=None):
    units = wide_ref.shape[1]
    block = 256
    low_w2, low_n2 = halves(low_w), halves(low_n)

    def step(b, carry):
        if ready is not None:
            ready(b)
        at = pl.ds(pl.multiple_of(b * block, block), block)
        widened = nn(z_ref[...], wide_ref[:, at]) + tn(low_w2, twice(pack_ref[rank : 2 * rank, at]))
        grad = nt(gy_ref[...], thin_ref[at, :]) + tn(low_n2, twice(pack_ref[2 * rank : 3 * rank, at]))
        act_ref[:, at], grad_ref[:, at] = bend_of(widened, grad)
        return carry

    lax.fori_loop(0, units // block, step, 0)
    sums_ref[:rank] = folded(nn(low_w2, grad_ref[...]))
    sums_ref[rank:] = folded(nn(low_n2, act_ref[...]))
    return (
        nn(act_ref[...], thin_ref[...]),
        nt(grad_ref[...], wide_ref[...]),
        nt(pack_ref[2 * rank : 3 * rank], act_ref[...]),
        nt(pack_ref[rank : 2 * rank], grad_ref[...]),
    )


def feed_units(z_ref, gy_ref, wide_ref, thin_ref, outer, inner, low_w, low_n, act_ref, grad_ref, ready):
    units = wide_ref.shape[0]
    block = 256
    low_w2, low_n2 = halves(low_w), halves(low_n)
    for start in range(0, units, block):
        ready(start // block)
        at = slice(start, min(start + block, units))
        widened = nt(z_ref[...], wide_ref[at]) + tn(low_w2, twice(outer[:, at]))
        grad = nt(gy_ref[...], thin_ref[at]) + tn(low_n2, twice(inner[:, at]))
        act_ref[:, at], grad_ref[:, at] = bend_of(widened, grad)
    sums = jnp.concatenate(
        [folded(nn(low_w2, grad_ref[...])), folded(nn(low_n2, act_ref[...]))], axis=0
    )
    return (
        nn(act_ref[...], thin_ref[...]),
        nn(grad_ref[...], wide_ref[...]),
        nt(inner, act_ref[...]),
        nt(outer, grad_ref[...]),
        sums,
    )


def output_inner_rows(pack_ref, side_ref, received_ref, far_side_ref, rank, base, width):
    lanes = slice(3 * width, 4 * width)
    return [
        pack_ref[:rank, lanes],
        side_ref[:rank, lanes],
        received_ref[base : base + rank, lanes],
        far_side_ref[:rank, lanes],
    ]


def feed_open(spot, pick, lengths, contexts, outs_w, far, packs, tables, inputs, received, gain, shift):
    rows, features = inputs.shape[1:]
    tokens = 2 * rows
    width = contexts[0].shape[1]
    rank = tables[0].shape[1]
    pack, side, far_side = packs
    base = received.shape[0] - 3 * rank

    def body(spot_ref, pick_ref, length_ref, c01, c23, wo0, wo1, far_ref, pack_ref, side_ref, far_side_ref, received_ref, oo, wi, xa, gain_ref, shift_ref, hidden_ref, z_ref, lows_ref):
        states = jnp.concatenate([xa[0], received_ref[:rows]], axis=0).astype(f32)
        mask = live_column(spot_ref, length_ref, rows, (0, 2)).astype(f32)
        inner_o = output_inner_rows(pack_ref, side_ref, received_ref, far_side_ref, rank, base, width)
        contexts_all = [c01[0], c01[1], c23[0], c23[1]]
        weights_all = [wo0[...], wo1[...], far_ref[0, 0], far_ref[1, 0]]
        joined = jnp.concatenate(contexts_all, axis=0)
        attended = tn(joined, jnp.concatenate(weights_all, axis=0))
        low_o = nn(jnp.concatenate(inner_o, axis=1), joined)
        attended = attended + tn(halves(low_o), twice(oo[0]))
        hidden = states + mask * attended
        hidden_ref[...] = hidden
        z_ref[...] = normalize(hidden, gain_ref[...], shift_ref[...])[0].astype(bf16)
        lows_ref[:rank] = low_o
        lows_ref[rank:] = nt(wi[0], z_ref[...])

    operands = contexts + outs_w + [far, pack, side, far_side, received] + tables[:2]
    specs = [whole(c.shape) for c in contexts] + [whole(w.shape) for w in outs_w]
    specs += [placed_block((2, 1, width, features), lambda *_: (0, 3, 0, 0))]
    specs += [whole(p.shape) for p in packs] + [whole(received.shape)]
    specs += [placed_block((1, rank, features), of_mine(n)) for n in (3, 4)]
    operands += [inputs, gain, shift]
    specs += [placed_block((1, rows, features), lambda i, spot, *_: (spot[0], 0, 0))]
    specs += [whole(gain.shape), whole(shift.shape)]
    outs = [shaped((tokens, features), f32), shaped((tokens, features), bf16), shaped((2 * rank, tokens), f32)]
    return call(body, (spot, pick, lengths), operands, specs, outs, [KEEP] * 3)


def feed_first(spot, pick, lengths, z, lows, table, cotangent, cot_side, pack, dense):
    tokens, features = z.shape
    rows = tokens // 2
    rank = table.shape[1]
    units = dense[0].shape[1]

    def body(spot_ref, pick_ref, length_ref, z_ref, lows_in, no, ca, cb, pack_ref, wide, thin, gy_ref, branch_ref, second_ref, lows_ref, sums_ref, act_ref, grad_ref):
        mask = live_column(spot_ref, length_ref, rows, (0, 2)).astype(f32)
        grad_in = jnp.concatenate([ca[0], cb[...]], axis=0).astype(f32)
        gy_ref[...] = (mask * grad_in).astype(bf16)
        low_n = nt(no[0], gy_ref[...])
        lows_ref[: 2 * rank] = lows_in[...]
        lows_ref[2 * rank : 3 * rank] = low_n
        branch_ref[...], second_ref[...], lows_ref[3 * rank : 4 * rank], lows_ref[4 * rank :] = feed_quarter(
            z_ref, gy_ref, wide, thin, pack_ref, rank, lows_in[rank:], low_n, act_ref, grad_ref, sums_ref
        )

    operands = [z, lows, table, cotangent, cot_side, pack] + dense
    specs = [KEEP, KEEP, placed_block((1, rank, features), of_mine(5))]
    specs += [placed_block((1, rows, features), lambda i, spot, *_: (spot[0], 0, 0))] + [KEEP] * 4
    outs = [
        shaped((tokens, features), bf16),
        shaped((tokens, features), f32),
        shaped((tokens, features), f32),
        shaped((5 * rank, tokens), f32),
        shaped((2 * rank, units), f32),
    ]
    scratch = [pltpu.VMEM((tokens, units), bf16)] * 2
    return call(body, (spot, pick, lengths), operands, specs, outs, [KEEP] * 5, scratch=scratch)


def feed_near(z, gy, branch, second, lows, pack, dense):
    tokens, features = z.shape
    units = dense[0].shape[1]
    rank = lows.shape[0] // 5
    blocks = units // 256

    def body(z_ref, gy_ref, branch_in, second_in, lows_in, pack_ref, wide_hbm, thin_hbm, branch_ref, second_ref, lows_ref, sums_ref, wide, thin, act_ref, grad_ref, sems):
        def copies(b):
            at = pl.ds(pl.multiple_of(b * 256, 256), 256)
            return (
                pltpu.make_async_copy(wide_hbm.at[:, at], wide.at[:, at], sems.at[0, b]),
                pltpu.make_async_copy(thin_hbm.at[at], thin.at[at], sems.at[1, b]),
            )

        for b in range(blocks):
            for c in copies(b):
                c.start()

        def ready(b):
            for c in copies(b):
                c.wait()

        sums = feed_quarter(
            z_ref, gy_ref, wide, thin, pack_ref, rank, lows_in[rank : 2 * rank], lows_in[2 * rank : 3 * rank],
            act_ref, grad_ref, sums_ref, ready,
        )
        branch_ref[...] = branch_in[...] + sums[0]
        second_ref[...] = second_in[...] + sums[1]
        lows_ref[: 3 * rank] = lows_in[: 3 * rank]
        lows_ref[3 * rank : 4 * rank] = lows_in[3 * rank : 4 * rank] + sums[2]
        lows_ref[4 * rank :] = lows_in[4 * rank :] + sums[3]

    operands = [z, gy, branch, second, lows, pack] + dense
    outs = [shaped(branch.shape, f32), shaped(second.shape, f32), shaped(lows.shape, f32), shaped((2 * rank, units), f32)]
    scratch = [pltpu.VMEM(d.shape, bf16) for d in dense] + [pltpu.VMEM((tokens, units), bf16)] * 2
    scratch += [pltpu.SemaphoreType.DMA((2, blocks))]
    return call(
        body, (), operands, [KEEP] * 6 + [remain] * 2, outs, [KEEP] * 4, scratch=scratch, aliases={2: 0, 3: 1}, limit=24
    )


def far_copies(count, ins, wide, thin, sems):
    part = ins[0].shape[0]
    copies = []
    for n in range(count):
        for q in range(2):
            at = slice(q * part, (q + 1) * part)
            copies.append(pltpu.make_async_copy(ins[4 * n + q], wide.at[n, at], sems.at[4 * n + 2 * q]))
            copies.append(pltpu.make_async_copy(ins[4 * n + 2 + q], thin.at[n, at], sems.at[4 * n + 2 * q + 1]))
    for c in copies:
        c.start()
    return copies


def far_parts(parts, z_ref, gy_ref, copies, wide, thin, received_ref, far_side_ref, rank, base, low_w, low_n, act_ref, grad_ref, sums_ref):
    count = wide.shape[1] // 2
    total = None
    for n, r in enumerate(parts):
        lanes = slice(r * count, (r + 1) * count)
        outer = jnp.concatenate(
            [received_ref[base + rank : base + 2 * rank, lanes], far_side_ref[rank : 2 * rank, lanes]], axis=1
        )
        inner = jnp.concatenate(
            [received_ref[base + 2 * rank : base + 3 * rank, lanes], far_side_ref[2 * rank : 3 * rank, lanes]], axis=1
        )

        def ready(b):
            if b < 2:
                for c in copies[4 * n + 2 * b : 4 * n + 2 * b + 2]:
                    c.wait()

        found = feed_units(
            z_ref, gy_ref, wide.at[n], thin.at[n], outer, inner, low_w, low_n, act_ref, grad_ref, ready
        )
        sums_ref[n] = found[4]
        total = found[:4] if total is None else [a + b for a, b in zip(total, found[:4])]
    return total


def far_scratch(count, part, features, tokens):
    return [pltpu.VMEM((count, 2 * part, features), bf16)] * 2 + [pltpu.VMEM((tokens, 2 * part), bf16)] * 2 + [
        pltpu.SemaphoreType.DMA((4 * count,))
    ]


def feed_far(parts, z, gy, branch, second, lows, received, far_side, weights):
    tokens, features = z.shape
    part = weights[0].shape[0]
    rank = lows.shape[0] // 5
    base = received.shape[0] - 3 * rank
    count = len(weights)

    def body(z_ref, gy_ref, branch_in, second_in, lows_in, received_ref, far_side_ref, *refs):
        ins, (branch_ref, second_ref, lows_ref, sums_ref) = refs[:count], refs[count : count + 4]
        wide, thin, act_ref, grad_ref, sems = refs[count + 4 :]
        copies = far_copies(len(parts), ins, wide, thin, sems)
        total = far_parts(
            parts, z_ref, gy_ref, copies, wide, thin, received_ref, far_side_ref, rank, base,
            lows_in[rank : 2 * rank], lows_in[2 * rank : 3 * rank], act_ref, grad_ref, sums_ref,
        )
        branch_ref[...] = branch_in[...] + total[0]
        second_ref[...] = second_in[...] + total[1]
        lows_ref[: 3 * rank] = lows_in[: 3 * rank]
        lows_ref[3 * rank : 4 * rank] = lows_in[3 * rank : 4 * rank] + total[2]
        lows_ref[4 * rank :] = lows_in[4 * rank :] + total[3]

    operands = [z, gy, branch, second, lows, received, far_side] + weights
    outs = [
        shaped(branch.shape, f32),
        shaped(second.shape, f32),
        shaped(lows.shape, f32),
        shaped((len(parts), 2 * rank, 2 * part), f32),
    ]
    return call(
        body, (), operands, [KEEP] * 7 + [remain] * count, outs, [KEEP] * 4,
        scratch=far_scratch(len(parts), part, features, tokens), aliases={2: 0, 3: 1},
    )


def shares(array, core):
    half = array.shape[1] // 2
    low, high = array[:, :half], array[:, half:]
    return jnp.where(core == 0, low, high), jnp.where(core == 0, high, low)


def padded(array, count):
    return jnp.concatenate([array, jnp.zeros((array.shape[0], count - array.shape[1]), array.dtype)], axis=1)


def lanes_up(count):
    return (count + 127) // 128 * 128


def feed_close(parts, spot, pick, lengths, hidden, z, gy, branch, second, lows, near_sums, far_sums, contexts, outs_w, far, packs, tables, received, cotangent, cot_side, gain, weights):
    tokens, features = hidden.shape
    rows = tokens // 2
    width = contexts[0].shape[1]
    rank = tables[0].shape[1]
    pack, side, far_side = packs
    base = received.shape[0] - 3 * rank
    part = weights[0].shape[0]
    units = 4 * part
    heads = width // HEAD_DIM
    half = features // 2
    tail = lanes_up(width)
    total_lanes = 3 * half + 2 * (2 * units + tail)

    def body(spot_ref, pick_ref, length_ref, hidden_ref, z_ref, gy_ref, branch_in, second_in, lows_ref, near0, near1, far0, far3, c01, c23, wo0, wo1, far_ref, pack_ref, side_ref, far_side_ref, received_ref, oo, wi, no, ca, cb, gain_ref, *refs):
        hbm, (out_ref, outb_ref, gh_ref, gc_ref, delta_ref, keep_ref, give_ref) = refs[:8], refs[8:15]
        wide, thin, act_ref, grad_ref, sems, last, ga_ref = refs[15:]
        copies = far_copies(len(parts), hbm, wide, thin, sems)
        low_w = lows_ref[rank : 2 * rank]
        low_n = lows_ref[2 * rank : 3 * rank]
        found = far_parts(
            parts, z_ref, gy_ref, copies, wide, thin, received_ref, far_side_ref, rank, base,
            low_w, low_n, act_ref, grad_ref, last,
        )
        branch = branch_in[...] + found[0]
        grad_second = second_in[...] + found[1]
        low_next = lows_ref[3 * rank : 4 * rank] + found[2]
        grad_low = lows_ref[4 * rank :] + found[3]
        mask = live_column(spot_ref, length_ref, rows, (0, 2)).astype(f32)
        branch = branch + tn(halves(low_next), twice(no[0]))
        grad_second = grad_second + tn(halves(grad_low), twice(wi[0]))
        hidden_now = hidden_ref[...]
        output = (hidden_now + mask * branch).astype(bf16)
        out_ref[0] = output[:rows]
        outb_ref[...] = output[rows:]
        _, unit, scaled = normalize(hidden_now, gain_ref[...], gain_ref[...])
        grad_in = jnp.concatenate([ca[0], cb[...]], axis=0).astype(f32)
        grad_hidden = grad_in + normalize_back(grad_second, unit, scaled, gain_ref[...])
        gh_ref[...] = grad_hidden
        ga_ref[...] = (mask * grad_hidden).astype(bf16)
        grad_low_o = nt(oo[0], ga_ref[...])
        low_o2 = halves(grad_low_o)
        inner_o = output_inner_rows(pack_ref, side_ref, received_ref, far_side_ref, rank, base, width)
        contexts_all = [c01[0], c01[1], c23[0], c23[1]]
        weights_all = [wo0, wo1, far_ref.at[0, 0], far_ref.at[1, 0]]
        inner_sums = []
        for i in range(4):
            grad = (nt(weights_all[i][...], ga_ref[...]) + tn(twice(inner_o[i]), low_o2)).astype(bf16)
            gc_ref[i] = grad
            product = grad.astype(f32) * contexts_all[i].astype(f32)
            for h in range(heads):
                delta_ref[heads * i + h] = jnp.sum(
                    product[h * HEAD_DIM : (h + 1) * HEAD_DIM], axis=0, keepdims=True
                )
            inner_sums.append(folded(nt(low_o2, contexts_all[i])))
        core = spot_ref[3] & 1
        quad = spot_ref[2]
        shared = (
            folded(nn(halves(grad_low), z_ref[...])),
            folded(nn(halves(lows_ref[:rank]), ga_ref[...])),
            folded(nn(halves(low_next), gy_ref[...])),
        )
        for n in range(3):
            keep_ref[:, n * half : (n + 1) * half], give_ref[:, n * half : (n + 1) * half] = shares(shared[n], core)
        quarters = []
        for near in (near0, near1):
            quarters.append((near[:rank], near[rank:]))
        for q in range(2):
            lanes = slice(q * part, (q + 1) * part)
            pieces = [far0[0, :, lanes], last[0, :, lanes], last[1, :, lanes], far3[0, :, lanes]]
            joined = shuffled(jnp.concatenate(pieces, axis=1), quad)
            quarters.append((joined[:rank], joined[rank:]))
        for i in range(4):
            ref = (keep_ref, give_ref)[i % 2]
            at = 3 * half + (i // 2) * (2 * units + tail)
            ref[:, at : at + units] = quarters[i][0]
            ref[:, at + units : at + 2 * units] = quarters[i][1]
            ref[:, at + 2 * units : at + 2 * units + tail] = padded(inner_sums[i], tail)

    operands = [hidden, z, gy, branch, second, lows] + near_sums + far_sums + contexts + outs_w
    specs = [whole(hidden.shape), KEEP, KEEP, KEEP, KEEP] + [whole(o.shape) for o in operands[5:]]
    operands += [far, pack, side, far_side, received] + tables
    specs += [placed_block((2, 1, width, features), lambda *_: (0, 3, 0, 0))]
    specs += [whole(p.shape) for p in packs] + [whole(received.shape)]
    specs += [placed_block((1, rank, features), of_mine(n)) for n in (3, 4, 5)]
    operands += [cotangent, cot_side, gain] + weights
    specs += [placed_block((1, rows, features), lambda i, spot, *_: (spot[0], 0, 0))]
    specs += [whole(cot_side.shape), whole(gain.shape)] + [remain] * 8
    outs = [
        shaped((2, rows, features), bf16),
        shaped((rows, features), bf16),
        shaped((tokens, features), f32),
        shaped((4, width, tokens), bf16),
        shaped((4 * heads, 1, tokens), f32),
        shaped((rank, total_lanes), f32),
        shaped((rank, total_lanes), f32),
    ]
    scratch = far_scratch(2, part, features, tokens)
    scratch += [pltpu.VMEM((2, 2 * rank, 2 * part), f32), pltpu.VMEM((tokens, features), bf16)]
    out_specs = [placed_block((1, rows, features), lambda i, spot, *_: (spot[0], 0, 0))] + [KEEP] * 6
    return call(body, (spot, pick, lengths), operands, specs, outs, out_specs, scratch=scratch, limit=24)


def gather_grads(spot, quarters, z, low, packs, received):
    tokens, features = z.shape
    rank = low.shape[0] // 3
    width = quarters[0][0].shape[0]
    pack, side, far_side = packs
    base = received.shape[0] - 3 * rank
    half = features // 2
    tail = lanes_up(3 * width)
    total_lanes = 3 * half + 2 * tail

    def body(spot_ref, *refs):
        groups = [refs[3 * i : 3 * i + 3] for i in range(4)]
        z_ref, low_ref, pack_ref, side_ref, far_side_ref, received_ref, g_ref, gl_ref, keep_ref, give_ref = refs[12:]
        places = ((pack_ref, 0), (side_ref, 0), (received_ref, base), (far_side_ref, 0))
        lows = [halves(low_ref[n * rank : (n + 1) * rank]) for n in range(3)]
        total = [jnp.zeros((rank, tokens), f32) for _ in range(3)]
        core = spot_ref[3] & 1
        for i in range(4):
            q, own, other = groups[i][0], groups[i][1], groups[i ^ 1][2]
            ref, start = places[i]
            outers = []
            for n in range(3):
                if n == 0:
                    g = q[...]
                else:
                    g = (own[n - 1] + other[n - 1].astype(f32)).astype(bf16)
                g_ref[i, n] = g
                lanes = slice(n * width, (n + 1) * width)
                total[n] = total[n] + nn(ref[start : start + rank, lanes], g)
                outers.append(folded(nt(lows[n], g)))
            at = 3 * half + (i // 2) * tail
            (keep_ref, give_ref)[i % 2][:, at : at + tail] = padded(jnp.concatenate(outers, axis=1), tail)
        for n in range(3):
            gl_ref[n * rank : (n + 1) * rank] = total[n]
            inner = folded(nn(halves(total[n]), z_ref[...]))
            keep_ref[:, n * half : (n + 1) * half], give_ref[:, n * half : (n + 1) * half] = shares(inner, core)

    operands = [a for q in quarters for a in q] + [z, low] + list(packs) + [received]
    outs = [
        shaped((4, 3, width, tokens), bf16),
        shaped((3 * rank, tokens), f32),
        shaped((rank, total_lanes), f32),
        shaped((rank, total_lanes), f32),
    ]
    return call(
        body, (spot,), operands, [whole(o.shape) for o in operands], outs, [whole(o.shape) for o in outs], weight=5)


def settle(spot, pick, keep, moved, common, with_picks):
    rank, lanes = keep.shape
    own = (lanes - common) // 2
    extra = 128 if with_picks else 0

    def body(spot_ref, pick_ref, keep_ref, moved_ref, here_ref, there_ref):
        total = (keep_ref[...] + moved_ref[...]).astype(bf16)
        here_ref[:, : common + own] = total[:, : common + own]
        there_ref[:, :common] = total[:, :common]
        there_ref[:, common : common + own] = total[:, common + own :]
        if with_picks:
            iota = lax.broadcasted_iota(jnp.int32, (rank, 128), 1)
            line = jnp.zeros((rank, 128), f32)
            for n in range(6):
                line = jnp.where(iota == n, pick_ref[spot_ref[0], n].astype(f32), line)
            here_ref[:, common + own :] = line.astype(bf16)
            there_ref[:, common + own :] = line.astype(bf16)

    out = shaped((rank, common + own + extra), bf16)
    return call(body, (spot, pick), [keep, moved], [whole(keep.shape)] * 2, [out, out], [whole(out.shape)] * 2, weight=1)


def combine(spot, picks, arrays, groups, rows_of_table):
    per, rank = arrays[0].shape[:2]
    half = groups[0][1]

    def body(spot_ref, pick_ref, *refs):
        ins, outs = refs[: len(arrays)], refs[len(arrays) :]
        places = [outs[0].at[n] for n in range(3)] + list(outs[4:])
        for out in places:
            out[...] = jnp.zeros(out.shape, f32)
        for a, ref in enumerate(ins):
            for c in range(per):
                for (start, count, number), out in zip(groups, places):
                    row = pick_ref[a * per + c, number]
                    out[row] += ref[c, :, start : start + count].astype(f32)
        for n in range(3):
            outs[1 + n][...] = outs[0][n]

    outs = [shaped((3, rows_of_table, rank, half), f32)] + [shaped((rows_of_table, rank, 2 * half), f32)] * 3
    outs += [shaped((rows_of_table, rank, count), f32) for _, count, _ in groups[3:]]
    own = placed_block((rows_of_table, rank, half), lambda i, spot, pick: (0, 0, spot[3] & 1))
    specs = [KEEP] + [own] * 3 + [KEEP] * (len(groups) - 3)
    return call(body, (spot, picks), list(arrays), [KEEP] * len(arrays), outs, specs, weight=100)


def complete(spot, tables, moved):
    _, count, rank, half = moved.shape

    def body(spot_ref, moved_ref, *refs):
        for n in range(3):
            refs[3 + n][...] = moved_ref[n]

    out = shaped((count, rank, 2 * half), f32)
    theirs = placed_block((count, rank, half), lambda i, spot: (0, 0, 1 - (spot[3] & 1)))
    return call(
        body, (spot,), [moved] + list(tables), [KEEP] + [remain] * 3, [out] * 3, [theirs] * 3,
        aliases={2: 0, 3: 1, 4: 2}, weight=2)


def pair_up(spot, array, second):
    rows, features = second.shape

    def body(spot_ref, array_ref, second_ref, out_ref):
        out_ref[0] = second_ref[...].astype(array.dtype)

    out_spec = placed_block((1, rows, features), lambda i, spot: (spot[1], 0, 0))
    return call(
        body, (spot,), [array, second], [remain, KEEP], shaped(array.shape, array.dtype), out_spec, aliases={1: 0}, weight=1)


def join(groups):
    flat = [a for g in groups for a in g]
    outs = [shaped((sum(a.shape[0] for a in g),) + g[0].shape[1:], g[0].dtype) for g in groups]

    def body(*refs):
        at = 0
        for g, out in zip(groups, refs[len(flat) :]):
            start = 0
            for a in g:
                out[start : start + a.shape[0]] = refs[at][...]
                start += a.shape[0]
                at += 1

    return call(body, (), flat, [KEEP] * len(flat), outs, [KEEP] * len(outs), weight=1)


def finish(spot, pick, g, gl, inners, weights, far, inputs, received, grad_hidden, gain):
    rows, features = inputs.shape[1:]
    tokens = 2 * rows
    width = g.shape[2]
    rank = gl.shape[0] // 3

    def body(spot_ref, pick_ref, g_ref, gl_ref, iq, ik, iv, *refs):
        ws, (far_ref, xa, xb, gh_ref, gain_ref, grad_ref, gradb_ref) = refs[:6], refs[6:]
        low = [halves(gl_ref[n * rank : (n + 1) * rank]) for n in range(3)]
        total = tn(
            jnp.concatenate(low, axis=0),
            jnp.concatenate([twice(iq[0]), twice(ik[0]), twice(iv[0])], axis=0),
        )
        for i in range(4):
            if i < 2:
                weight = jnp.concatenate([w[...] for w in ws[3 * i : 3 * i + 3]], axis=0)
            else:
                weight = far_ref[i - 2].reshape(3 * width, features)
            total = total + tn(g_ref[i].reshape(3 * width, tokens), weight)
        states = jnp.concatenate([xa[0], xb[...]], axis=0).astype(f32)
        _, unit, scaled = normalize(states, gain_ref[...], gain_ref[...])
        grad = gh_ref[...] + normalize_back(total, unit, scaled, gain_ref[...])
        grad_ref[0] = grad[:rows]
        gradb_ref[...] = grad[rows:].astype(bf16)

    operands = [g, gl] + inners + weights + [far, inputs, received, grad_hidden, gain]
    specs = [whole(g.shape), whole(gl.shape)]
    specs += [placed_block((1, rank, features), of_mine(n)) for n in range(3)]
    specs += [whole(w.shape) for w in weights]
    specs += [placed_block((2, 3, width, features), lambda *_: (0, 0, 0, 0))]
    specs += [placed_block((1, rows, features), lambda i, spot, *_: (spot[0], 0, 0))]
    specs += [placed_block((rows, features), lambda *_: (0, 0)), whole(grad_hidden.shape), whole(gain.shape)]
    outs = [shaped((2, rows, features), f32), shaped((rows, features), bf16)]
    out_specs = [placed_block((1, rows, features), lambda i, spot, *_: (spot[0], 0, 0)), KEEP]
    return call(body, (spot, pick), operands, specs, outs, out_specs, weight=9)


def make_body(dp_size, tensor_size):
    def across(array):
        return swap(array, "tensor", 2, tensor_size)

    def beside(array):
        return swap(array, "tensor", 1, tensor_size)

    def along(array, bits):
        return swap(array, "dp", bits, dp_size)

    def body(
        inputs,
        cotangent,
        lengths,
        adapter_pick,
        first_gain,
        first_bias,
        query_weight,
        key_weight,
        value_weight,
        output_weight,
        second_gain,
        second_bias,
        widen_weight,
        narrow_weight,
        query_inner,
        query_outer,
        key_inner,
        key_outer,
        value_inner,
        value_outer,
        output_inner,
        output_outer,
        widen_inner,
        widen_outer,
        narrow_inner,
        narrow_outer,
    ):
        rows, features = inputs.shape[1:]
        place = lax.axis_index("tensor")
        quad = lax.axis_index("dp") & 3
        mine = place >> 1
        spot = jnp.stack([mine, 1 - mine, quad, place]).astype(jnp.int32)
        pick = adapter_pick

        def flip(array):
            return jnp.swapaxes(array, 1, 2)

        small = [query_outer, key_outer, value_outer, flip(output_inner), widen_outer, flip(narrow_inner)]
        inners = [flip(query_inner), flip(key_inner), flip(value_inner)]
        tables = [output_outer, flip(widen_inner), narrow_outer]
        gains = [v.reshape(1, -1) for v in (first_gain, first_bias, second_gain, second_bias)]
        heads = [query_weight.T, key_weight.T, value_weight.T, output_weight]
        dense = [widen_weight, narrow_weight]
        width = query_outer.shape[2]
        half = features // 2

        part_heads = stage_heads(spot, heads)
        far0 = across(part_heads)
        send, pack = stage(after(spot, part_heads), pick, inputs, small)
        received = across(send)
        near_heads = [beside(w) for w in after(heads, part_heads)]
        side = beside(pack)
        near_dense = [beside(w) for w in after(dense, near_heads)]
        part_wide, part_thin, part_last, cot_send = stage_dense(
            after(spot, pack), widen_weight, narrow_weight, cotangent
        )
        far1, far2 = along(after(far0, near_dense), 1), along(after(far0, near_dense), 2)
        side0 = beside(after(far0, side, near_dense, part_wide))
        wide0 = across(after(part_wide, far0))
        z, low, kv01 = project_near(
            spot, pick, inputs, after(received, side0), gains[0], gains[1], inners, pack, side,
            [heads[1], heads[2], near_heads[1], near_heads[2]],
        )
        kv01_side = beside(kv01)
        far3, far4 = along(after(far2[:2], kv01), 1), along(after(far1[2:], kv01), 2)
        side1 = beside(after(far1, kv01))
        q01 = queries_near(after(z, kv01), low, pack, side, [heads[0], near_heads[0]])
        side2 = beside(after(far2, q01, side1))
        c01, total01 = attend(spot, lengths, q01, kv01, after(kv01_side, side1))
        far_side = beside(after(received[rows:], c01))
        side3, side4 = beside(after(far3, c01, side2)), beside(after(far4, c01, side2))
        wide1, wide2 = along(after(wide0, c01), 1), along(after(wide0, c01), 2)
        cot_side = across(after(cot_send, c01))
        far, kv23 = project_far(
            spot, after(z, c01), low, received, far_side,
            [[far0, far1, far2, far3, far4], [side0, side1, side2, side3, side4]],
        )
        kv23_side = beside(kv23)
        thin0 = across(after(part_thin, kv23))
        q23 = queries_far(after(z, kv23), low, received, far_side, far)
        c23, total23 = attend(spot, lengths, q23, kv23, kv23_side)
        packs = [pack, side, far_side]
        outs_w = [heads[3], near_heads[3]]
        hidden, z2, lows = feed_open(
            spot, pick, lengths, [c01, c23], outs_w, far, packs, tables, inputs, received, gains[2], gains[3]
        )
        wide3 = along(after(wide2, lows), 1)
        thin3 = across(after(part_last, lows))
        wide_sides = [beside(after(w, lows)) for w in (wide0, wide1, wide2)]
        gy, branch, second, lows, sums0 = feed_first(
            spot, pick, lengths, z2, lows, tables[2], cotangent, cot_side, pack, dense
        )
        thin1, thin2 = along(after(thin0, lows), 1), along(after(thin0, lows), 2)
        thin_sides = [beside(after(thin0, lows))]
        branch, second, lows, sums1 = feed_near(
            z2, gy, branch, second, after(lows, wide_sides), side, near_dense
        )
        wide_sides.append(beside(after(wide3, sums1)))
        branch, second, lows, sums2 = feed_far(
            (0,), z2, gy, branch, second, lows, received, far_side, [wide0, wide_sides[0], thin0, thin_sides[0]]
        )
        thin_sides += [beside(after(t, sums2)) for t in (thin1, thin2, thin3)]
        branch, second, lows, sums3 = feed_far(
            (3,), z2, gy, branch, second, lows, received, far_side, [wide3, wide_sides[3], thin3, thin_sides[3]]
        )
        output, outb, grad_hidden, grad_context, deltas, keep, give = feed_close(
            (1, 2), spot, pick, lengths, hidden, z2, gy, branch, second, lows, [sums0, sums1], [sums2, sums3],
            [c01, c23], outs_w, far, packs, tables, received, cotangent, cot_side, gains[2],
            [wide1, wide_sides[1], thin1, thin_sides[1], wide2, wide_sides[2], thin2, thin_sides[2]],
        )

        def first_turn(here, other, crossed):
            one, two = join([[here[None], crossed[0][None]], [other[None], crossed[1][None]]])
            return [(one, along(one, 1)), (two, along(two, 2))]

        def second_turn(turns):
            one, two = join(turns)
            return [one, along(one, 2), two, along(two, 1)]

        def whole_sum(table):
            bits = 8
            while bits < dp_size:
                table = table + along(table, bits)
                bits *= 2
            return table

        def back(number, q, kv, kv_side, totals):
            gq, own, other = attend_back(spot, lengths, q, kv, kv_side, grad_context, totals, deltas, number)
            return gq, own, other

        moved = beside(give)
        here, there = settle(spot, pick, keep, moved, 3 * half, True)
        other = across(there)
        crossed = [along(here, 4)]
        quarters = [back(0, after(q01, here), kv01, kv01_side, total01)]
        quarters.append(back(1, after(q01, quarters[0][0]), kv01, kv01_side, total01))
        sides = [beside(after(quarters[0][2], quarters[1][0]))]
        crossed.append(along(after(other, quarters[0][0]), 4))
        out_side = across(after(outb, quarters[1][0]))
        quarters.append(back(2, after(q23, quarters[1][0]), kv23, kv23_side, total23))
        sides.append(beside(after(quarters[1][2], quarters[2][0], sides[0])))
        turns = first_turn(here, other, after(crossed, quarters[2][0]))
        quarters.append(back(3, after(q23, quarters[2][0], turns[0][0]), kv23, kv23_side, total23))
        sides += [beside(after(quarters[2][2], quarters[3][0], sides[1])), beside(quarters[3][2])]
        quarters = [(gq, own, sided) for (gq, own, _), sided in zip(quarters, sides)]
        early = second_turn(after(turns, quarters[3][0]))
        g, gl, keep, give = gather_grads(spot, quarters, after(z, early[0], early[2]), low, packs, received)
        moved = beside(give)
        here, there = settle(spot, pick, keep, moved, 3 * half, False)
        other = across(there)
        crossed = [along(here, 4)]
        crossed.append(along(other, 4))
        grad, gradb = finish(
            spot, pick, after(g, other), gl, inners, heads[:3] + near_heads[:3], far, inputs, received, grad_hidden,
            gains[0],
        )
        grad_side = across(after(gradb, crossed))
        turns = first_turn(here, other, after(crossed, gradb))
        output = pair_up(spot, output, after(out_side, gradb))
        picks = jnp.concatenate([a[:, 0, -128:-122] for a in early]).astype(jnp.int32)
        adapters = query_inner.shape[0]
        units = widen_weight.shape[1]
        base = 3 * half
        early = combine(
            spot,
            after(picks, gradb),
            early,
            [
                (0, half, 4),
                (half, half, 3),
                (2 * half, half, 5),
                (base, units, 4),
                (base + units, units, 5),
                (base + 2 * units, width, 3),
            ],
            adapters,
        )
        early = [whole_sum(t) for t in early]
        early_shared = complete(spot, early[1:4], beside(early[0]))
        late = second_turn(turns)
        input_grad = pair_up(spot, grad, grad_side)
        late = combine(
            spot,
            after(picks, grad_side),
            late,
            [(n * half, half, n) for n in range(3)] + [(base + n * width, width, n) for n in range(3)],
            adapters,
        )
        late = [whole_sum(t) for t in late]
        late_shared = complete(spot, late[1:4], beside(late[0]))
        return (
            output,
            input_grad,
            flip(late_shared[0]),
            late[4],
            flip(late_shared[1]),
            late[5],
            flip(late_shared[2]),
            late[6],
            flip(early[6]),
            early_shared[1],
            flip(early_shared[0]),
            early[4],
            flip(early[5]),
            early_shared[2],
        )

    return body


def solution(mesh):
    placed = (
        P("dp", "tensor", None),
        P("dp", "tensor", None),
        P("dp"),
        P("dp", None),
        P(),
        P(),
        P(None, "tensor"),
        P(None, "tensor"),
        P(None, "tensor"),
        P("tensor", None),
        P(),
        P(),
        P(None, "tensor"),
        P("tensor", None),
        P(),
        P(None, None, "tensor"),
        P(),
        P(None, None, "tensor"),
        P(),
        P(None, None, "tensor"),
        P(None, "tensor", None),
        P(),
        P(),
        P(None, None, "tensor"),
        P(None, "tensor", None),
        P(),
    )
    return jax.shard_map(
        make_body(mesh.shape["dp"], mesh.shape["tensor"]),
        mesh=mesh,
        in_specs=placed,
        out_specs=(
            P("dp", "tensor", None),
            P("dp", "tensor", None),
            P(),
            P(None, None, "tensor"),
            P(),
            P(None, None, "tensor"),
            P(),
            P(None, None, "tensor"),
            P(None, "tensor", None),
            P(),
            P(),
            P(None, None, "tensor"),
            P(None, "tensor", None),
            P(),
        ),
        check_vma=False,
    )
```

```python
import functools
import math

import jax
import jax.numpy as jnp
from jax import lax
from jax.experimental import pallas as pl
from jax.experimental.pallas import tpu as pltpu
from jax.sharding import PartitionSpec as P

HEAD_DIM = 80
f32 = jnp.float32
bf16 = jnp.bfloat16
neg_fill = -1000000000.0
score_scale = 1.0 / math.sqrt(HEAD_DIM)
log2_e = math.log2(math.e)
LIMIT = 16
KEEP = pl.BlockSpec(memory_space=pltpu.VMEM)
remain = pl.BlockSpec(memory_space=pl.ANY)
in_hbm = pl.BlockSpec(memory_space=pltpu.HBM)


def swap(array, axis, bits, size):
    return lax.ppermute(array, axis, [(i, i ^ bits) for i in range(size)])


def nn(a, b):
    return jnp.dot(a, b, preferred_element_type=f32)


def nt(a, b):
    return lax.dot_general(a, b, (((1,), (1,)), ((), ())), preferred_element_type=f32)


def tn(a, b):
    return lax.dot_general(a, b, (((0,), (0,)), ((), ())), preferred_element_type=f32)


def halves(low):
    top = low.astype(bf16)
    return jnp.concatenate([top, (low - top.astype(f32)).astype(bf16)], axis=0)


def twice(factor):
    return jnp.concatenate([factor, factor], axis=0)


def folded(pair):
    count = pair.shape[0] // 2
    return pair[:count] + pair[count:]


def normalize(states, gain, shift):
    centre = states - jnp.mean(states, axis=-1, keepdims=True)
    scaled = lax.rsqrt(jnp.mean(centre * centre, axis=-1, keepdims=True) + 1e-05)
    unit = centre * scaled
    return unit * gain + shift, unit, scaled


def normalize_back(grad_rows, unit, scaled, gain):
    grad_unit = grad_rows * gain
    return scaled * (
        grad_unit
        - jnp.mean(grad_unit, axis=-1, keepdims=True)
        - unit * jnp.mean(grad_unit * unit, axis=-1, keepdims=True)
    )


def live_column(spot_ref, length_ref, rows, bits):
    iota = lax.broadcasted_iota(jnp.int32, (2 * rows, 1), 0)
    place = spot_ref[3]
    first, second = place ^ bits[0], place ^ bits[1]
    position = jnp.where(iota < rows, first * rows + iota, second * rows + iota - rows)
    return position < length_ref[spot_ref[0]]


def whole(shape):
    return KEEP


def placed_block(shape, index):
    return pl.BlockSpec(shape, index, pipeline_mode=pl.Buffered(1))


def call(body, scalars, operands, specs, outs, out_specs, grid=(1,), scratch=(), limit=LIMIT, aliases=None, weight=100):
    return pl.pallas_call(
        body,
        grid_spec=pltpu.PrefetchScalarGridSpec(
            num_scalar_prefetch=len(scalars),
            grid=grid,
            in_specs=specs,
            out_specs=out_specs,
            scratch_shapes=list(scratch),
        ),
        out_shape=outs,
        cost_estimate=pl.CostEstimate(flops=weight * 10**9, bytes_accessed=100000, transcendentals=0),
        input_output_aliases=aliases or {},
        compiler_params=pltpu.CompilerParams(vmem_limit_bytes=limit * 2**20),
    )(*scalars, *operands)


def shaped(shape, dtype):
    return jax.ShapeDtypeStruct(shape, dtype)


def of_mine(number):
    return lambda i, spot, pick, *_: (pick[spot[0], number], 0, 0)


def of_other(number):
    return lambda i, spot, pick, *_: (pick[spot[1], number], 0, 0)


def after(values, *others):
    return lax.optimization_barrier((values, others))[0]


def shuffled(array, quad):
    count = array.shape[1] // 4
    blocks = [array[:, n * count : (n + 1) * count] for n in range(4)]
    for bits in (1, 2):
        on = ((quad >> (bits - 1)) & 1) == 1
        blocks = [jnp.where(on, blocks[n ^ bits], blocks[n]) for n in range(4)]
    return jnp.concatenate(blocks, axis=1)


def stage(spot, pick, inputs, factors):
    rows, features = inputs.shape[1:]
    rank = factors[0].shape[1]

    def body(spot_ref, pick_ref, inputs_ref, *refs):
        send_ref, pack_ref = refs[12:]
        send_ref[:rows] = inputs_ref[0]
        quad = spot_ref[2]
        for group, ref, base in ((refs[:6], pack_ref, 0), (refs[6:12], send_ref, rows)):
            ref[base : base + rank] = jnp.concatenate([r[0] for r in group[:4]], axis=1)
            wide, thin = group[4][0], group[5][0]
            if base:
                wide, thin = shuffled(wide, quad), shuffled(thin, quad)
            ref[base + rank : base + 2 * rank] = wide
            ref[base + 2 * rank : base + 3 * rank] = thin

    specs = [placed_block((1, rows, features), lambda i, spot, *_: (spot[1], 0, 0))]
    for of in (of_mine, of_other):
        specs += [placed_block((1,) + f.shape[1:], of(n)) for n, f in enumerate(factors)]
    outs = [shaped((rows + 3 * rank, features), bf16), shaped((3 * rank, features), bf16)]
    return call(body, (spot, pick), [inputs] + factors * 2, specs, outs, [whole(o.shape) for o in outs])


def stage_dense(spot, wide, thin, cotangent):
    features, units = wide.shape
    part = units // 4
    rows = cotangent.shape[1]

    def body(spot_ref, wide_ref, thin_ref, last_ref, cot_ref, wide_out, thin_out, last_out, cot_out):
        for r in range(4):

            @pl.when(spot_ref[2] == r)
            def _():
                wide_out[...] = wide_ref[:, r * part : (r + 1) * part].T

        thin_out[...] = thin_ref[...]
        last_out[...] = last_ref[...]
        cot_out[...] = cot_ref[0]

    specs = [
        whole(wide.shape),
        placed_block((part, features), lambda i, spot: (spot[2], 0)),
        placed_block((part, features), lambda i, spot: (spot[2] ^ 3, 0)),
        placed_block((1, rows, features), lambda i, spot: (spot[1], 0, 0)),
    ]
    outs = [shaped((part, features), bf16)] * 3 + [shaped((rows, features), bf16)]
    return call(body, (spot,), [wide, thin, thin, cotangent], specs, outs, [whole(o.shape) for o in outs])


def project_rows(weight, rows_in, outer, low):
    return (nt(weight, rows_in) + tn(twice(outer), halves(low))).astype(bf16)


def project_near(spot, pick, inputs, received, gain, shift, inners, pack, side, weights):
    rows, features = inputs.shape[1:]
    tokens = 2 * rows
    width = weights[0].shape[0]
    rank = inners[0].shape[1]

    def body(spot_ref, pick_ref, xa, xb, gain_ref, shift_ref, iq, ik, iv, pack_ref, side_ref, *refs):
        hbm, (z_ref, low_ref, kv_ref, ws, sems) = refs[:4], refs[4:]
        copies = [pltpu.make_async_copy(hbm[n], ws.at[n], sems.at[n]) for n in range(4)]
        for c in copies:
            c.start()
        states = jnp.concatenate([xa[0], xb[...]], axis=0).astype(f32)
        z_ref[...] = normalize(states, gain_ref[...], shift_ref[...])[0].astype(bf16)
        low = nt(jnp.concatenate([iq[0], ik[0], iv[0]], axis=0), z_ref[...])
        low_ref[...] = low
        for i, packs in enumerate((pack_ref, side_ref)):
            for n in (1, 2):
                outer = packs[:rank, n * width : (n + 1) * width]
                copies[2 * i + n - 1].wait()
                kv_ref[i, n - 1] = project_rows(
                    ws[2 * i + n - 1], z_ref[...], outer, low[n * rank : (n + 1) * rank]
                )

    specs = [
        placed_block((1, rows, features), lambda i, spot, *_: (spot[0], 0, 0)),
        placed_block((rows, features), lambda *_: (0, 0)),
        whole((1, features)),
        whole((1, features)),
    ]
    specs += [placed_block((1, rank, features), of_mine(n)) for n in range(3)]
    specs += [whole(pack.shape), whole(side.shape)] + [in_hbm] * 4
    outs = [
        shaped((tokens, features), bf16),
        shaped((3 * rank, tokens), f32),
        shaped((2, 2, width, tokens), bf16),
    ]
    return call(
        body,
        (spot, pick),
        [inputs, received, gain, shift] + inners + [pack, side] + weights,
        specs,
        outs,
        [whole(o.shape) for o in outs],
        scratch=[pltpu.VMEM((4, width, features), bf16), pltpu.SemaphoreType.DMA((4,))],
    )


def queries_near(z, low, pack, side, weights):
    tokens, features = z.shape
    width = weights[0].shape[0]
    rank = low.shape[0] // 3

    def body(z_ref, low_ref, pack_ref, side_ref, w0, w1, q_ref):
        for i, (packs, w) in enumerate(((pack_ref, w0), (side_ref, w1))):
            q_ref[i] = project_rows(w[...], z_ref[...], packs[:rank, :width], low_ref[:rank])

    operands = [z, low, pack, side] + weights
    out = shaped((2, width, tokens), bf16)
    return call(body, (), operands, [whole(o.shape) for o in operands], out, whole(out.shape))


def project_far(spot, z, low, received, side, parts):
    tokens, features = z.shape
    head_rows = parts[0][0].shape[1]
    width = 4 * head_rows
    rank = low.shape[0] // 3
    base = received.shape[0] - 3 * rank
    flat = [p for group in parts for p in group]

    def body(spot_ref, z_ref, low_ref, received_ref, side_ref, *refs):
        ins, (out_ref, kv_ref, q_ref, weight_ref, sems) = refs[:10], refs[10:]
        for i in range(2):
            group = ins[5 * i : 5 * i + 5]
            for n in range(4):
                for r in range(4):
                    at = pl.ds(pl.multiple_of((spot_ref[0] ^ r) * head_rows, 16), head_rows)
                    if r < 3:
                        weight_ref[i, n, at] = group[r][n]
                    else:
                        weight_ref[i, n, at] = group[3 + n // 2][n % 2]
        copies = [pltpu.make_async_copy(weight_ref.at[i], out_ref.at[i], sems.at[i]) for i in range(2)]
        for c in copies:
            c.start()
        for i, (ref, start) in enumerate(((received_ref, base), (side_ref, 0))):
            for n in range(3):
                outer = ref[start : start + rank, n * width : (n + 1) * width]
                y = project_rows(weight_ref[i, n], z_ref[...], outer, low_ref[n * rank : (n + 1) * rank])
                if n == 0:
                    q_ref[i] = y
                else:
                    kv_ref[i, n - 1] = y
        for c in copies:
            c.wait()

    operands = [z, low, received, side] + flat
    outs = [
        shaped((2, 4, width, features), bf16),
        shaped((2, 2, width, tokens), bf16),
        shaped((2, width, tokens), bf16),
    ]
    return call(
        body, (spot[2:3],), operands, [KEEP] * len(operands), outs, [remain, KEEP, KEEP],
        scratch=[pltpu.VMEM((2, 4, width, features), bf16), pltpu.SemaphoreType.DMA((2,))],
    )


def attend(spot, lengths, q, kv, kv_side):
    _, width, tokens = q.shape
    rows = tokens // 2
    pair = 2 * HEAD_DIM
    steps = width // pair

    def body(spot_ref, length_ref, q_ref, k1, k2, v1, v2, ctx_ref, total_ref):
        bias1 = jnp.where(live_column(spot_ref, length_ref, rows, (0, 2)), 0.0, neg_fill * log2_e)
        bias2 = jnp.where(live_column(spot_ref, length_ref, rows, (1, 3)), 0.0, neg_fill * log2_e)
        for h in range(2):
            at = slice(h * HEAD_DIM, (h + 1) * HEAD_DIM)
            query = q_ref[0, at]
            s1 = tn(k1[0, 0, at], query) * (score_scale * log2_e) + bias1
            s2 = tn(k2[0, 0, at], query) * (score_scale * log2_e) + bias2
            top = jnp.maximum(jnp.max(s1, axis=0, keepdims=True), jnp.max(s2, axis=0, keepdims=True))
            p1 = jnp.exp2(s1 - top)
            p2 = jnp.exp2(s2 - top)
            total = jnp.sum(p1, axis=0, keepdims=True) + jnp.sum(p2, axis=0, keepdims=True)
            context = nn(v1[0, 0, at], p1.astype(bf16)) + nn(v2[0, 0, at], p2.astype(bf16))
            ctx_ref[0, at] = (context * (1.0 / total)).astype(bf16)
            total_ref[h] = top + jnp.log2(total)

    def own(n):
        return pl.BlockSpec((1, 1, pair, tokens), lambda h, *_: (h // steps, n, h % steps, 0))

    def beside(n):
        return pl.BlockSpec((1, 1, pair, tokens), lambda h, *_: (1 - h // steps, n, h % steps, 0))

    rows_spec = pl.BlockSpec((1, pair, tokens), lambda h, *_: (h // steps, h % steps, 0))
    return call(
        body,
        (spot, lengths),
        [q, kv, kv_side, kv, kv_side],
        [rows_spec, own(0), beside(0), own(1), beside(1)],
        [shaped(q.shape, bf16), shaped((4 * steps, 1, tokens), f32)],
        [rows_spec, pl.BlockSpec((2, 1, tokens), lambda h, *_: (h, 0, 0))],
        grid=(2 * steps,),
    )


def attend_back(spot, lengths, q, kv, kv_side, grad_context, totals, deltas, number):
    _, width, tokens = q.shape
    rows = tokens // 2
    pair = 2 * HEAD_DIM
    steps = width // pair
    at_hand = number % 2

    def body(spot_ref, length_ref, q_ref, k1, k2, v1, v2, g_ref, total_ref, delta_ref, gq, own_ref, other_ref):
        bias1 = jnp.where(live_column(spot_ref, length_ref, rows, (0, 2)), 0.0, neg_fill * log2_e)
        bias2 = jnp.where(live_column(spot_ref, length_ref, rows, (1, 3)), 0.0, neg_fill * log2_e)
        for h in range(2):
            at = slice(h * HEAD_DIM, (h + 1) * HEAD_DIM)
            query = q_ref[0, at]
            grad = g_ref[0, at]
            grad_query = None
            for k, v, bias, out in ((k1, v1, bias1, own_ref), (k2, v2, bias2, other_ref)):
                s = tn(k[0, 0, at], query) * (score_scale * log2_e) + bias
                soft = jnp.exp2(s - total_ref[h])
                grad_soft = tn(v[0, 0, at], grad)
                grad_scores = (soft * (grad_soft - delta_ref[h])).astype(bf16)
                part = nn(k[0, 0, at], grad_scores)
                grad_query = part if grad_query is None else grad_query + part
                out[0, at] = (nt(query, grad_scores) * score_scale).astype(out.dtype)
                out[1, at] = nt(grad, soft.astype(bf16)).astype(out.dtype)
            gq[at] = (grad_query * score_scale).astype(bf16)

    def own(n):
        return pl.BlockSpec((1, 1, pair, tokens), lambda h, *_: (at_hand, n, h, 0))

    def beside(n):
        return pl.BlockSpec((1, 1, pair, tokens), lambda h, *_: (1 - at_hand, n, h, 0))

    rows_spec = pl.BlockSpec((1, pair, tokens), lambda h, *_: (at_hand, h, 0))
    grads_spec = pl.BlockSpec((1, pair, tokens), lambda h, *_: (number, h, 0))
    line = pl.BlockSpec((2, 1, tokens), lambda h, *_: (steps * at_hand + h, 0, 0))
    line_at = pl.BlockSpec((2, 1, tokens), lambda h, *_: (steps * number + h, 0, 0))
    both = pl.BlockSpec((2, pair, tokens), lambda h, *_: (0, h, 0))
    return call(
        body,
        (spot, lengths),
        [q, kv, kv_side, kv, kv_side, grad_context, totals, deltas],
        [rows_spec, own(0), beside(0), own(1), beside(1), grads_spec, line, line_at],
        [shaped(q.shape[1:], bf16), shaped(kv.shape[1:], f32), shaped(kv.shape[1:], bf16)],
        [pl.BlockSpec((pair, tokens), lambda h, *_: (h, 0)), both, both],
        grid=(steps,), weight=8)


cubic = 0.044715
BLOCK = 512
BIG = 20
root = math.sqrt(2.0 / math.pi)


def bend_of(widened, grad):
    square = widened * widened
    bend = jnp.tanh(root * widened * (1.0 + cubic * square))
    up = 0.5 * (1.0 + bend)
    slope = up + widened * (0.5 * root) * (1.0 - bend * bend) * (1.0 + 3.0 * cubic * square)
    return (widened * up).astype(bf16), (grad * slope).astype(bf16)


def feed_quarter(z_ref, gy_ref, wide_ref, thin_ref, pack_ref, rank, low_w, low_n, act_ref, grad_ref, sums_ref, ready=None):
    units = wide_ref.shape[1]
    low_w2, low_n2 = halves(low_w), halves(low_n)
    for start in range(0, units, BLOCK):
        at = slice(start, min(start + BLOCK, units))
        if ready is not None:
            ready(at)
        widened = nn(z_ref[...], wide_ref[:, at]) + tn(low_w2, twice(pack_ref[rank : 2 * rank, at]))
        grad = nt(gy_ref[...], thin_ref[at, :]) + tn(low_n2, twice(pack_ref[2 * rank : 3 * rank, at]))
        act_ref[:, at], grad_ref[:, at] = bend_of(widened, grad)
    sums_ref[:rank] = folded(nn(low_w2, grad_ref[...]))
    sums_ref[rank:] = folded(nn(low_n2, act_ref[...]))
    return (
        nn(act_ref[...], thin_ref[...]),
        nt(grad_ref[...], wide_ref[...]),
        nt(pack_ref[2 * rank : 3 * rank], act_ref[...]),
        nt(pack_ref[rank : 2 * rank], grad_ref[...]),
    )


def feed_units(z_ref, gy_ref, wide_ref, thin_ref, outer, inner, low_w, low_n, act_ref, grad_ref, ready):
    units = wide_ref.shape[0]
    low_w2, low_n2 = halves(low_w), halves(low_n)
    for start in range(0, units, BLOCK):
        at = slice(start, min(start + BLOCK, units))
        ready(at.stop)
        widened = nt(z_ref[...], wide_ref[at]) + tn(low_w2, twice(outer[:, at]))
        grad = nt(gy_ref[...], thin_ref[at]) + tn(low_n2, twice(inner[:, at]))
        act_ref[:, at], grad_ref[:, at] = bend_of(widened, grad)
    sums = jnp.concatenate(
        [folded(nn(low_w2, grad_ref[...])), folded(nn(low_n2, act_ref[...]))], axis=0
    )
    return (
        nn(act_ref[...], thin_ref[...]),
        nn(grad_ref[...], wide_ref[...]),
        nt(inner, act_ref[...]),
        nt(outer, grad_ref[...]),
        sums,
    )


def output_inner_rows(pack_ref, side_ref, received_ref, far_side_ref, rank, base, width):
    lanes = slice(3 * width, 4 * width)
    return [
        pack_ref[:rank, lanes],
        side_ref[:rank, lanes],
        received_ref[base : base + rank, lanes],
        far_side_ref[:rank, lanes],
    ]


def feed_open(spot, pick, lengths, contexts, outs_w, far, packs, tables, inputs, received, gain, shift):
    rows, features = inputs.shape[1:]
    tokens = 2 * rows
    width = contexts[0].shape[1]
    rank = tables[0].shape[1]
    pack, side, far_side = packs
    base = received.shape[0] - 3 * rank

    def body(spot_ref, pick_ref, length_ref, c01, c23, wo0, wo1, far_ref, pack_ref, side_ref, far_side_ref, received_ref, oo, wi, xa, gain_ref, shift_ref, hidden_ref, z_ref, lows_ref):
        states = jnp.concatenate([xa[0], received_ref[:rows]], axis=0).astype(f32)
        mask = live_column(spot_ref, length_ref, rows, (0, 2)).astype(f32)
        inner_o = output_inner_rows(pack_ref, side_ref, received_ref, far_side_ref, rank, base, width)
        contexts_all = [c01[0], c01[1], c23[0], c23[1]]
        weights_all = [wo0[...], wo1[...], far_ref[0, 0], far_ref[1, 0]]
        joined = jnp.concatenate(contexts_all, axis=0)
        attended = tn(joined, jnp.concatenate(weights_all, axis=0))
        low_o = nn(jnp.concatenate(inner_o, axis=1), joined)
        attended = attended + tn(halves(low_o), twice(oo[0]))
        hidden = states + mask * attended
        hidden_ref[...] = hidden
        z_ref[...] = normalize(hidden, gain_ref[...], shift_ref[...])[0].astype(bf16)
        lows_ref[:rank] = low_o
        lows_ref[rank:] = nt(wi[0], z_ref[...])

    operands = contexts + outs_w + [far, pack, side, far_side, received] + tables[:2]
    specs = [whole(c.shape) for c in contexts] + [whole(w.shape) for w in outs_w]
    specs += [placed_block((2, 1, width, features), lambda *_: (0, 3, 0, 0))]
    specs += [whole(p.shape) for p in packs] + [whole(received.shape)]
    specs += [placed_block((1, rank, features), of_mine(n)) for n in (3, 4)]
    operands += [inputs, gain, shift]
    specs += [placed_block((1, rows, features), lambda i, spot, *_: (spot[0], 0, 0))]
    specs += [whole(gain.shape), whole(shift.shape)]
    outs = [shaped((tokens, features), f32), shaped((tokens, features), bf16), shaped((2 * rank, tokens), f32)]
    return call(body, (spot, pick, lengths), operands, specs, outs, [KEEP] * 3)


def feed_first(spot, pick, lengths, z, lows, table, cotangent, cot_side, pack, dense):
    tokens, features = z.shape
    rows = tokens // 2
    rank = table.shape[1]
    units = dense[0].shape[1]

    def body(spot_ref, pick_ref, length_ref, z_ref, lows_in, no, ca, cb, pack_ref, wide, thin, gy_ref, branch_ref, second_ref, lows_ref, sums_ref, act_ref, grad_ref):
        mask = live_column(spot_ref, length_ref, rows, (0, 2)).astype(f32)
        grad_in = jnp.concatenate([ca[0], cb[...]], axis=0).astype(f32)
        gy_ref[...] = (mask * grad_in).astype(bf16)
        low_n = nt(no[0], gy_ref[...])
        lows_ref[: 2 * rank] = lows_in[...]
        lows_ref[2 * rank : 3 * rank] = low_n
        branch_ref[...], second_ref[...], lows_ref[3 * rank : 4 * rank], lows_ref[4 * rank :] = feed_quarter(
            z_ref, gy_ref, wide, thin, pack_ref, rank, lows_in[rank:], low_n, act_ref, grad_ref, sums_ref
        )

    operands = [z, lows, table, cotangent, cot_side, pack] + dense
    specs = [KEEP, KEEP, placed_block((1, rank, features), of_mine(5))]
    specs += [placed_block((1, rows, features), lambda i, spot, *_: (spot[0], 0, 0))] + [KEEP] * 4
    outs = [
        shaped((tokens, features), bf16),
        shaped((tokens, features), f32),
        shaped((tokens, features), f32),
        shaped((5 * rank, tokens), f32),
        shaped((2 * rank, units), f32),
    ]
    scratch = [pltpu.VMEM((tokens, units), bf16)] * 2
    return call(body, (spot, pick, lengths), operands, specs, outs, [KEEP] * 5, scratch=scratch, limit=BIG)


def feed_near(z, gy, branch, second, lows, pack, dense):
    tokens, features = z.shape
    units = dense[0].shape[1]
    rank = lows.shape[0] // 5
    blocks = [slice(n, min(n + BLOCK, units)) for n in range(0, units, BLOCK)]

    def body(z_ref, gy_ref, branch_in, second_in, lows_in, pack_ref, wide_hbm, thin_hbm, branch_ref, second_ref, lows_ref, sums_ref, wide, thin, act_ref, grad_ref, sems):
        copies = {}
        for n, at in enumerate(blocks):
            copies[at.start] = (
                pltpu.make_async_copy(wide_hbm.at[:, at], wide.at[:, at], sems.at[0, n]),
                pltpu.make_async_copy(thin_hbm.at[at], thin.at[at], sems.at[1, n]),
            )
            for c in copies[at.start]:
                c.start()

        def ready(at):
            for c in copies[at.start]:
                c.wait()

        sums = feed_quarter(
            z_ref, gy_ref, wide, thin, pack_ref, rank, lows_in[rank : 2 * rank], lows_in[2 * rank : 3 * rank],
            act_ref, grad_ref, sums_ref, ready,
        )
        branch_ref[...] = branch_in[...] + sums[0]
        second_ref[...] = second_in[...] + sums[1]
        lows_ref[: 3 * rank] = lows_in[: 3 * rank]
        lows_ref[3 * rank : 4 * rank] = lows_in[3 * rank : 4 * rank] + sums[2]
        lows_ref[4 * rank :] = lows_in[4 * rank :] + sums[3]

    operands = [z, gy, branch, second, lows, pack] + dense
    outs = [shaped(branch.shape, f32), shaped(second.shape, f32), shaped(lows.shape, f32), shaped((2 * rank, units), f32)]
    scratch = [pltpu.VMEM(d.shape, bf16) for d in dense] + [pltpu.VMEM((tokens, units), bf16)] * 2
    scratch += [pltpu.SemaphoreType.DMA((2, len(blocks)))]
    return call(
        body, (), operands, [KEEP] * 6 + [in_hbm] * 2, outs, [KEEP] * 4, scratch=scratch, aliases={2: 0, 3: 1}, limit=BIG
    )


def far_copies(ins, wide, thin, sems):
    part = ins[0].shape[0]
    copies = []
    for n in range(len(ins) // 4):
        for q in range(2):
            k = 2 * n + q
            at = slice(k * part, (k + 1) * part)
            copies.append(pltpu.make_async_copy(ins[4 * n + q], wide.at[at], sems.at[2 * k]))
            copies.append(pltpu.make_async_copy(ins[4 * n + 2 + q], thin.at[at], sems.at[2 * k + 1]))
    for c in copies:
        c.start()
    return copies


def far_parts(parts, z_ref, gy_ref, copies, wide, thin, received_ref, far_side_ref, rank, base, low_w, low_n, act_ref, grad_ref, sums_ref):
    count = wide.shape[0] // (2 * len(parts))
    outer, inner = [], []
    for r in parts:
        lanes = slice(r * count, (r + 1) * count)
        outer += [received_ref[base + rank : base + 2 * rank, lanes], far_side_ref[rank : 2 * rank, lanes]]
        inner += [received_ref[base + 2 * rank : base + 3 * rank, lanes], far_side_ref[2 * rank : 3 * rank, lanes]]
    arrived = []

    def ready(end):
        while len(arrived) * count < min(end, wide.shape[0]):
            n = len(arrived)
            copies[2 * n].wait()
            copies[2 * n + 1].wait()
            arrived.append(n)

    *total, sums = feed_units(
        z_ref, gy_ref, wide, thin, jnp.concatenate(outer, axis=1), jnp.concatenate(inner, axis=1), low_w, low_n,
        act_ref, grad_ref, ready,
    )
    sums_ref[...] = sums
    return total


def far_scratch(parts, part, features, tokens):
    units = 2 * len(parts) * part
    return [pltpu.VMEM((units, features), bf16)] * 2 + [pltpu.VMEM((tokens, units), bf16)] * 2 + [
        pltpu.SemaphoreType.DMA((4 * len(parts),))
    ]


def feed_far(parts, z, gy, branch, second, lows, received, far_side, weights):
    tokens, features = z.shape
    part = weights[0].shape[0]
    rank = lows.shape[0] // 5
    base = received.shape[0] - 3 * rank
    count = len(weights)

    def body(z_ref, gy_ref, branch_in, second_in, lows_in, received_ref, far_side_ref, *refs):
        ins, (branch_ref, second_ref, lows_ref, sums_ref) = refs[:count], refs[count : count + 4]
        wide, thin, act_ref, grad_ref, sems = refs[count + 4 :]
        copies = far_copies(ins, wide, thin, sems)
        total = far_parts(
            parts, z_ref, gy_ref, copies, wide, thin, received_ref, far_side_ref, rank, base,
            lows_in[rank : 2 * rank], lows_in[2 * rank : 3 * rank], act_ref, grad_ref, sums_ref,
        )
        branch_ref[...] = branch_in[...] + total[0]
        second_ref[...] = second_in[...] + total[1]
        lows_ref[: 3 * rank] = lows_in[: 3 * rank]
        lows_ref[3 * rank : 4 * rank] = lows_in[3 * rank : 4 * rank] + total[2]
        lows_ref[4 * rank :] = lows_in[4 * rank :] + total[3]

    operands = [z, gy, branch, second, lows, received, far_side] + weights
    outs = [
        shaped(branch.shape, f32),
        shaped(second.shape, f32),
        shaped(lows.shape, f32),
        shaped((2 * rank, 2 * len(parts) * part), f32),
    ]
    return call(
        body, (), operands, [KEEP] * 7 + [in_hbm] * count, outs, [KEEP] * 4,
        scratch=far_scratch(parts, part, features, tokens), aliases={2: 0, 3: 1}, limit=BIG,
    )


def shares(array, core):
    half = array.shape[1] // 2
    low, high = array[:, :half], array[:, half:]
    return jnp.where(core == 0, low, high), jnp.where(core == 0, high, low)


def padded(array, count):
    return jnp.concatenate([array, jnp.zeros((array.shape[0], count - array.shape[1]), array.dtype)], axis=1)


def lanes_up(count):
    return (count + 127) // 128 * 128


def feed_close(parts, spot, pick, lengths, hidden, z, gy, branch, second, lows, near_sums, far_sums, contexts, outs_w, far, packs, tables, received, cotangent, cot_side, gain, weights):
    tokens, features = hidden.shape
    rows = tokens // 2
    width = contexts[0].shape[1]
    rank = tables[0].shape[1]
    pack, side, far_side = packs
    base = received.shape[0] - 3 * rank
    part = weights[0].shape[0]
    units = 4 * part
    heads = width // HEAD_DIM
    half = features // 2
    tail = lanes_up(width)
    total_lanes = 3 * half + 2 * (2 * units + tail)

    def body(spot_ref, pick_ref, length_ref, hidden_ref, z_ref, gy_ref, branch_in, second_in, lows_ref, near0, near1, far0, far3, c01, c23, wo0, wo1, far_ref, pack_ref, side_ref, far_side_ref, received_ref, oo, wi, no, ca, cb, gain_ref, *refs):
        hbm, (out_ref, outb_ref, gh_ref, gc_ref, delta_ref, keep_ref, give_ref) = refs[:8], refs[8:15]
        wide, thin, act_ref, grad_ref, sems, last, ga_ref = refs[15:]
        copies = far_copies(hbm, wide, thin, sems)
        low_w = lows_ref[rank : 2 * rank]
        low_n = lows_ref[2 * rank : 3 * rank]
        found = far_parts(
            parts, z_ref, gy_ref, copies, wide, thin, received_ref, far_side_ref, rank, base,
            low_w, low_n, act_ref, grad_ref, last,
        )
        branch = branch_in[...] + found[0]
        grad_second = second_in[...] + found[1]
        low_next = lows_ref[3 * rank : 4 * rank] + found[2]
        grad_low = lows_ref[4 * rank :] + found[3]
        mask = live_column(spot_ref, length_ref, rows, (0, 2)).astype(f32)
        branch = branch + tn(halves(low_next), twice(no[0]))
        grad_second = grad_second + tn(halves(grad_low), twice(wi[0]))
        hidden_now = hidden_ref[...]
        output = (hidden_now + mask * branch).astype(bf16)
        out_ref[0] = output[:rows]
        outb_ref[...] = output[rows:]
        _, unit, scaled = normalize(hidden_now, gain_ref[...], gain_ref[...])
        grad_in = jnp.concatenate([ca[0], cb[...]], axis=0).astype(f32)
        grad_hidden = grad_in + normalize_back(grad_second, unit, scaled, gain_ref[...])
        gh_ref[...] = grad_hidden
        ga_ref[...] = (mask * grad_hidden).astype(bf16)
        grad_low_o = nt(oo[0], ga_ref[...])
        low_o2 = halves(grad_low_o)
        inner_o = output_inner_rows(pack_ref, side_ref, received_ref, far_side_ref, rank, base, width)
        contexts_all = [c01[0], c01[1], c23[0], c23[1]]
        weights_all = [wo0, wo1, far_ref.at[0, 0], far_ref.at[1, 0]]
        inner_sums = []
        for i in range(4):
            grad = (nt(weights_all[i][...], ga_ref[...]) + tn(twice(inner_o[i]), low_o2)).astype(bf16)
            gc_ref[i] = grad
            product = grad.astype(f32) * contexts_all[i].astype(f32)
            for h in range(heads):
                delta_ref[heads * i + h] = jnp.sum(
                    product[h * HEAD_DIM : (h + 1) * HEAD_DIM], axis=0, keepdims=True
                )
            inner_sums.append(folded(nt(low_o2, contexts_all[i])))
        core = spot_ref[3] & 1
        quad = spot_ref[2]
        shared = (
            folded(nn(halves(grad_low), z_ref[...])),
            folded(nn(halves(lows_ref[:rank]), ga_ref[...])),
            folded(nn(halves(low_next), gy_ref[...])),
        )
        for n in range(3):
            keep_ref[:, n * half : (n + 1) * half], give_ref[:, n * half : (n + 1) * half] = shares(shared[n], core)
        quarters = []
        for near in (near0, near1):
            quarters.append((near[:rank], near[rank:]))
        for q in range(2):
            lanes = slice(q * part, (q + 1) * part)
            later = slice((2 + q) * part, (3 + q) * part)
            pieces = [far0[:, lanes], last[:, lanes], last[:, later], far3[:, lanes]]
            joined = shuffled(jnp.concatenate(pieces, axis=1), quad)
            quarters.append((joined[:rank], joined[rank:]))
        for i in range(4):
            ref = (keep_ref, give_ref)[i % 2]
            at = 3 * half + (i // 2) * (2 * units + tail)
            ref[:, at : at + units] = quarters[i][0]
            ref[:, at + units : at + 2 * units] = quarters[i][1]
            ref[:, at + 2 * units : at + 2 * units + tail] = padded(inner_sums[i], tail)

    operands = [hidden, z, gy, branch, second, lows] + near_sums + far_sums + contexts + outs_w
    specs = [whole(hidden.shape), KEEP, KEEP, KEEP, KEEP] + [whole(o.shape) for o in operands[5:]]
    operands += [far, pack, side, far_side, received] + tables
    specs += [placed_block((2, 1, width, features), lambda *_: (0, 3, 0, 0))]
    specs += [whole(p.shape) for p in packs] + [whole(received.shape)]
    specs += [placed_block((1, rank, features), of_mine(n)) for n in (3, 4, 5)]
    operands += [cotangent, cot_side, gain] + weights
    specs += [placed_block((1, rows, features), lambda i, spot, *_: (spot[0], 0, 0))]
    specs += [whole(cot_side.shape), whole(gain.shape)] + [remain] * 8
    outs = [
        shaped((2, rows, features), bf16),
        shaped((rows, features), bf16),
        shaped((tokens, features), f32),
        shaped((4, width, tokens), bf16),
        shaped((4 * heads, 1, tokens), f32),
        shaped((rank, total_lanes), f32),
        shaped((rank, total_lanes), f32),
    ]
    scratch = far_scratch(parts, part, features, tokens)
    scratch += [pltpu.VMEM((2 * rank, 4 * part), f32), pltpu.VMEM((tokens, features), bf16)]
    out_specs = [placed_block((1, rows, features), lambda i, spot, *_: (spot[0], 0, 0))] + [KEEP] * 6
    return call(body, (spot, pick, lengths), operands, specs, outs, out_specs, scratch=scratch, limit=BIG)


def gather_pair(quarters, low, factors, before=None):
    rank = low.shape[0] // 3
    width, tokens = quarters[0][0].shape
    tail = lanes_up(3 * width)
    extra = 0 if before is None else 1

    def body(*refs):
        groups = [refs[3 * i : 3 * i + 3] for i in range(2)]
        low_ref, *places = refs[6:9]
        g_ref, gl_ref, keep_ref, give_ref = refs[9 + extra :]
        lows = [halves(low_ref[n * rank : (n + 1) * rank]) for n in range(3)]
        for n in range(3):
            at = slice(n * rank, (n + 1) * rank)
            total = jnp.zeros((rank, tokens), f32) if before is None else refs[9][at]
            for i in range(2):
                q, own, other = groups[i][0], groups[i][1], groups[1 - i][2]
                if n == 0:
                    g = q[...]
                else:
                    g = (own[n - 1] + other[n - 1].astype(f32)).astype(bf16)
                g_ref[i, n] = g
                total = total + nn(places[i][:rank, n * width : (n + 1) * width], g)
                (keep_ref, give_ref)[i][:, n * width : (n + 1) * width] = folded(nt(lows[n], g))
            gl_ref[at] = total
        for ref in (keep_ref, give_ref):
            ref[:, 3 * width :] = jnp.zeros((rank, tail - 3 * width), f32)

    operands = [a for q in quarters for a in q] + [low] + list(factors) + ([] if before is None else [before])
    outs = [
        shaped((2, 3, width, tokens), bf16),
        shaped((3 * rank, tokens), f32),
        shaped((rank, tail), f32),
        shaped((rank, tail), f32),
    ]
    return call(body, (), operands, [KEEP] * len(operands), outs, [KEEP] * 4, weight=3)


def gather_inner(spot, gl, z, first, second):
    features = z.shape[1]
    rank = gl.shape[0] // 3
    half = features // 2
    tail = first[0].shape[1]

    def body(spot_ref, gl_ref, z_ref, a0, b0, a1, b1, keep_ref, give_ref):
        core = spot_ref[3] & 1
        for n in range(3):
            inner = folded(nn(halves(gl_ref[n * rank : (n + 1) * rank]), z_ref[...]))
            keep_ref[:, n * half : (n + 1) * half], give_ref[:, n * half : (n + 1) * half] = shares(inner, core)
        for ref, pieces in ((keep_ref, (a0, a1)), (give_ref, (b0, b1))):
            for i in range(2):
                ref[:, 3 * half + i * tail : 3 * half + (i + 1) * tail] = pieces[i][...]

    out = shaped((rank, 3 * half + 2 * tail), f32)
    operands = [gl, z] + list(first) + list(second)
    return call(body, (spot,), operands, [KEEP] * 6, [out, out], [KEEP] * 2, weight=2)


def settle(spot, pick, keep, moved, common, with_picks):
    rank, lanes = keep.shape
    own = (lanes - common) // 2
    extra = 128 if with_picks else 0

    def body(spot_ref, pick_ref, keep_ref, moved_ref, here_ref, there_ref):
        total = (keep_ref[...] + moved_ref[...]).astype(bf16)
        here_ref[:, : common + own] = total[:, : common + own]
        there_ref[:, :common] = total[:, :common]
        there_ref[:, common : common + own] = total[:, common + own :]
        if with_picks:
            iota = lax.broadcasted_iota(jnp.int32, (rank, 128), 1)
            line = jnp.zeros((rank, 128), f32)
            for n in range(6):
                line = jnp.where(iota == n, pick_ref[spot_ref[0], n].astype(f32), line)
            here_ref[:, common + own :] = line.astype(bf16)
            there_ref[:, common + own :] = line.astype(bf16)

    out = shaped((rank, common + own + extra), bf16)
    return call(body, (spot, pick), [keep, moved], [whole(keep.shape)] * 2, [out, out], [whole(out.shape)] * 2, weight=1)


def combine(spot, picks, arrays, groups, rows_of_table):
    per, rank = arrays[0].shape[:2]
    half = groups[0][1]

    def body(spot_ref, pick_ref, *refs):
        ins, outs = refs[: len(arrays)], refs[len(arrays) :]
        places = [outs[0].at[n] for n in range(3)] + list(outs[4:])
        for out in places:
            out[...] = jnp.zeros(out.shape, f32)
        for a, ref in enumerate(ins):
            for c in range(per):
                for (start, count, number), out in zip(groups, places):
                    row = pick_ref[a * per + c, number]
                    out[row] += ref[c, :, start : start + count].astype(f32)
        for n in range(3):
            outs[1 + n][...] = outs[0][n]

    outs = [shaped((3, rows_of_table, rank, half), f32)] + [shaped((rows_of_table, rank, 2 * half), f32)] * 3
    outs += [shaped((rows_of_table, rank, count), f32) for _, count, _ in groups[3:]]
    own = placed_block((rows_of_table, rank, half), lambda i, spot, pick: (0, 0, spot[3] & 1))
    specs = [KEEP] + [own] * 3 + [KEEP] * (len(groups) - 3)
    return call(body, (spot, picks), list(arrays), [KEEP] * len(arrays), outs, specs, weight=100)


def complete(spot, tables, moved):
    _, count, rank, half = moved.shape

    def body(spot_ref, moved_ref, *refs):
        for n in range(3):
            refs[3 + n][...] = moved_ref[n]

    out = shaped((count, rank, 2 * half), f32)
    theirs = placed_block((count, rank, half), lambda i, spot: (0, 0, 1 - (spot[3] & 1)))
    return call(
        body, (spot,), [moved] + list(tables), [KEEP] + [remain] * 3, [out] * 3, [theirs] * 3,
        aliases={2: 0, 3: 1, 4: 2}, weight=2)


def pair_up(spot, array, second):
    rows, features = second.shape

    def body(spot_ref, array_ref, second_ref, out_ref):
        out_ref[0] = second_ref[...].astype(array.dtype)

    out_spec = placed_block((1, rows, features), lambda i, spot: (spot[1], 0, 0))
    return call(
        body, (spot,), [array, second], [remain, KEEP], shaped(array.shape, array.dtype), out_spec, aliases={1: 0}, weight=1)


def join(groups):
    flat = [a for g in groups for a in g]
    outs = [shaped((sum(a.shape[0] for a in g),) + g[0].shape[1:], g[0].dtype) for g in groups]

    def body(*refs):
        at = 0
        for g, out in zip(groups, refs[len(flat) :]):
            start = 0
            for a in g:
                out[start : start + a.shape[0]] = refs[at][...]
                start += a.shape[0]
                at += 1

    return call(body, (), flat, [KEEP] * len(flat), outs, [KEEP] * len(outs), weight=1)


def finish(spot, pick, g01, g23, gl, inners, weights, far, states, grad_hidden, gain, block):
    features = gain.shape[1]
    rows = g01.shape[3] // 2
    width = g01.shape[2]
    rank = gl.shape[0] // 3
    at = slice(block * rows, (block + 1) * rows)

    def body(spot_ref, pick_ref, g01_ref, g23_ref, gl_ref, iq, ik, iv, *refs):
        ws, (far_ref, x_ref, gh_ref, gain_ref, grad_ref) = refs[:6], refs[6:]
        low = [halves(gl_ref[n * rank : (n + 1) * rank, at]) for n in range(3)]
        total = tn(
            jnp.concatenate(low, axis=0),
            jnp.concatenate([twice(iq[0]), twice(ik[0]), twice(iv[0])], axis=0),
        )
        for i in range(4):
            if i < 2:
                weight = jnp.concatenate([w[...] for w in ws[3 * i : 3 * i + 3]], axis=0)
            else:
                weight = far_ref[i - 2].reshape(3 * width, features)
            g_ref = (g01_ref, g23_ref)[i // 2]
            total = total + tn(g_ref[i % 2, :, :, at].reshape(3 * width, rows), weight)
        x = x_ref[0] if block == 0 else x_ref[...]
        _, unit, scaled = normalize(x.astype(f32), gain_ref[...], gain_ref[...])
        grad = gh_ref[at] + normalize_back(total, unit, scaled, gain_ref[...])
        if block == 0:
            grad_ref[0] = grad
        else:
            grad_ref[...] = grad.astype(bf16)

    operands = [g01, g23, gl] + inners + weights + [far, states, grad_hidden, gain]
    specs = [KEEP] * 3
    specs += [placed_block((1, rank, features), of_mine(n)) for n in range(3)]
    specs += [KEEP] * 6
    specs += [placed_block((2, 3, width, features), lambda *_: (0, 0, 0, 0))]
    if block == 0:
        specs += [placed_block((1, rows, features), lambda i, spot, *_: (spot[0], 0, 0))]
        out, out_spec = shaped((2, rows, features), f32), placed_block((1, rows, features), lambda i, spot, *_: (spot[0], 0, 0))
    else:
        specs += [placed_block((rows, features), lambda *_: (0, 0))]
        out, out_spec = shaped((rows, features), bf16), KEEP
    specs += [KEEP] * 2
    return call(body, (spot, pick), operands, specs, out, out_spec, weight=5)


def make_body(dp_size, tensor_size):
    def across(array):
        return swap(array, "tensor", 2, tensor_size)

    def beside(array):
        return swap(array, "tensor", 1, tensor_size)

    def along(array, bits):
        return swap(array, "dp", bits, dp_size)

    def body(
        inputs,
        cotangent,
        lengths,
        adapter_pick,
        first_gain,
        first_bias,
        query_weight,
        key_weight,
        value_weight,
        output_weight,
        second_gain,
        second_bias,
        widen_weight,
        narrow_weight,
        query_inner,
        query_outer,
        key_inner,
        key_outer,
        value_inner,
        value_outer,
        output_inner,
        output_outer,
        widen_inner,
        widen_outer,
        narrow_inner,
        narrow_outer,
    ):
        rows, features = inputs.shape[1:]
        place = lax.axis_index("tensor")
        quad = lax.axis_index("dp") & 3
        mine = place >> 1
        spot = jnp.stack([mine, 1 - mine, quad, place]).astype(jnp.int32)
        pick = adapter_pick

        def flip(array):
            return jnp.swapaxes(array, 1, 2)

        small = [query_outer, key_outer, value_outer, flip(output_inner), widen_outer, flip(narrow_inner)]
        inners = [flip(query_inner), flip(key_inner), flip(value_inner)]
        tables = [output_outer, flip(widen_inner), narrow_outer]
        gains = [v.reshape(1, -1) for v in (first_gain, first_bias, second_gain, second_bias)]
        heads = [query_weight.T, key_weight.T, value_weight.T, output_weight]
        dense = [widen_weight, narrow_weight]
        width = query_outer.shape[2]
        half = features // 2

        head_rows = heads[0].shape[0] // 4
        part_heads = jnp.stack([lax.dynamic_slice_in_dim(w, quad * head_rows, head_rows, 0) for w in heads])
        far0 = across(part_heads)
        send, pack = stage(after(spot, part_heads), pick, inputs, small)
        near_heads = [beside(w) for w in after(heads, part_heads)]
        received = across(after(send, near_heads[:2]))
        side = beside(pack)
        near_dense = [beside(after(dense[0], near_heads))]
        near_dense.append(beside(after(dense[1], near_dense[0])))
        part_wide, part_thin, part_last, cot_send = stage_dense(
            after(spot, pack), widen_weight, narrow_weight, cotangent
        )
        far1, far2 = along(far0, 1), along(far0, 2)
        wide0 = across(after(part_wide, far0))
        z, low, kv01 = project_near(
            spot, pick, inputs, after(received, part_wide, side, far0, near_dense), gains[0], gains[1], inners, pack,
            side, [heads[1], heads[2], near_heads[1], near_heads[2]],
        )
        kv01_side = beside(kv01)
        q01 = queries_near(after(z, kv01), low, pack, side, [heads[0], near_heads[0]])
        far3, far4 = along(after(far2[:2], kv01), 1), along(after(far1[2:], kv01), 2)
        side0 = beside(after(far0, kv01))
        side1 = beside(after(far1, kv01, side0))
        c01, total01 = attend(spot, lengths, q01, kv01, after(kv01_side, side1))
        side2 = beside(after(far2, c01, side1))
        far_side = beside(after(received[rows:], c01))
        side3, side4 = beside(after(far3, c01)), beside(after(far4, c01))
        wide1, wide2 = along(after(wide0, c01), 1), along(after(wide0, c01), 2)
        cot_side = across(after(cot_send, c01))
        far, kv23, q23 = project_far(
            spot, after(z, c01, wide0), low, received, far_side,
            [[far0, far1, far2, far3, far4], [side0, side1, side2, side3, side4]],
        )
        kv23_side = beside(kv23)
        thin0 = across(after(part_thin, kv23))
        c23, total23 = attend(spot, lengths, q23, kv23, kv23_side)
        packs = [pack, side, far_side]
        outs_w = [heads[3], near_heads[3]]
        hidden, z2, lows = feed_open(
            spot, pick, lengths, [c01, c23], outs_w, far, packs, tables, inputs, received, gains[2], gains[3]
        )
        wide3 = along(after(wide2, lows), 1)
        thin3 = across(after(part_last, lows))
        wide_sides = [beside(after(w, lows)) for w in (wide0, wide1, wide2)]
        gy, branch, second, lows, sums0 = feed_first(
            spot, pick, lengths, z2, lows, tables[2], cotangent, cot_side, pack, dense
        )
        thin1, thin2 = along(after(thin0, lows), 1), along(after(thin0, lows), 2)
        thin_sides = [beside(after(thin0, lows))]
        branch, second, lows, sums1 = feed_near(
            z2, gy, branch, second, after(lows, wide_sides), side, near_dense
        )
        wide_sides.append(beside(after(wide3, sums1)))
        branch, second, lows, sums2 = feed_far(
            (0,), z2, gy, branch, second, lows, received, far_side, [wide0, wide_sides[0], thin0, thin_sides[0]]
        )
        thin_sides += [beside(after(t, sums2)) for t in (thin1, thin2, thin3)]
        branch, second, lows, sums3 = feed_far(
            (3,), z2, gy, branch, second, lows, received, far_side, [wide3, wide_sides[3], thin3, thin_sides[3]]
        )
        output, outb, grad_hidden, grad_context, deltas, keep, give = feed_close(
            (1, 2), spot, pick, lengths, hidden, z2, gy, branch, second, lows, [sums0, sums1], [sums2, sums3],
            [c01, c23], outs_w, far, packs, tables, received, cotangent, cot_side, gains[2],
            [wide1, wide_sides[1], thin1, thin_sides[1], wide2, wide_sides[2], thin2, thin_sides[2]],
        )

        def first_turn(here, other, crossed):
            one, two = join([[here[None], crossed[0][None]], [other[None], crossed[1][None]]])
            return [(one, along(one, 1)), (two, along(two, 2))]

        def second_turn(turns):
            one, two = join(turns)
            return [one, along(one, 2), two, along(two, 1)]

        def whole_sum(table):
            bits = 8
            while bits < dp_size:
                table = table + along(table, bits)
                bits *= 2
            return table

        def back(number, q, kv, kv_side, totals):
            gq, own, other = attend_back(spot, lengths, q, kv, kv_side, grad_context, totals, deltas, number)
            return gq, own, other

        moved = beside(give)
        here, there = settle(spot, pick, keep, moved, 3 * half, True)
        other = across(there)
        out_side = across(outb)
        crossed = [along(here, 4)]
        quarters = [back(0, after(q01, here), kv01, kv01_side, total01)]
        quarters.append(back(1, after(q01, quarters[0][0]), kv01, kv01_side, total01))
        sides = [beside(after(quarters[0][2], quarters[1][0]))]
        crossed.append(along(after(other, quarters[1][0]), 4))
        quarters.append(back(2, after(q23, quarters[1][0], out_side), kv23, kv23_side, total23))
        sides.append(beside(after(quarters[1][2], quarters[2][0], sides[0])))
        turns = first_turn(here, other, after(crossed, quarters[2][0]))
        quarters.append(back(3, after(q23, quarters[2][0], turns[0][0]), kv23, kv23_side, total23))
        pieces = [(gq, own, sided) for (gq, own, _), sided in zip(quarters, sides)]
        g01, gl, *first = gather_pair(
            [pieces[0], (after(pieces[1][0], quarters[3][0]),) + pieces[1][1:]], after(low, turns), [pack, side]
        )
        early = second_turn(after(turns, g01))
        sides += [beside(after(q[2], g01)) for q in quarters[2:]]
        pieces += [(gq, own, sided) for (gq, own, _), sided in zip(quarters[2:], sides[2:])]
        far_factors = [received[rows:], far_side]
        g23, gl, *second = gather_pair(pieces[2:], low, far_factors, gl)
        keep, give = gather_inner(spot, gl, z, first, second)
        moved = beside(give)
        here, there = settle(spot, pick, keep, moved, 3 * half, False)
        other = across(there)
        crossed = [along(here, 4)]
        crossed.append(along(other, 4))
        ends = (gl, inners, heads[:3] + near_heads[:3], far)
        gradb = finish(spot, pick, g01, after(g23, other), *ends, received, grad_hidden, gains[0], 1)
        grad_side = across(gradb)
        grad = finish(spot, pick, g01, after(g23, gradb, crossed), *ends, inputs, grad_hidden, gains[0], 0)
        turns = first_turn(here, other, after(crossed, gradb))
        output = pair_up(spot, output, after(out_side, grad))
        early = after(early, gradb, turns[0][0])
        picks = jnp.concatenate([a[:, 0, -128:-122] for a in early]).astype(jnp.int32)
        adapters = query_inner.shape[0]
        units = widen_weight.shape[1]
        base = 3 * half
        early = combine(
            spot,
            after(picks, gradb),
            early,
            [
                (0, half, 4),
                (half, half, 3),
                (2 * half, half, 5),
                (base, units, 4),
                (base + units, units, 5),
                (base + 2 * units, width, 3),
            ],
            adapters,
        )
        early = [whole_sum(t) for t in early]
        early_shared = complete(spot, early[1:4], beside(early[0]))
        late = second_turn(turns)
        input_grad = pair_up(spot, grad, grad_side)
        late = combine(
            spot,
            after(picks, grad_side, output),
            late,
            [(n * half, half, n) for n in range(3)] + [(base + n * width, width, n) for n in range(3)],
            adapters,
        )
        late = [whole_sum(t) for t in late]
        late_shared = complete(spot, late[1:4], beside(late[0]))
        return (
            output,
            input_grad,
            flip(late_shared[0]),
            late[4],
            flip(late_shared[1]),
            late[5],
            flip(late_shared[2]),
            late[6],
            flip(early[6]),
            early_shared[1],
            flip(early_shared[0]),
            early[4],
            flip(early[5]),
            early_shared[2],
        )

    return body


def solution(mesh):
    placed = (
        P("dp", "tensor", None),
        P("dp", "tensor", None),
        P("dp"),
        P("dp", None),
        P(),
        P(),
        P(None, "tensor"),
        P(None, "tensor"),
        P(None, "tensor"),
        P("tensor", None),
        P(),
        P(),
        P(None, "tensor"),
        P("tensor", None),
        P(),
        P(None, None, "tensor"),
        P(),
        P(None, None, "tensor"),
        P(),
        P(None, None, "tensor"),
        P(None, "tensor", None),
        P(),
        P(),
        P(None, None, "tensor"),
        P(None, "tensor", None),
        P(),
    )
    return jax.shard_map(
        make_body(mesh.shape["dp"], mesh.shape["tensor"]),
        mesh=mesh,
        in_specs=placed,
        out_specs=(
            P("dp", "tensor", None),
            P("dp", "tensor", None),
            P(),
            P(None, None, "tensor"),
            P(),
            P(None, None, "tensor"),
            P(),
            P(None, None, "tensor"),
            P(None, "tensor", None),
            P(),
            P(),
            P(None, None, "tensor"),
            P(None, "tensor", None),
            P(),
        ),
        check_vma=False,
    )
```

```python
import functools
import math

import jax
import jax.numpy as jnp
from jax import lax
from jax.experimental import pallas as pl
from jax.experimental.pallas import tpu as pltpu
from jax.sharding import PartitionSpec as P

HEAD_DIM = 80
f32 = jnp.float32
bf16 = jnp.bfloat16
neg_fill = -1000000000.0
score_scale = 1.0 / math.sqrt(HEAD_DIM)
log2_e = math.log2(math.e)
LIMIT = 16
KEEP = pl.BlockSpec(memory_space=pltpu.VMEM)
remain = pl.BlockSpec(memory_space=pl.ANY)
in_hbm = pl.BlockSpec(memory_space=pltpu.HBM)


def swap(array, axis, bits, size):
    return lax.ppermute(array, axis, [(i, i ^ bits) for i in range(size)])


def nn(a, b):
    return jnp.dot(a, b, preferred_element_type=f32)


def nt(a, b):
    return lax.dot_general(a, b, (((1,), (1,)), ((), ())), preferred_element_type=f32)


def tn(a, b):
    return lax.dot_general(a, b, (((0,), (0,)), ((), ())), preferred_element_type=f32)


def halves(low):
    top = low.astype(bf16)
    return jnp.concatenate([top, (low - top.astype(f32)).astype(bf16)], axis=0)


def twice(factor):
    return jnp.concatenate([factor, factor], axis=0)


def folded(pair):
    count = pair.shape[0] // 2
    return pair[:count] + pair[count:]


def normalize(states, gain, shift):
    centre = states - jnp.mean(states, axis=-1, keepdims=True)
    scaled = lax.rsqrt(jnp.mean(centre * centre, axis=-1, keepdims=True) + 1e-05)
    unit = centre * scaled
    return unit * gain + shift, unit, scaled


def normalize_back(grad_rows, unit, scaled, gain):
    grad_unit = grad_rows * gain
    return scaled * (
        grad_unit
        - jnp.mean(grad_unit, axis=-1, keepdims=True)
        - unit * jnp.mean(grad_unit * unit, axis=-1, keepdims=True)
    )


def live_column(spot_ref, length_ref, rows, bits):
    iota = lax.broadcasted_iota(jnp.int32, (2 * rows, 1), 0)
    place = spot_ref[3]
    first, second = place ^ bits[0], place ^ bits[1]
    position = jnp.where(iota < rows, first * rows + iota, second * rows + iota - rows)
    return position < length_ref[spot_ref[0]]


def whole(shape):
    return KEEP


def placed_block(shape, index):
    return pl.BlockSpec(shape, index, pipeline_mode=pl.Buffered(1))


def call(body, scalars, operands, specs, outs, out_specs, grid=(1,), scratch=(), limit=LIMIT, aliases=None, weight=100):
    return pl.pallas_call(
        body,
        grid_spec=pltpu.PrefetchScalarGridSpec(
            num_scalar_prefetch=len(scalars),
            grid=grid,
            in_specs=specs,
            out_specs=out_specs,
            scratch_shapes=list(scratch),
        ),
        out_shape=outs,
        cost_estimate=pl.CostEstimate(flops=weight * 10**9, bytes_accessed=100000, transcendentals=0),
        input_output_aliases=aliases or {},
        compiler_params=pltpu.CompilerParams(vmem_limit_bytes=limit * 2**20),
    )(*scalars, *operands)


def shaped(shape, dtype):
    return jax.ShapeDtypeStruct(shape, dtype)


def of_mine(number):
    return lambda i, spot, pick, *_: (pick[spot[0], number], 0, 0)


def of_other(number):
    return lambda i, spot, pick, *_: (pick[spot[1], number], 0, 0)


def after(values, *others):
    return lax.optimization_barrier((values, others))[0]


def shuffled(array, quad):
    count = array.shape[1] // 4
    blocks = [array[:, n * count : (n + 1) * count] for n in range(4)]
    for bits in (1, 2):
        on = ((quad >> (bits - 1)) & 1) == 1
        blocks = [jnp.where(on, blocks[n ^ bits], blocks[n]) for n in range(4)]
    return jnp.concatenate(blocks, axis=1)


def stage(spot, pick, inputs, factors):
    rows, features = inputs.shape[1:]
    rank = factors[0].shape[1]

    def body(spot_ref, pick_ref, inputs_ref, *refs):
        send_ref, pack_ref = refs[12:]
        send_ref[:rows] = inputs_ref[0]
        quad = spot_ref[2]
        for group, ref, base in ((refs[:6], pack_ref, 0), (refs[6:12], send_ref, rows)):
            ref[base : base + rank] = jnp.concatenate([r[0] for r in group[:4]], axis=1)
            wide, thin = group[4][0], group[5][0]
            if base:
                wide, thin = shuffled(wide, quad), shuffled(thin, quad)
            ref[base + rank : base + 2 * rank] = wide
            ref[base + 2 * rank : base + 3 * rank] = thin

    specs = [placed_block((1, rows, features), lambda i, spot, *_: (spot[1], 0, 0))]
    for of in (of_mine, of_other):
        specs += [placed_block((1,) + f.shape[1:], of(n)) for n, f in enumerate(factors)]
    outs = [shaped((rows + 3 * rank, features), bf16), shaped((3 * rank, features), bf16)]
    return call(body, (spot, pick), [inputs] + factors * 2, specs, outs, [whole(o.shape) for o in outs])


def stage_dense(spot, wide, thin, cotangent):
    features, units = wide.shape
    part = units // 4
    rows = cotangent.shape[1]

    def body(spot_ref, wide_ref, thin_ref, last_ref, cot_ref, wide_out, thin_out, last_out, cot_out):
        for r in range(4):

            @pl.when(spot_ref[2] == r)
            def _():
                wide_out[...] = wide_ref[:, r * part : (r + 1) * part].T

        thin_out[...] = thin_ref[...]
        last_out[...] = last_ref[...]
        cot_out[...] = cot_ref[0]

    specs = [
        whole(wide.shape),
        placed_block((part, features), lambda i, spot: (spot[2], 0)),
        placed_block((part, features), lambda i, spot: (spot[2] ^ 3, 0)),
        placed_block((1, rows, features), lambda i, spot: (spot[1], 0, 0)),
    ]
    outs = [shaped((part, features), bf16)] * 3 + [shaped((rows, features), bf16)]
    return call(body, (spot,), [wide, thin, thin, cotangent], specs, outs, [whole(o.shape) for o in outs])


def project_rows(weight, rows_in, outer, low):
    return (nt(weight, rows_in) + tn(twice(outer), halves(low))).astype(bf16)


def project_near(spot, pick, inputs, received, gain, shift, inners, pack, side, weights):
    rows, features = inputs.shape[1:]
    tokens = 2 * rows
    width = weights[0].shape[0]
    rank = inners[0].shape[1]

    def body(spot_ref, pick_ref, xa, xb, gain_ref, shift_ref, iq, ik, iv, pack_ref, side_ref, *refs):
        hbm, (z_ref, low_ref, kv_ref, ws, sems) = refs[:4], refs[4:]
        copies = [pltpu.make_async_copy(hbm[n], ws.at[n], sems.at[n]) for n in range(4)]
        for c in copies:
            c.start()
        states = jnp.concatenate([xa[0], xb[...]], axis=0).astype(f32)
        z_ref[...] = normalize(states, gain_ref[...], shift_ref[...])[0].astype(bf16)
        low = nt(jnp.concatenate([iq[0], ik[0], iv[0]], axis=0), z_ref[...])
        low_ref[...] = low
        for i, packs in enumerate((pack_ref, side_ref)):
            for n in (1, 2):
                outer = packs[:rank, n * width : (n + 1) * width]
                copies[2 * i + n - 1].wait()
                kv_ref[i, n - 1] = project_rows(
                    ws[2 * i + n - 1], z_ref[...], outer, low[n * rank : (n + 1) * rank]
                )

    specs = [
        placed_block((1, rows, features), lambda i, spot, *_: (spot[0], 0, 0)),
        placed_block((rows, features), lambda *_: (0, 0)),
        whole((1, features)),
        whole((1, features)),
    ]
    specs += [placed_block((1, rank, features), of_mine(n)) for n in range(3)]
    specs += [whole(pack.shape), whole(side.shape)] + [in_hbm] * 4
    outs = [
        shaped((tokens, features), bf16),
        shaped((3 * rank, tokens), f32),
        shaped((2, 2, width, tokens), bf16),
    ]
    return call(
        body,
        (spot, pick),
        [inputs, received, gain, shift] + inners + [pack, side] + weights,
        specs,
        outs,
        [whole(o.shape) for o in outs],
        scratch=[pltpu.VMEM((4, width, features), bf16), pltpu.SemaphoreType.DMA((4,))],
    )


def queries_near(z, low, pack, side, weights):
    tokens, features = z.shape
    width = weights[0].shape[0]
    rank = low.shape[0] // 3

    def body(z_ref, low_ref, pack_ref, side_ref, w0, w1, q_ref):
        for i, (packs, w) in enumerate(((pack_ref, w0), (side_ref, w1))):
            q_ref[i] = project_rows(w[...], z_ref[...], packs[:rank, :width], low_ref[:rank])

    operands = [z, low, pack, side] + weights
    out = shaped((2, width, tokens), bf16)
    return call(body, (), operands, [whole(o.shape) for o in operands], out, whole(out.shape))


def project_far(spot, z, low, received, side, parts):
    tokens, features = z.shape
    head_rows = parts[0][0].shape[1]
    width = 4 * head_rows
    rank = low.shape[0] // 3
    base = received.shape[0] - 3 * rank
    flat = [p for group in parts for p in group]

    def body(spot_ref, z_ref, low_ref, received_ref, side_ref, *refs):
        ins, (out_ref, kv_ref, q_ref, weight_ref, sems) = refs[:10], refs[10:]
        for i in range(2):
            group = ins[5 * i : 5 * i + 5]
            for n in range(4):
                for r in range(4):
                    at = pl.ds(pl.multiple_of((spot_ref[0] ^ r) * head_rows, 16), head_rows)
                    if r < 3:
                        weight_ref[i, n, at] = group[r][n]
                    else:
                        weight_ref[i, n, at] = group[3 + n // 2][n % 2]
        copies = [pltpu.make_async_copy(weight_ref.at[i], out_ref.at[i], sems.at[i]) for i in range(2)]
        for c in copies:
            c.start()
        for i, (ref, start) in enumerate(((received_ref, base), (side_ref, 0))):
            for n in range(3):
                outer = ref[start : start + rank, n * width : (n + 1) * width]
                y = project_rows(weight_ref[i, n], z_ref[...], outer, low_ref[n * rank : (n + 1) * rank])
                if n == 0:
                    q_ref[i] = y
                else:
                    kv_ref[i, n - 1] = y
        for c in copies:
            c.wait()

    operands = [z, low, received, side] + flat
    outs = [
        shaped((2, 4, width, features), bf16),
        shaped((2, 2, width, tokens), bf16),
        shaped((2, width, tokens), bf16),
    ]
    return call(
        body, (spot[2:3],), operands, [KEEP] * len(operands), outs, [remain, KEEP, KEEP],
        scratch=[pltpu.VMEM((2, 4, width, features), bf16), pltpu.SemaphoreType.DMA((2,))],
    )


def attend(spot, lengths, q, kv, kv_side):
    _, width, tokens = q.shape
    rows = tokens // 2
    pair = 2 * HEAD_DIM
    steps = width // pair

    def body(spot_ref, length_ref, q_ref, k1, k2, v1, v2, ctx_ref, total_ref):
        bias1 = jnp.where(live_column(spot_ref, length_ref, rows, (0, 2)), 0.0, neg_fill * log2_e)
        bias2 = jnp.where(live_column(spot_ref, length_ref, rows, (1, 3)), 0.0, neg_fill * log2_e)
        for h in range(2):
            at = slice(h * HEAD_DIM, (h + 1) * HEAD_DIM)
            query = q_ref[0, at]
            s1 = tn(k1[0, 0, at], query) * (score_scale * log2_e) + bias1
            s2 = tn(k2[0, 0, at], query) * (score_scale * log2_e) + bias2
            top = jnp.maximum(jnp.max(s1, axis=0, keepdims=True), jnp.max(s2, axis=0, keepdims=True))
            p1 = jnp.exp2(s1 - top)
            p2 = jnp.exp2(s2 - top)
            total = jnp.sum(p1, axis=0, keepdims=True) + jnp.sum(p2, axis=0, keepdims=True)
            context = nn(v1[0, 0, at], p1.astype(bf16)) + nn(v2[0, 0, at], p2.astype(bf16))
            ctx_ref[0, at] = (context * (1.0 / total)).astype(bf16)
            total_ref[h] = top + jnp.log2(total)

    def own(n):
        return pl.BlockSpec((1, 1, pair, tokens), lambda h, *_: (h // steps, n, h % steps, 0))

    def beside(n):
        return pl.BlockSpec((1, 1, pair, tokens), lambda h, *_: (1 - h // steps, n, h % steps, 0))

    rows_spec = pl.BlockSpec((1, pair, tokens), lambda h, *_: (h // steps, h % steps, 0))
    return call(
        body,
        (spot, lengths),
        [q, kv, kv_side, kv, kv_side],
        [rows_spec, own(0), beside(0), own(1), beside(1)],
        [shaped(q.shape, bf16), shaped((4 * steps, 1, tokens), f32)],
        [rows_spec, pl.BlockSpec((2, 1, tokens), lambda h, *_: (h, 0, 0))],
        grid=(2 * steps,),
    )


def attend_back(spot, lengths, q, kv, kv_side, grad_context, totals, deltas, number):
    _, width, tokens = q.shape
    rows = tokens // 2
    pair = 2 * HEAD_DIM
    steps = width // pair
    at_hand = number % 2

    def body(spot_ref, length_ref, q_ref, k1, k2, v1, v2, g_ref, total_ref, delta_ref, gq, own_ref, other_ref):
        bias1 = jnp.where(live_column(spot_ref, length_ref, rows, (0, 2)), 0.0, neg_fill * log2_e)
        bias2 = jnp.where(live_column(spot_ref, length_ref, rows, (1, 3)), 0.0, neg_fill * log2_e)
        for h in range(2):
            at = slice(h * HEAD_DIM, (h + 1) * HEAD_DIM)
            query = q_ref[0, at]
            grad = g_ref[0, at]
            grad_query = None
            for k, v, bias, out in ((k1, v1, bias1, own_ref), (k2, v2, bias2, other_ref)):
                s = tn(k[0, 0, at], query) * (score_scale * log2_e) + bias
                soft = jnp.exp2(s - total_ref[h])
                grad_soft = tn(v[0, 0, at], grad)
                grad_scores = (soft * (grad_soft - delta_ref[h])).astype(bf16)
                part = nn(k[0, 0, at], grad_scores)
                grad_query = part if grad_query is None else grad_query + part
                out[0, at] = (nt(query, grad_scores) * score_scale).astype(out.dtype)
                out[1, at] = nt(grad, soft.astype(bf16)).astype(out.dtype)
            gq[at] = (grad_query * score_scale).astype(bf16)

    def own(n):
        return pl.BlockSpec((1, 1, pair, tokens), lambda h, *_: (at_hand, n, h, 0))

    def beside(n):
        return pl.BlockSpec((1, 1, pair, tokens), lambda h, *_: (1 - at_hand, n, h, 0))

    rows_spec = pl.BlockSpec((1, pair, tokens), lambda h, *_: (at_hand, h, 0))
    grads_spec = pl.BlockSpec((1, pair, tokens), lambda h, *_: (number, h, 0))
    line = pl.BlockSpec((2, 1, tokens), lambda h, *_: (steps * at_hand + h, 0, 0))
    line_at = pl.BlockSpec((2, 1, tokens), lambda h, *_: (steps * number + h, 0, 0))
    both = pl.BlockSpec((2, pair, tokens), lambda h, *_: (0, h, 0))
    return call(
        body,
        (spot, lengths),
        [q, kv, kv_side, kv, kv_side, grad_context, totals, deltas],
        [rows_spec, own(0), beside(0), own(1), beside(1), grads_spec, line, line_at],
        [shaped(q.shape[1:], bf16), shaped(kv.shape[1:], f32), shaped(kv.shape[1:], bf16)],
        [pl.BlockSpec((pair, tokens), lambda h, *_: (h, 0)), both, both],
        grid=(steps,), weight=8)


cubic = 0.044715
BLOCK = 512
BIG = 20
root = math.sqrt(2.0 / math.pi)


def bend_of(widened, grad):
    square = widened * widened
    bend = jnp.tanh(root * widened * (1.0 + cubic * square))
    up = 0.5 * (1.0 + bend)
    slope = up + widened * (0.5 * root) * (1.0 - bend * bend) * (1.0 + 3.0 * cubic * square)
    return (widened * up).astype(bf16), (grad * slope).astype(bf16)


def feed_quarter(z_ref, gy_ref, wide_ref, thin_ref, pack_ref, rank, low_w, low_n, act_ref, grad_ref, sums_ref, ready=None):
    units = wide_ref.shape[1]
    low_w2, low_n2 = halves(low_w), halves(low_n)
    for start in range(0, units, BLOCK):
        at = slice(start, min(start + BLOCK, units))
        if ready is not None:
            ready(at)
        widened = nn(z_ref[...], wide_ref[:, at]) + tn(low_w2, twice(pack_ref[rank : 2 * rank, at]))
        grad = nt(gy_ref[...], thin_ref[at, :]) + tn(low_n2, twice(pack_ref[2 * rank : 3 * rank, at]))
        act_ref[:, at], grad_ref[:, at] = bend_of(widened, grad)
    sums_ref[:rank] = folded(nn(low_w2, grad_ref[...]))
    sums_ref[rank:] = folded(nn(low_n2, act_ref[...]))
    return (
        nn(act_ref[...], thin_ref[...]),
        nt(grad_ref[...], wide_ref[...]),
        nt(pack_ref[2 * rank : 3 * rank], act_ref[...]),
        nt(pack_ref[rank : 2 * rank], grad_ref[...]),
    )


def feed_units(z_ref, gy_ref, wide_ref, thin_ref, outer, inner, low_w, low_n, act_ref, grad_ref, ready):
    units = wide_ref.shape[0]
    low_w2, low_n2 = halves(low_w), halves(low_n)
    for start in range(0, units, BLOCK):
        at = slice(start, min(start + BLOCK, units))
        ready(at.stop)
        widened = nt(z_ref[...], wide_ref[at]) + tn(low_w2, twice(outer[:, at]))
        grad = nt(gy_ref[...], thin_ref[at]) + tn(low_n2, twice(inner[:, at]))
        act_ref[:, at], grad_ref[:, at] = bend_of(widened, grad)
    sums = jnp.concatenate(
        [folded(nn(low_w2, grad_ref[...])), folded(nn(low_n2, act_ref[...]))], axis=0
    )
    return (
        nn(act_ref[...], thin_ref[...]),
        nn(grad_ref[...], wide_ref[...]),
        nt(inner, act_ref[...]),
        nt(outer, grad_ref[...]),
        sums,
    )


def output_inner_rows(pack_ref, side_ref, received_ref, far_side_ref, rank, base, width):
    lanes = slice(3 * width, 4 * width)
    return [
        pack_ref[:rank, lanes],
        side_ref[:rank, lanes],
        received_ref[base : base + rank, lanes],
        far_side_ref[:rank, lanes],
    ]


def feed_open(spot, pick, lengths, contexts, outs_w, far, packs, tables, inputs, received, gain, shift):
    rows, features = inputs.shape[1:]
    tokens = 2 * rows
    width = contexts[0].shape[1]
    rank = tables[0].shape[1]
    pack, side, far_side = packs
    base = received.shape[0] - 3 * rank

    def body(spot_ref, pick_ref, length_ref, c01, c23, wo0, wo1, far_ref, pack_ref, side_ref, far_side_ref, received_ref, oo, wi, xa, gain_ref, shift_ref, hidden_ref, z_ref, lows_ref):
        states = jnp.concatenate([xa[0], received_ref[:rows]], axis=0).astype(f32)
        mask = live_column(spot_ref, length_ref, rows, (0, 2)).astype(f32)
        inner_o = output_inner_rows(pack_ref, side_ref, received_ref, far_side_ref, rank, base, width)
        contexts_all = [c01[0], c01[1], c23[0], c23[1]]
        weights_all = [wo0[...], wo1[...], far_ref[0, 0], far_ref[1, 0]]
        joined = jnp.concatenate(contexts_all, axis=0)
        attended = tn(joined, jnp.concatenate(weights_all, axis=0))
        low_o = nn(jnp.concatenate(inner_o, axis=1), joined)
        attended = attended + tn(halves(low_o), twice(oo[0]))
        hidden = states + mask * attended
        hidden_ref[...] = hidden
        z_ref[...] = normalize(hidden, gain_ref[...], shift_ref[...])[0].astype(bf16)
        lows_ref[:rank] = low_o
        lows_ref[rank:] = nt(wi[0], z_ref[...])

    operands = contexts + outs_w + [far, pack, side, far_side, received] + tables[:2]
    specs = [whole(c.shape) for c in contexts] + [whole(w.shape) for w in outs_w]
    specs += [placed_block((2, 1, width, features), lambda *_: (0, 3, 0, 0))]
    specs += [whole(p.shape) for p in packs] + [whole(received.shape)]
    specs += [placed_block((1, rank, features), of_mine(n)) for n in (3, 4)]
    operands += [inputs, gain, shift]
    specs += [placed_block((1, rows, features), lambda i, spot, *_: (spot[0], 0, 0))]
    specs += [whole(gain.shape), whole(shift.shape)]
    outs = [shaped((tokens, features), f32), shaped((tokens, features), bf16), shaped((2 * rank, tokens), f32)]
    return call(body, (spot, pick, lengths), operands, specs, outs, [KEEP] * 3)


def feed_first(spot, pick, lengths, z, lows, table, cotangent, cot_side, pack, dense):
    tokens, features = z.shape
    rows = tokens // 2
    rank = table.shape[1]
    units = dense[0].shape[1]

    def body(spot_ref, pick_ref, length_ref, z_ref, lows_in, no, ca, cb, pack_ref, wide, thin, gy_ref, branch_ref, second_ref, lows_ref, sums_ref, act_ref, grad_ref):
        mask = live_column(spot_ref, length_ref, rows, (0, 2)).astype(f32)
        grad_in = jnp.concatenate([ca[0], cb[...]], axis=0).astype(f32)
        gy_ref[...] = (mask * grad_in).astype(bf16)
        low_n = nt(no[0], gy_ref[...])
        lows_ref[: 2 * rank] = lows_in[...]
        lows_ref[2 * rank : 3 * rank] = low_n
        branch_ref[...], second_ref[...], lows_ref[3 * rank : 4 * rank], lows_ref[4 * rank :] = feed_quarter(
            z_ref, gy_ref, wide, thin, pack_ref, rank, lows_in[rank:], low_n, act_ref, grad_ref, sums_ref
        )

    operands = [z, lows, table, cotangent, cot_side, pack] + dense
    specs = [KEEP, KEEP, placed_block((1, rank, features), of_mine(5))]
    specs += [placed_block((1, rows, features), lambda i, spot, *_: (spot[0], 0, 0))] + [KEEP] * 4
    outs = [
        shaped((tokens, features), bf16),
        shaped((tokens, features), f32),
        shaped((tokens, features), f32),
        shaped((5 * rank, tokens), f32),
        shaped((2 * rank, units), f32),
    ]
    scratch = [pltpu.VMEM((tokens, units), bf16)] * 2
    return call(body, (spot, pick, lengths), operands, specs, outs, [KEEP] * 5, scratch=scratch, limit=BIG)


def feed_near(z, gy, branch, second, lows, pack, dense):
    tokens, features = z.shape
    units = dense[0].shape[1]
    rank = lows.shape[0] // 5
    blocks = [slice(n, min(n + BLOCK, units)) for n in range(0, units, BLOCK)]

    def body(z_ref, gy_ref, branch_in, second_in, lows_in, pack_ref, wide_hbm, thin_hbm, branch_ref, second_ref, lows_ref, sums_ref, wide, thin, act_ref, grad_ref, sems):
        copies = {}
        for n, at in enumerate(blocks):
            copies[at.start] = (
                pltpu.make_async_copy(wide_hbm.at[:, at], wide.at[:, at], sems.at[0, n]),
                pltpu.make_async_copy(thin_hbm.at[at], thin.at[at], sems.at[1, n]),
            )
            for c in copies[at.start]:
                c.start()

        def ready(at):
            for c in copies[at.start]:
                c.wait()

        sums = feed_quarter(
            z_ref, gy_ref, wide, thin, pack_ref, rank, lows_in[rank : 2 * rank], lows_in[2 * rank : 3 * rank],
            act_ref, grad_ref, sums_ref, ready,
        )
        branch_ref[...] = branch_in[...] + sums[0]
        second_ref[...] = second_in[...] + sums[1]
        lows_ref[: 3 * rank] = lows_in[: 3 * rank]
        lows_ref[3 * rank : 4 * rank] = lows_in[3 * rank : 4 * rank] + sums[2]
        lows_ref[4 * rank :] = lows_in[4 * rank :] + sums[3]

    operands = [z, gy, branch, second, lows, pack] + dense
    outs = [shaped(branch.shape, f32), shaped(second.shape, f32), shaped(lows.shape, f32), shaped((2 * rank, units), f32)]
    scratch = [pltpu.VMEM(d.shape, bf16) for d in dense] + [pltpu.VMEM((tokens, units), bf16)] * 2
    scratch += [pltpu.SemaphoreType.DMA((2, len(blocks)))]
    return call(
        body, (), operands, [KEEP] * 6 + [in_hbm] * 2, outs, [KEEP] * 4, scratch=scratch, aliases={2: 0, 3: 1}, limit=BIG
    )


def far_copies(ins, wide, thin, sems):
    part = ins[0].shape[0]
    copies = []
    for n in range(len(ins) // 4):
        for q in range(2):
            k = 2 * n + q
            at = slice(k * part, (k + 1) * part)
            copies.append(pltpu.make_async_copy(ins[4 * n + q], wide.at[at], sems.at[2 * k]))
            copies.append(pltpu.make_async_copy(ins[4 * n + 2 + q], thin.at[at], sems.at[2 * k + 1]))
    for c in copies:
        c.start()
    return copies


def far_parts(parts, z_ref, gy_ref, copies, wide, thin, received_ref, far_side_ref, rank, base, low_w, low_n, act_ref, grad_ref, sums_ref):
    count = wide.shape[0] // (2 * len(parts))
    outer, inner = [], []
    for r in parts:
        lanes = slice(r * count, (r + 1) * count)
        outer += [received_ref[base + rank : base + 2 * rank, lanes], far_side_ref[rank : 2 * rank, lanes]]
        inner += [received_ref[base + 2 * rank : base + 3 * rank, lanes], far_side_ref[2 * rank : 3 * rank, lanes]]
    arrived = []

    def ready(end):
        while len(arrived) * count < min(end, wide.shape[0]):
            n = len(arrived)
            copies[2 * n].wait()
            copies[2 * n + 1].wait()
            arrived.append(n)

    *total, sums = feed_units(
        z_ref, gy_ref, wide, thin, jnp.concatenate(outer, axis=1), jnp.concatenate(inner, axis=1), low_w, low_n,
        act_ref, grad_ref, ready,
    )
    sums_ref[...] = sums
    return total


def far_scratch(parts, part, features, tokens):
    units = 2 * len(parts) * part
    return [pltpu.VMEM((units, features), bf16)] * 2 + [pltpu.VMEM((tokens, units), bf16)] * 2 + [
        pltpu.SemaphoreType.DMA((4 * len(parts),))
    ]


def feed_far(parts, z, gy, branch, second, lows, received, far_side, weights):
    tokens, features = z.shape
    part = weights[0].shape[0]
    rank = lows.shape[0] // 5
    base = received.shape[0] - 3 * rank
    count = len(weights)

    def body(z_ref, gy_ref, branch_in, second_in, lows_in, received_ref, far_side_ref, *refs):
        ins, (branch_ref, second_ref, lows_ref, sums_ref) = refs[:count], refs[count : count + 4]
        wide, thin, act_ref, grad_ref, sems = refs[count + 4 :]
        copies = far_copies(ins, wide, thin, sems)
        total = far_parts(
            parts, z_ref, gy_ref, copies, wide, thin, received_ref, far_side_ref, rank, base,
            lows_in[rank : 2 * rank], lows_in[2 * rank : 3 * rank], act_ref, grad_ref, sums_ref,
        )
        branch_ref[...] = branch_in[...] + total[0]
        second_ref[...] = second_in[...] + total[1]
        lows_ref[: 3 * rank] = lows_in[: 3 * rank]
        lows_ref[3 * rank : 4 * rank] = lows_in[3 * rank : 4 * rank] + total[2]
        lows_ref[4 * rank :] = lows_in[4 * rank :] + total[3]

    operands = [z, gy, branch, second, lows, received, far_side] + weights
    outs = [
        shaped(branch.shape, f32),
        shaped(second.shape, f32),
        shaped(lows.shape, f32),
        shaped((2 * rank, 2 * len(parts) * part), f32),
    ]
    return call(
        body, (), operands, [KEEP] * 7 + [in_hbm] * count, outs, [KEEP] * 4,
        scratch=far_scratch(parts, part, features, tokens), aliases={2: 0, 3: 1}, limit=BIG,
    )


def shares(array, core):
    half = array.shape[1] // 2
    low, high = array[:, :half], array[:, half:]
    return jnp.where(core == 0, low, high), jnp.where(core == 0, high, low)


def padded(array, count):
    return jnp.concatenate([array, jnp.zeros((array.shape[0], count - array.shape[1]), array.dtype)], axis=1)


def lanes_up(count):
    return (count + 127) // 128 * 128


def feed_close(parts, spot, pick, lengths, hidden, z, gy, branch, second, lows, near_sums, far_sums, contexts, outs_w, far, packs, tables, received, cotangent, cot_side, gain, weights):
    tokens, features = hidden.shape
    rows = tokens // 2
    width = contexts[0].shape[1]
    rank = tables[0].shape[1]
    pack, side, far_side = packs
    base = received.shape[0] - 3 * rank
    part = weights[0].shape[0]
    units = 4 * part
    heads = width // HEAD_DIM
    half = features // 2
    tail = lanes_up(width)
    total_lanes = 3 * half + 2 * (2 * units + tail)

    def body(spot_ref, pick_ref, length_ref, hidden_ref, z_ref, gy_ref, branch_in, second_in, lows_ref, near0, near1, far0, far3, c01, c23, wo0, wo1, far_ref, pack_ref, side_ref, far_side_ref, received_ref, oo, wi, no, ca, cb, gain_ref, *refs):
        hbm, (out_ref, outb_ref, gh_ref, gc_ref, delta_ref, keep_ref, give_ref) = refs[:8], refs[8:15]
        wide, thin, act_ref, grad_ref, sems, last, ga_ref = refs[15:]
        copies = far_copies(hbm, wide, thin, sems)
        low_w = lows_ref[rank : 2 * rank]
        low_n = lows_ref[2 * rank : 3 * rank]
        found = far_parts(
            parts, z_ref, gy_ref, copies, wide, thin, received_ref, far_side_ref, rank, base,
            low_w, low_n, act_ref, grad_ref, last,
        )
        branch = branch_in[...] + found[0]
        grad_second = second_in[...] + found[1]
        low_next = lows_ref[3 * rank : 4 * rank] + found[2]
        grad_low = lows_ref[4 * rank :] + found[3]
        mask = live_column(spot_ref, length_ref, rows, (0, 2)).astype(f32)
        branch = branch + tn(halves(low_next), twice(no[0]))
        grad_second = grad_second + tn(halves(grad_low), twice(wi[0]))
        hidden_now = hidden_ref[...]
        output = (hidden_now + mask * branch).astype(bf16)
        out_ref[0] = output[:rows]
        outb_ref[...] = output[rows:]
        _, unit, scaled = normalize(hidden_now, gain_ref[...], gain_ref[...])
        grad_in = jnp.concatenate([ca[0], cb[...]], axis=0).astype(f32)
        grad_hidden = grad_in + normalize_back(grad_second, unit, scaled, gain_ref[...])
        gh_ref[...] = grad_hidden
        ga_ref[...] = (mask * grad_hidden).astype(bf16)
        grad_low_o = nt(oo[0], ga_ref[...])
        low_o2 = halves(grad_low_o)
        inner_o = output_inner_rows(pack_ref, side_ref, received_ref, far_side_ref, rank, base, width)
        contexts_all = [c01[0], c01[1], c23[0], c23[1]]
        weights_all = [wo0, wo1, far_ref.at[0, 0], far_ref.at[1, 0]]
        inner_sums = []
        for i in range(4):
            grad = (nt(weights_all[i][...], ga_ref[...]) + tn(twice(inner_o[i]), low_o2)).astype(bf16)
            gc_ref[i] = grad
            product = grad.astype(f32) * contexts_all[i].astype(f32)
            for h in range(heads):
                delta_ref[heads * i + h] = jnp.sum(
                    product[h * HEAD_DIM : (h + 1) * HEAD_DIM], axis=0, keepdims=True
                )
            inner_sums.append(folded(nt(low_o2, contexts_all[i])))
        core = spot_ref[3] & 1
        quad = spot_ref[2]
        shared = (
            folded(nn(halves(grad_low), z_ref[...])),
            folded(nn(halves(lows_ref[:rank]), ga_ref[...])),
            folded(nn(halves(low_next), gy_ref[...])),
        )
        for n in range(3):
            keep_ref[:, n * half : (n + 1) * half], give_ref[:, n * half : (n + 1) * half] = shares(shared[n], core)
        quarters = []
        for near in (near0, near1):
            quarters.append((near[:rank], near[rank:]))
        for q in range(2):
            lanes = slice(q * part, (q + 1) * part)
            later = slice((2 + q) * part, (3 + q) * part)
            pieces = [far0[:, lanes], last[:, lanes], last[:, later], far3[:, lanes]]
            joined = shuffled(jnp.concatenate(pieces, axis=1), quad)
            quarters.append((joined[:rank], joined[rank:]))
        for i in range(4):
            ref = (keep_ref, give_ref)[i % 2]
            at = 3 * half + (i // 2) * (2 * units + tail)
            ref[:, at : at + units] = quarters[i][0]
            ref[:, at + units : at + 2 * units] = quarters[i][1]
            ref[:, at + 2 * units : at + 2 * units + tail] = padded(inner_sums[i], tail)

    operands = [hidden, z, gy, branch, second, lows] + near_sums + far_sums + contexts + outs_w
    specs = [whole(hidden.shape), KEEP, KEEP, KEEP, KEEP] + [whole(o.shape) for o in operands[5:]]
    operands += [far, pack, side, far_side, received] + tables
    specs += [placed_block((2, 1, width, features), lambda *_: (0, 3, 0, 0))]
    specs += [whole(p.shape) for p in packs] + [whole(received.shape)]
    specs += [placed_block((1, rank, features), of_mine(n)) for n in (3, 4, 5)]
    operands += [cotangent, cot_side, gain] + weights
    specs += [placed_block((1, rows, features), lambda i, spot, *_: (spot[0], 0, 0))]
    specs += [whole(cot_side.shape), whole(gain.shape)] + [remain] * 8
    outs = [
        shaped((2, rows, features), bf16),
        shaped((rows, features), bf16),
        shaped((tokens, features), f32),
        shaped((4, width, tokens), bf16),
        shaped((4 * heads, 1, tokens), f32),
        shaped((rank, total_lanes), f32),
        shaped((rank, total_lanes), f32),
    ]
    scratch = far_scratch(parts, part, features, tokens)
    scratch += [pltpu.VMEM((2 * rank, 4 * part), f32), pltpu.VMEM((tokens, features), bf16)]
    out_specs = [placed_block((1, rows, features), lambda i, spot, *_: (spot[0], 0, 0))] + [KEEP] * 6
    return call(body, (spot, pick, lengths), operands, specs, outs, out_specs, scratch=scratch, limit=BIG)


def gather_pair(quarters, low, factors, before=None):
    rank = low.shape[0] // 3
    width, tokens = quarters[0][0].shape
    tail = lanes_up(3 * width)
    extra = 0 if before is None else 1

    def body(*refs):
        groups = [refs[3 * i : 3 * i + 3] for i in range(2)]
        low_ref, *places = refs[6:9]
        g_ref, gl_ref, keep_ref, give_ref = refs[9 + extra :]
        lows = [halves(low_ref[n * rank : (n + 1) * rank]) for n in range(3)]
        for n in range(3):
            at = slice(n * rank, (n + 1) * rank)
            total = jnp.zeros((rank, tokens), f32) if before is None else refs[9][at]
            for i in range(2):
                q, own, other = groups[i][0], groups[i][1], groups[1 - i][2]
                if n == 0:
                    g = q[...]
                else:
                    g = (own[n - 1] + other[n - 1].astype(f32)).astype(bf16)
                g_ref[i, n] = g
                total = total + nn(places[i][:rank, n * width : (n + 1) * width], g)
                (keep_ref, give_ref)[i][:, n * width : (n + 1) * width] = folded(nt(lows[n], g))
            gl_ref[at] = total
        for ref in (keep_ref, give_ref):
            ref[:, 3 * width :] = jnp.zeros((rank, tail - 3 * width), f32)

    operands = [a for q in quarters for a in q] + [low] + list(factors) + ([] if before is None else [before])
    outs = [
        shaped((2, 3, width, tokens), bf16),
        shaped((3 * rank, tokens), f32),
        shaped((rank, tail), f32),
        shaped((rank, tail), f32),
    ]
    return call(body, (), operands, [KEEP] * len(operands), outs, [KEEP] * 4, weight=3)


def gather_inner(spot, gl, z, first, second):
    features = z.shape[1]
    rank = gl.shape[0] // 3
    half = features // 2
    tail = first[0].shape[1]

    def body(spot_ref, gl_ref, z_ref, a0, b0, a1, b1, keep_ref, give_ref):
        core = spot_ref[3] & 1
        for n in range(3):
            inner = folded(nn(halves(gl_ref[n * rank : (n + 1) * rank]), z_ref[...]))
            keep_ref[:, n * half : (n + 1) * half], give_ref[:, n * half : (n + 1) * half] = shares(inner, core)
        for ref, pieces in ((keep_ref, (a0, a1)), (give_ref, (b0, b1))):
            for i in range(2):
                ref[:, 3 * half + i * tail : 3 * half + (i + 1) * tail] = pieces[i][...]

    out = shaped((rank, 3 * half + 2 * tail), f32)
    operands = [gl, z] + list(first) + list(second)
    return call(body, (spot,), operands, [KEEP] * 6, [out, out], [KEEP] * 2, weight=2)


def settle(spot, pick, keep, moved, common, with_picks):
    rank, lanes = keep.shape
    own = (lanes - common) // 2
    extra = 128 if with_picks else 0

    def body(spot_ref, pick_ref, keep_ref, moved_ref, here_ref, there_ref):
        total = (keep_ref[...] + moved_ref[...]).astype(bf16)
        here_ref[:, : common + own] = total[:, : common + own]
        there_ref[:, :common] = total[:, :common]
        there_ref[:, common : common + own] = total[:, common + own :]
        if with_picks:
            iota = lax.broadcasted_iota(jnp.int32, (rank, 128), 1)
            line = jnp.zeros((rank, 128), f32)
            for n in range(6):
                line = jnp.where(iota == n, pick_ref[spot_ref[0], n].astype(f32), line)
            here_ref[:, common + own :] = line.astype(bf16)
            there_ref[:, common + own :] = line.astype(bf16)

    out = shaped((rank, common + own + extra), bf16)
    return call(body, (spot, pick), [keep, moved], [whole(keep.shape)] * 2, [out, out], [whole(out.shape)] * 2, weight=1)


def combine(spot, picks, arrays, groups, rows_of_table):
    per, rank = arrays[0].shape[:2]
    half = groups[0][1]

    def body(spot_ref, pick_ref, *refs):
        ins, outs = refs[: len(arrays)], refs[len(arrays) :]
        places = [outs[0].at[n] for n in range(3)] + list(outs[4:])
        for out in places:
            out[...] = jnp.zeros(out.shape, f32)
        for a, ref in enumerate(ins):
            for c in range(per):
                for (start, count, number), out in zip(groups, places):
                    row = pick_ref[a * per + c, number]
                    out[row] += ref[c, :, start : start + count].astype(f32)
        for n in range(3):
            outs[1 + n][...] = outs[0][n]

    outs = [shaped((3, rows_of_table, rank, half), f32)] + [shaped((rows_of_table, rank, 2 * half), f32)] * 3
    outs += [shaped((rows_of_table, rank, count), f32) for _, count, _ in groups[3:]]
    own = placed_block((rows_of_table, rank, half), lambda i, spot, pick: (0, 0, spot[3] & 1))
    specs = [KEEP] + [own] * 3 + [KEEP] * (len(groups) - 3)
    return call(body, (spot, picks), list(arrays), [KEEP] * len(arrays), outs, specs, weight=100)


def complete(spot, tables, moved):
    _, count, rank, half = moved.shape

    def body(spot_ref, moved_ref, *refs):
        for n in range(3):
            refs[3 + n][...] = moved_ref[n]

    out = shaped((count, rank, 2 * half), f32)
    theirs = placed_block((count, rank, half), lambda i, spot: (0, 0, 1 - (spot[3] & 1)))
    return call(
        body, (spot,), [moved] + list(tables), [KEEP] + [remain] * 3, [out] * 3, [theirs] * 3,
        aliases={2: 0, 3: 1, 4: 2}, weight=2)


def pair_up(spot, array, second):
    rows, features = second.shape

    def body(spot_ref, array_ref, second_ref, out_ref):
        out_ref[0] = second_ref[...].astype(array.dtype)

    out_spec = placed_block((1, rows, features), lambda i, spot: (spot[1], 0, 0))
    return call(
        body, (spot,), [array, second], [remain, KEEP], shaped(array.shape, array.dtype), out_spec, aliases={1: 0}, weight=1)


def join(groups):
    flat = [a for g in groups for a in g]
    outs = [shaped((sum(a.shape[0] for a in g),) + g[0].shape[1:], g[0].dtype) for g in groups]

    def body(*refs):
        at = 0
        for g, out in zip(groups, refs[len(flat) :]):
            start = 0
            for a in g:
                out[start : start + a.shape[0]] = refs[at][...]
                start += a.shape[0]
                at += 1

    return call(body, (), flat, [KEEP] * len(flat), outs, [KEEP] * len(outs), weight=1)


def finish(spot, pick, g01, g23, gl, inners, weights, far, states, grad_hidden, gain, block):
    features = gain.shape[1]
    rows = g01.shape[3] // 2
    width = g01.shape[2]
    rank = gl.shape[0] // 3
    at = slice(block * rows, (block + 1) * rows)

    def body(spot_ref, pick_ref, g01_ref, g23_ref, gl_ref, iq, ik, iv, *refs):
        ws, (far_ref, x_ref, gh_ref, gain_ref, grad_ref) = refs[:6], refs[6:]
        low = [halves(gl_ref[n * rank : (n + 1) * rank, at]) for n in range(3)]
        total = tn(
            jnp.concatenate(low, axis=0),
            jnp.concatenate([twice(iq[0]), twice(ik[0]), twice(iv[0])], axis=0),
        )
        for i in range(4):
            if i < 2:
                weight = jnp.concatenate([w[...] for w in ws[3 * i : 3 * i + 3]], axis=0)
            else:
                weight = far_ref[i - 2].reshape(3 * width, features)
            g_ref = (g01_ref, g23_ref)[i // 2]
            total = total + tn(g_ref[i % 2, :, :, at].reshape(3 * width, rows), weight)
        x = x_ref[0] if block == 0 else x_ref[...]
        _, unit, scaled = normalize(x.astype(f32), gain_ref[...], gain_ref[...])
        grad = gh_ref[at] + normalize_back(total, unit, scaled, gain_ref[...])
        if block == 0:
            grad_ref[0] = grad
        else:
            grad_ref[...] = grad.astype(bf16)

    operands = [g01, g23, gl] + inners + weights + [far, states, grad_hidden, gain]
    specs = [KEEP] * 3
    specs += [placed_block((1, rank, features), of_mine(n)) for n in range(3)]
    specs += [KEEP] * 6
    specs += [placed_block((2, 3, width, features), lambda *_: (0, 0, 0, 0))]
    if block == 0:
        specs += [placed_block((1, rows, features), lambda i, spot, *_: (spot[0], 0, 0))]
        out, out_spec = shaped((2, rows, features), f32), placed_block((1, rows, features), lambda i, spot, *_: (spot[0], 0, 0))
    else:
        specs += [placed_block((rows, features), lambda *_: (0, 0))]
        out, out_spec = shaped((rows, features), bf16), KEEP
    specs += [KEEP] * 2
    return call(body, (spot, pick), operands, specs, out, out_spec, weight=5)


def make_body(dp_size, tensor_size):
    def across(array):
        return swap(array, "tensor", 2, tensor_size)

    def beside(array):
        return swap(array, "tensor", 1, tensor_size)

    def along(array, bits):
        return swap(array, "dp", bits, dp_size)

    def body(
        inputs,
        cotangent,
        lengths,
        adapter_pick,
        first_gain,
        first_bias,
        query_weight,
        key_weight,
        value_weight,
        output_weight,
        second_gain,
        second_bias,
        widen_weight,
        narrow_weight,
        query_inner,
        query_outer,
        key_inner,
        key_outer,
        value_inner,
        value_outer,
        output_inner,
        output_outer,
        widen_inner,
        widen_outer,
        narrow_inner,
        narrow_outer,
    ):
        rows, features = inputs.shape[1:]
        place = lax.axis_index("tensor")
        quad = lax.axis_index("dp") & 3
        mine = place >> 1
        spot = jnp.stack([mine, 1 - mine, quad, place]).astype(jnp.int32)
        pick = adapter_pick

        def flip(array):
            return jnp.swapaxes(array, 1, 2)

        small = [query_outer, key_outer, value_outer, flip(output_inner), widen_outer, flip(narrow_inner)]
        inners = [flip(query_inner), flip(key_inner), flip(value_inner)]
        tables = [output_outer, flip(widen_inner), narrow_outer]
        gains = [v.reshape(1, -1) for v in (first_gain, first_bias, second_gain, second_bias)]
        heads = [query_weight.T, key_weight.T, value_weight.T, output_weight]
        dense = [widen_weight, narrow_weight]
        width = query_outer.shape[2]
        half = features // 2

        head_rows = heads[0].shape[0] // 4
        together = jnp.stack([w.reshape(4, head_rows, features) for w in heads], axis=1)
        part_heads = lax.dynamic_index_in_dim(together, quad, 0, keepdims=False)
        far0 = across(part_heads)
        send, pack = stage(after(spot, part_heads), pick, inputs, small)
        near_heads = [beside(w) for w in after(heads, part_heads)]
        received = across(after(send, near_heads[:2]))
        side = beside(pack)
        near_dense = [beside(after(dense[0], near_heads))]
        near_dense.append(beside(after(dense[1], near_dense[0])))
        part_wide, part_thin, part_last, cot_send = stage_dense(
            after(spot, pack), widen_weight, narrow_weight, cotangent
        )
        far1, far2 = along(far0, 1), along(far0, 2)
        wide0 = across(after(part_wide, far0))
        z, low, kv01 = project_near(
            spot, pick, inputs, after(received, part_wide, side, far0, near_dense), gains[0], gains[1], inners, pack,
            side, [heads[1], heads[2], near_heads[1], near_heads[2]],
        )
        kv01_side = beside(kv01)
        q01 = queries_near(after(z, kv01), low, pack, side, [heads[0], near_heads[0]])
        side0 = beside(after(far0, kv01))
        side1 = beside(after(far1, kv01, side0))
        far3, far4 = along(after(far2[:2], q01), 1), along(after(far1[2:], q01), 2)
        c01, total01 = attend(spot, lengths, q01, kv01, after(kv01_side, side1))
        side2 = beside(after(far2, c01, side1))
        far_side = beside(after(received[rows:], c01))
        side3, side4 = beside(after(far3, c01)), beside(after(far4, c01))
        wide1, wide2 = along(after(wide0, c01), 1), along(after(wide0, c01), 2)
        cot_side = across(after(cot_send, c01))
        far, kv23, q23 = project_far(
            spot, after(z, c01, wide0), low, received, far_side,
            [[far0, far1, far2, far3, far4], [side0, side1, side2, side3, side4]],
        )
        kv23_side = beside(kv23)
        thin0 = across(after(part_thin, kv23))
        c23, total23 = attend(spot, lengths, q23, kv23, kv23_side)
        packs = [pack, side, far_side]
        outs_w = [heads[3], near_heads[3]]
        hidden, z2, lows = feed_open(
            spot, pick, lengths, [c01, c23], outs_w, far, packs, tables, inputs, received, gains[2], gains[3]
        )
        wide3 = along(after(wide2, lows), 1)
        thin3 = across(after(part_last, lows))
        wide_sides = [beside(after(w, lows)) for w in (wide0, wide1, wide2)]
        gy, branch, second, lows, sums0 = feed_first(
            spot, pick, lengths, z2, lows, tables[2], cotangent, cot_side, pack, dense
        )
        thin1, thin2 = along(after(thin0, lows), 1), along(after(thin0, lows), 2)
        thin_sides = [beside(after(thin0, lows))]
        branch, second, lows, sums1 = feed_near(
            z2, gy, branch, second, after(lows, wide_sides), side, near_dense
        )
        wide_sides.append(beside(after(wide3, sums1)))
        branch, second, lows, sums2 = feed_far(
            (0,), z2, gy, branch, second, lows, received, far_side, [wide0, wide_sides[0], thin0, thin_sides[0]]
        )
        thin_sides += [beside(after(t, sums2)) for t in (thin1, thin2, thin3)]
        branch, second, lows, sums3 = feed_far(
            (3,), z2, gy, branch, second, lows, received, far_side, [wide3, wide_sides[3], thin3, thin_sides[3]]
        )
        output, outb, grad_hidden, grad_context, deltas, keep, give = feed_close(
            (1, 2), spot, pick, lengths, hidden, z2, gy, branch, second, lows, [sums0, sums1], [sums2, sums3],
            [c01, c23], outs_w, far, packs, tables, received, cotangent, cot_side, gains[2],
            [wide1, wide_sides[1], thin1, thin_sides[1], wide2, wide_sides[2], thin2, thin_sides[2]],
        )

        def first_turn(here, other, crossed):
            one, two = join([[here[None], crossed[0][None]], [other[None], crossed[1][None]]])
            return [(one, along(one, 1)), (two, along(two, 2))]

        def second_turn(turns):
            one, two = join(turns)
            return [one, along(one, 2), two, along(two, 1)]

        def whole_sum(table):
            bits = 8
            while bits < dp_size:
                table = table + along(table, bits)
                bits *= 2
            return table

        def back(number, q, kv, kv_side, totals):
            gq, own, other = attend_back(spot, lengths, q, kv, kv_side, grad_context, totals, deltas, number)
            return gq, own, other

        moved = beside(give)
        here, there = settle(spot, pick, keep, moved, 3 * half, True)
        other = across(there)
        out_side = across(outb)
        crossed = [along(here, 4)]
        quarters = [back(0, after(q01, here), kv01, kv01_side, total01)]
        quarters.append(back(1, after(q01, quarters[0][0]), kv01, kv01_side, total01))
        sides = [beside(after(quarters[0][2], quarters[1][0]))]
        crossed.append(along(after(other, quarters[1][0]), 4))
        quarters.append(back(2, after(q23, quarters[1][0], out_side), kv23, kv23_side, total23))
        sides.append(beside(after(quarters[1][2], quarters[2][0], sides[0])))
        turns = first_turn(here, other, after(crossed, quarters[2][0]))
        quarters.append(back(3, after(q23, quarters[2][0], turns[0][0]), kv23, kv23_side, total23))
        pieces = [(gq, own, sided) for (gq, own, _), sided in zip(quarters, sides)]
        g01, gl, *first = gather_pair(
            [pieces[0], (after(pieces[1][0], quarters[3][0]),) + pieces[1][1:]], after(low, turns), [pack, side]
        )
        early = second_turn(after(turns, g01))
        sides += [beside(after(q[2], g01)) for q in quarters[2:]]
        pieces += [(gq, own, sided) for (gq, own, _), sided in zip(quarters[2:], sides[2:])]
        far_factors = [received[rows:], far_side]
        g23, gl, *second = gather_pair(pieces[2:], low, far_factors, gl)
        keep, give = gather_inner(spot, gl, z, first, second)
        moved = beside(give)
        here, there = settle(spot, pick, keep, moved, 3 * half, False)
        other = across(there)
        crossed = [along(here, 4)]
        crossed.append(along(other, 4))
        ends = (gl, inners, heads[:3] + near_heads[:3], far)
        gradb = finish(spot, pick, g01, after(g23, other), *ends, received, grad_hidden, gains[0], 1)
        grad_side = across(gradb)
        grad = finish(spot, pick, g01, after(g23, gradb, crossed), *ends, inputs, grad_hidden, gains[0], 0)
        turns = first_turn(here, other, after(crossed, gradb))
        output = pair_up(spot, output, after(out_side, grad))
        early = after(early, gradb, turns[0][0])
        picks = jnp.concatenate([a[:, 0, -128:-122] for a in early]).astype(jnp.int32)
        adapters = query_inner.shape[0]
        units = widen_weight.shape[1]
        base = 3 * half
        early = combine(
            spot,
            after(picks, gradb),
            early,
            [
                (0, half, 4),
                (half, half, 3),
                (2 * half, half, 5),
                (base, units, 4),
                (base + units, units, 5),
                (base + 2 * units, width, 3),
            ],
            adapters,
        )
        early = [whole_sum(t) for t in early]
        early_shared = complete(spot, early[1:4], beside(early[0]))
        late = second_turn(turns)
        input_grad = pair_up(spot, grad, grad_side)
        late = combine(
            spot,
            after(picks, grad_side, output),
            late,
            [(n * half, half, n) for n in range(3)] + [(base + n * width, width, n) for n in range(3)],
            adapters,
        )
        late = [whole_sum(t) for t in late]
        late_shared = complete(spot, late[1:4], beside(late[0]))
        return (
            output,
            input_grad,
            flip(late_shared[0]),
            late[4],
            flip(late_shared[1]),
            late[5],
            flip(late_shared[2]),
            late[6],
            flip(early[6]),
            early_shared[1],
            flip(early_shared[0]),
            early[4],
            flip(early[5]),
            early_shared[2],
        )

    return body


def solution(mesh):
    placed = (
        P("dp", "tensor", None),
        P("dp", "tensor", None),
        P("dp"),
        P("dp", None),
        P(),
        P(),
        P(None, "tensor"),
        P(None, "tensor"),
        P(None, "tensor"),
        P("tensor", None),
        P(),
        P(),
        P(None, "tensor"),
        P("tensor", None),
        P(),
        P(None, None, "tensor"),
        P(),
        P(None, None, "tensor"),
        P(),
        P(None, None, "tensor"),
        P(None, "tensor", None),
        P(),
        P(),
        P(None, None, "tensor"),
        P(None, "tensor", None),
        P(),
    )
    return jax.shard_map(
        make_body(mesh.shape["dp"], mesh.shape["tensor"]),
        mesh=mesh,
        in_specs=placed,
        out_specs=(
            P("dp", "tensor", None),
            P("dp", "tensor", None),
            P(),
            P(None, None, "tensor"),
            P(),
            P(None, None, "tensor"),
            P(),
            P(None, None, "tensor"),
            P(None, "tensor", None),
            P(),
            P(),
            P(None, None, "tensor"),
            P(None, "tensor", None),
            P(),
        ),
        check_vma=False,
    )
```

```python
import functools
import math

import jax
import jax.numpy as jnp
from jax import lax
from jax.experimental import pallas as pl
from jax.experimental.pallas import tpu as pltpu
from jax.sharding import PartitionSpec as P

HEAD_DIM = 80
f32 = jnp.float32
bf16 = jnp.bfloat16
neg_fill = -1000000000.0
score_scale = 1.0 / math.sqrt(HEAD_DIM)
log2_e = math.log2(math.e)
LIMIT = 16
KEEP = pl.BlockSpec(memory_space=pltpu.VMEM)
remain = pl.BlockSpec(memory_space=pl.ANY)
in_hbm = pl.BlockSpec(memory_space=pltpu.HBM)


def swap(array, axis, bits, size):
    return lax.ppermute(array, axis, [(i, i ^ bits) for i in range(size)])


def nn(a, b):
    return jnp.dot(a, b, preferred_element_type=f32)


def nt(a, b):
    return lax.dot_general(a, b, (((1,), (1,)), ((), ())), preferred_element_type=f32)


def tn(a, b):
    return lax.dot_general(a, b, (((0,), (0,)), ((), ())), preferred_element_type=f32)


def halves(low):
    top = low.astype(bf16)
    return jnp.concatenate([top, (low - top.astype(f32)).astype(bf16)], axis=0)


def twice(factor):
    return jnp.concatenate([factor, factor], axis=0)


def folded(pair):
    count = pair.shape[0] // 2
    return pair[:count] + pair[count:]


def normalize(states, gain, shift):
    centre = states - jnp.mean(states, axis=-1, keepdims=True)
    scaled = lax.rsqrt(jnp.mean(centre * centre, axis=-1, keepdims=True) + 1e-05)
    unit = centre * scaled
    return unit * gain + shift, unit, scaled


def normalize_back(grad_rows, unit, scaled, gain):
    grad_unit = grad_rows * gain
    return scaled * (
        grad_unit
        - jnp.mean(grad_unit, axis=-1, keepdims=True)
        - unit * jnp.mean(grad_unit * unit, axis=-1, keepdims=True)
    )


def live_column(spot_ref, length_ref, rows, bits):
    iota = lax.broadcasted_iota(jnp.int32, (2 * rows, 1), 0)
    place = spot_ref[3]
    first, second = place ^ bits[0], place ^ bits[1]
    position = jnp.where(iota < rows, first * rows + iota, second * rows + iota - rows)
    return position < length_ref[spot_ref[0]]


def whole(shape):
    return KEEP


def placed_block(shape, index):
    return pl.BlockSpec(shape, index, pipeline_mode=pl.Buffered(1))


def call(body, scalars, operands, specs, outs, out_specs, grid=(1,), scratch=(), limit=LIMIT, aliases=None, weight=100):
    return pl.pallas_call(
        body,
        grid_spec=pltpu.PrefetchScalarGridSpec(
            num_scalar_prefetch=len(scalars),
            grid=grid,
            in_specs=specs,
            out_specs=out_specs,
            scratch_shapes=list(scratch),
        ),
        out_shape=outs,
        cost_estimate=pl.CostEstimate(flops=weight * 10**9, bytes_accessed=100000, transcendentals=0),
        input_output_aliases=aliases or {},
        compiler_params=pltpu.CompilerParams(vmem_limit_bytes=limit * 2**20),
    )(*scalars, *operands)


def shaped(shape, dtype):
    return jax.ShapeDtypeStruct(shape, dtype)


def of_mine(number):
    return lambda i, spot, pick, *_: (pick[spot[0], number], 0, 0)


def of_other(number):
    return lambda i, spot, pick, *_: (pick[spot[1], number], 0, 0)


def after(values, *others):
    return lax.optimization_barrier((values, others))[0]


def shuffled(array, quad):
    count = array.shape[1] // 4
    blocks = [array[:, n * count : (n + 1) * count] for n in range(4)]
    for bits in (1, 2):
        on = ((quad >> (bits - 1)) & 1) == 1
        blocks = [jnp.where(on, blocks[n ^ bits], blocks[n]) for n in range(4)]
    return jnp.concatenate(blocks, axis=1)


def stage(spot, pick, inputs, factors):
    rows, features = inputs.shape[1:]
    rank = factors[0].shape[1]

    def body(spot_ref, pick_ref, inputs_ref, *refs):
        send_ref, pack_ref = refs[12:]
        send_ref[:rows] = inputs_ref[0]
        quad = spot_ref[2]
        for group, ref, base in ((refs[:6], pack_ref, 0), (refs[6:12], send_ref, rows)):
            ref[base : base + rank] = jnp.concatenate([r[0] for r in group[:4]], axis=1)
            wide, thin = group[4][0], group[5][0]
            if base:
                wide, thin = shuffled(wide, quad), shuffled(thin, quad)
            ref[base + rank : base + 2 * rank] = wide
            ref[base + 2 * rank : base + 3 * rank] = thin

    specs = [placed_block((1, rows, features), lambda i, spot, *_: (spot[1], 0, 0))]
    for of in (of_mine, of_other):
        specs += [placed_block((1,) + f.shape[1:], of(n)) for n, f in enumerate(factors)]
    outs = [shaped((rows + 3 * rank, features), bf16), shaped((3 * rank, features), bf16)]
    return call(body, (spot, pick), [inputs] + factors * 2, specs, outs, [whole(o.shape) for o in outs])


def stage_dense(spot, wide, thin, cotangent):
    features, units = wide.shape
    part = units // 4
    rows = cotangent.shape[1]

    def body(spot_ref, wide_ref, thin_ref, last_ref, cot_ref, wide_out, thin_out, last_out, cot_out):
        for r in range(4):

            @pl.when(spot_ref[2] == r)
            def _():
                wide_out[...] = wide_ref[:, r * part : (r + 1) * part].T

        thin_out[...] = thin_ref[...]
        last_out[...] = last_ref[...]
        cot_out[...] = cot_ref[0]

    specs = [
        whole(wide.shape),
        placed_block((part, features), lambda i, spot: (spot[2], 0)),
        placed_block((part, features), lambda i, spot: (spot[2] ^ 3, 0)),
        placed_block((1, rows, features), lambda i, spot: (spot[1], 0, 0)),
    ]
    outs = [shaped((part, features), bf16)] * 3 + [shaped((rows, features), bf16)]
    return call(body, (spot,), [wide, thin, thin, cotangent], specs, outs, [whole(o.shape) for o in outs])


def project_rows(weight, rows_in, outer, low):
    return (nt(weight, rows_in) + tn(twice(outer), halves(low))).astype(bf16)


def project_near(spot, pick, inputs, received, gain, shift, inners, pack, side, weights):
    rows, features = inputs.shape[1:]
    tokens = 2 * rows
    width = weights[0].shape[0]
    rank = inners[0].shape[1]

    def body(spot_ref, pick_ref, xa, xb, gain_ref, shift_ref, iq, ik, iv, pack_ref, side_ref, *refs):
        hbm, (z_ref, low_ref, kv_ref, ws, sems) = refs[:4], refs[4:]
        copies = [pltpu.make_async_copy(hbm[n], ws.at[n], sems.at[n]) for n in range(4)]
        for c in copies:
            c.start()
        states = jnp.concatenate([xa[0], xb[...]], axis=0).astype(f32)
        z_ref[...] = normalize(states, gain_ref[...], shift_ref[...])[0].astype(bf16)
        low = nt(jnp.concatenate([iq[0], ik[0], iv[0]], axis=0), z_ref[...])
        low_ref[...] = low
        for i, packs in enumerate((pack_ref, side_ref)):
            for n in (1, 2):
                outer = packs[:rank, n * width : (n + 1) * width]
                copies[2 * i + n - 1].wait()
                kv_ref[i, n - 1] = project_rows(
                    ws[2 * i + n - 1], z_ref[...], outer, low[n * rank : (n + 1) * rank]
                )

    specs = [
        placed_block((1, rows, features), lambda i, spot, *_: (spot[0], 0, 0)),
        placed_block((rows, features), lambda *_: (0, 0)),
        whole((1, features)),
        whole((1, features)),
    ]
    specs += [placed_block((1, rank, features), of_mine(n)) for n in range(3)]
    specs += [whole(pack.shape), whole(side.shape)] + [in_hbm] * 4
    outs = [
        shaped((tokens, features), bf16),
        shaped((3 * rank, tokens), f32),
        shaped((2, 2, width, tokens), bf16),
    ]
    return call(
        body,
        (spot, pick),
        [inputs, received, gain, shift] + inners + [pack, side] + weights,
        specs,
        outs,
        [whole(o.shape) for o in outs],
        scratch=[pltpu.VMEM((4, width, features), bf16), pltpu.SemaphoreType.DMA((4,))],
    )


def queries_near(z, low, pack, side, weights):
    tokens, features = z.shape
    width = weights[0].shape[0]
    rank = low.shape[0] // 3

    def body(z_ref, low_ref, pack_ref, side_ref, w0, w1, q_ref):
        for i, (packs, w) in enumerate(((pack_ref, w0), (side_ref, w1))):
            q_ref[i] = project_rows(w[...], z_ref[...], packs[:rank, :width], low_ref[:rank])

    operands = [z, low, pack, side] + weights
    out = shaped((2, width, tokens), bf16)
    return call(body, (), operands, [whole(o.shape) for o in operands], out, whole(out.shape))


def project_far(spot, z, low, received, side, parts):
    tokens, features = z.shape
    head_rows = parts[0][0].shape[1]
    width = 4 * head_rows
    rank = low.shape[0] // 3
    base = received.shape[0] - 3 * rank
    flat = [p for group in parts for p in group]

    def body(spot_ref, z_ref, low_ref, received_ref, side_ref, *refs):
        ins, (out_ref, kv_ref, q_ref, weight_ref, sems) = refs[:10], refs[10:]
        for i in range(2):
            group = ins[5 * i : 5 * i + 5]
            for n in range(4):
                for r in range(4):
                    at = pl.ds(pl.multiple_of((spot_ref[0] ^ r) * head_rows, 16), head_rows)
                    if r < 3:
                        weight_ref[i, n, at] = group[r][n]
                    else:
                        weight_ref[i, n, at] = group[3 + n // 2][n % 2]
        copies = [pltpu.make_async_copy(weight_ref.at[i], out_ref.at[i], sems.at[i]) for i in range(2)]
        for c in copies:
            c.start()
        for i, (ref, start) in enumerate(((received_ref, base), (side_ref, 0))):
            for n in range(3):
                outer = ref[start : start + rank, n * width : (n + 1) * width]
                y = project_rows(weight_ref[i, n], z_ref[...], outer, low_ref[n * rank : (n + 1) * rank])
                if n == 0:
                    q_ref[i] = y
                else:
                    kv_ref[i, n - 1] = y
        for c in copies:
            c.wait()

    operands = [z, low, received, side] + flat
    outs = [
        shaped((2, 4, width, features), bf16),
        shaped((2, 2, width, tokens), bf16),
        shaped((2, width, tokens), bf16),
    ]
    return call(
        body, (spot[2:3],), operands, [KEEP] * len(operands), outs, [remain, KEEP, KEEP],
        scratch=[pltpu.VMEM((2, 4, width, features), bf16), pltpu.SemaphoreType.DMA((2,))],
    )


def attend(spot, lengths, q, kv, kv_side):
    _, width, tokens = q.shape
    rows = tokens // 2
    pair = 2 * HEAD_DIM
    steps = width // pair

    def body(spot_ref, length_ref, q_ref, k1, k2, v1, v2, ctx_ref, total_ref):
        bias1 = jnp.where(live_column(spot_ref, length_ref, rows, (0, 2)), 0.0, neg_fill * log2_e)
        bias2 = jnp.where(live_column(spot_ref, length_ref, rows, (1, 3)), 0.0, neg_fill * log2_e)
        for h in range(2):
            at = slice(h * HEAD_DIM, (h + 1) * HEAD_DIM)
            query = q_ref[0, at]
            s1 = tn(k1[0, 0, at], query) * (score_scale * log2_e) + bias1
            s2 = tn(k2[0, 0, at], query) * (score_scale * log2_e) + bias2
            top = jnp.maximum(jnp.max(s1, axis=0, keepdims=True), jnp.max(s2, axis=0, keepdims=True))
            p1 = jnp.exp2(s1 - top)
            p2 = jnp.exp2(s2 - top)
            total = jnp.sum(p1, axis=0, keepdims=True) + jnp.sum(p2, axis=0, keepdims=True)
            context = nn(v1[0, 0, at], p1.astype(bf16)) + nn(v2[0, 0, at], p2.astype(bf16))
            ctx_ref[0, at] = (context * (1.0 / total)).astype(bf16)
            total_ref[h] = top + jnp.log2(total)

    def own(n):
        return pl.BlockSpec((1, 1, pair, tokens), lambda h, *_: (h // steps, n, h % steps, 0))

    def beside(n):
        return pl.BlockSpec((1, 1, pair, tokens), lambda h, *_: (1 - h // steps, n, h % steps, 0))

    rows_spec = pl.BlockSpec((1, pair, tokens), lambda h, *_: (h // steps, h % steps, 0))
    return call(
        body,
        (spot, lengths),
        [q, kv, kv_side, kv, kv_side],
        [rows_spec, own(0), beside(0), own(1), beside(1)],
        [shaped(q.shape, bf16), shaped((4 * steps, 1, tokens), f32)],
        [rows_spec, pl.BlockSpec((2, 1, tokens), lambda h, *_: (h, 0, 0))],
        grid=(2 * steps,),
    )


def attend_back(spot, lengths, q, kv, kv_side, grad_context, totals, deltas, number):
    _, width, tokens = q.shape
    rows = tokens // 2
    pair = 2 * HEAD_DIM
    steps = width // pair
    at_hand = number % 2

    def body(spot_ref, length_ref, q_ref, k1, k2, v1, v2, g_ref, total_ref, delta_ref, gq, own_ref, other_ref):
        bias1 = jnp.where(live_column(spot_ref, length_ref, rows, (0, 2)), 0.0, neg_fill * log2_e)
        bias2 = jnp.where(live_column(spot_ref, length_ref, rows, (1, 3)), 0.0, neg_fill * log2_e)
        for h in range(2):
            at = slice(h * HEAD_DIM, (h + 1) * HEAD_DIM)
            query = q_ref[0, at]
            grad = g_ref[0, at]
            grad_query = None
            for k, v, bias, out in ((k1, v1, bias1, own_ref), (k2, v2, bias2, other_ref)):
                s = tn(k[0, 0, at], query) * (score_scale * log2_e) + bias
                soft = jnp.exp2(s - total_ref[h])
                grad_soft = tn(v[0, 0, at], grad)
                grad_scores = (soft * (grad_soft - delta_ref[h])).astype(bf16)
                part = nn(k[0, 0, at], grad_scores)
                grad_query = part if grad_query is None else grad_query + part
                out[0, at] = (nt(query, grad_scores) * score_scale).astype(out.dtype)
                out[1, at] = nt(grad, soft.astype(bf16)).astype(out.dtype)
            gq[at] = (grad_query * score_scale).astype(bf16)

    def own(n):
        return pl.BlockSpec((1, 1, pair, tokens), lambda h, *_: (at_hand, n, h, 0))

    def beside(n):
        return pl.BlockSpec((1, 1, pair, tokens), lambda h, *_: (1 - at_hand, n, h, 0))

    rows_spec = pl.BlockSpec((1, pair, tokens), lambda h, *_: (at_hand, h, 0))
    grads_spec = pl.BlockSpec((1, pair, tokens), lambda h, *_: (number, h, 0))
    line = pl.BlockSpec((2, 1, tokens), lambda h, *_: (steps * at_hand + h, 0, 0))
    line_at = pl.BlockSpec((2, 1, tokens), lambda h, *_: (steps * number + h, 0, 0))
    both = pl.BlockSpec((2, pair, tokens), lambda h, *_: (0, h, 0))
    return call(
        body,
        (spot, lengths),
        [q, kv, kv_side, kv, kv_side, grad_context, totals, deltas],
        [rows_spec, own(0), beside(0), own(1), beside(1), grads_spec, line, line_at],
        [shaped(q.shape[1:], bf16), shaped(kv.shape[1:], f32), shaped(kv.shape[1:], bf16)],
        [pl.BlockSpec((pair, tokens), lambda h, *_: (h, 0)), both, both],
        grid=(steps,), weight=8)


cubic = 0.044715
BLOCK = 512
BIG = 20
root = math.sqrt(2.0 / math.pi)


def bend_of(widened, grad):
    square = widened * widened
    bend = jnp.tanh(root * widened * (1.0 + cubic * square))
    up = 0.5 * (1.0 + bend)
    slope = up + widened * (0.5 * root) * (1.0 - bend * bend) * (1.0 + 3.0 * cubic * square)
    return (widened * up).astype(bf16), (grad * slope).astype(bf16)


def feed_quarter(z_ref, gy_ref, wide_ref, thin_ref, pack_ref, rank, low_w, low_n, act_ref, grad_ref, sums_ref, ready=None):
    units = wide_ref.shape[1]
    low_w2, low_n2 = halves(low_w), halves(low_n)
    for start in range(0, units, BLOCK):
        at = slice(start, min(start + BLOCK, units))
        if ready is not None:
            ready(at)
        widened = nn(z_ref[...], wide_ref[:, at]) + tn(low_w2, twice(pack_ref[rank : 2 * rank, at]))
        grad = nt(gy_ref[...], thin_ref[at, :]) + tn(low_n2, twice(pack_ref[2 * rank : 3 * rank, at]))
        act_ref[:, at], grad_ref[:, at] = bend_of(widened, grad)
    sums_ref[:rank] = folded(nn(low_w2, grad_ref[...]))
    sums_ref[rank:] = folded(nn(low_n2, act_ref[...]))
    return (
        nn(act_ref[...], thin_ref[...]),
        nt(grad_ref[...], wide_ref[...]),
        nt(pack_ref[2 * rank : 3 * rank], act_ref[...]),
        nt(pack_ref[rank : 2 * rank], grad_ref[...]),
    )


def feed_units(z_ref, gy_ref, wide_ref, thin_ref, outer, inner, low_w, low_n, act_ref, grad_ref, ready):
    units = wide_ref.shape[0]
    low_w2, low_n2 = halves(low_w), halves(low_n)
    for start in range(0, units, BLOCK):
        at = slice(start, min(start + BLOCK, units))
        ready(at.stop)
        widened = nt(z_ref[...], wide_ref[at]) + tn(low_w2, twice(outer[:, at]))
        grad = nt(gy_ref[...], thin_ref[at]) + tn(low_n2, twice(inner[:, at]))
        act_ref[:, at], grad_ref[:, at] = bend_of(widened, grad)
    sums = jnp.concatenate(
        [folded(nn(low_w2, grad_ref[...])), folded(nn(low_n2, act_ref[...]))], axis=0
    )
    return (
        nn(act_ref[...], thin_ref[...]),
        nn(grad_ref[...], wide_ref[...]),
        nt(inner, act_ref[...]),
        nt(outer, grad_ref[...]),
        sums,
    )


def output_inner_rows(pack_ref, side_ref, received_ref, far_side_ref, rank, base, width):
    lanes = slice(3 * width, 4 * width)
    return [
        pack_ref[:rank, lanes],
        side_ref[:rank, lanes],
        received_ref[base : base + rank, lanes],
        far_side_ref[:rank, lanes],
    ]


def feed_open(spot, pick, lengths, contexts, outs_w, far, packs, tables, inputs, received, gain, shift):
    rows, features = inputs.shape[1:]
    tokens = 2 * rows
    width = contexts[0].shape[1]
    rank = tables[0].shape[1]
    pack, side, far_side = packs
    base = received.shape[0] - 3 * rank

    def body(spot_ref, pick_ref, length_ref, c01, c23, wo0, wo1, far_ref, pack_ref, side_ref, far_side_ref, received_ref, oo, wi, xa, gain_ref, shift_ref, hidden_ref, z_ref, lows_ref):
        states = jnp.concatenate([xa[0], received_ref[:rows]], axis=0).astype(f32)
        mask = live_column(spot_ref, length_ref, rows, (0, 2)).astype(f32)
        inner_o = output_inner_rows(pack_ref, side_ref, received_ref, far_side_ref, rank, base, width)
        contexts_all = [c01[0], c01[1], c23[0], c23[1]]
        weights_all = [wo0[...], wo1[...], far_ref[0, 0], far_ref[1, 0]]
        joined = jnp.concatenate(contexts_all, axis=0)
        attended = tn(joined, jnp.concatenate(weights_all, axis=0))
        low_o = nn(jnp.concatenate(inner_o, axis=1), joined)
        attended = attended + tn(halves(low_o), twice(oo[0]))
        hidden = states + mask * attended
        hidden_ref[...] = hidden
        z_ref[...] = normalize(hidden, gain_ref[...], shift_ref[...])[0].astype(bf16)
        lows_ref[:rank] = low_o
        lows_ref[rank:] = nt(wi[0], z_ref[...])

    operands = contexts + outs_w + [far, pack, side, far_side, received] + tables[:2]
    specs = [whole(c.shape) for c in contexts] + [whole(w.shape) for w in outs_w]
    specs += [placed_block((2, 1, width, features), lambda *_: (0, 3, 0, 0))]
    specs += [whole(p.shape) for p in packs] + [whole(received.shape)]
    specs += [placed_block((1, rank, features), of_mine(n)) for n in (3, 4)]
    operands += [inputs, gain, shift]
    specs += [placed_block((1, rows, features), lambda i, spot, *_: (spot[0], 0, 0))]
    specs += [whole(gain.shape), whole(shift.shape)]
    outs = [shaped((tokens, features), f32), shaped((tokens, features), bf16), shaped((2 * rank, tokens), f32)]
    return call(body, (spot, pick, lengths), operands, specs, outs, [KEEP] * 3)


def feed_first(spot, pick, lengths, z, lows, table, cotangent, cot_side, pack, dense):
    tokens, features = z.shape
    rows = tokens // 2
    rank = table.shape[1]
    units = dense[0].shape[1]

    def body(spot_ref, pick_ref, length_ref, z_ref, lows_in, no, ca, cb, pack_ref, wide, thin, gy_ref, branch_ref, second_ref, lows_ref, sums_ref, act_ref, grad_ref):
        mask = live_column(spot_ref, length_ref, rows, (0, 2)).astype(f32)
        grad_in = jnp.concatenate([ca[0], cb[...]], axis=0).astype(f32)
        gy_ref[...] = (mask * grad_in).astype(bf16)
        low_n = nt(no[0], gy_ref[...])
        lows_ref[: 2 * rank] = lows_in[...]
        lows_ref[2 * rank : 3 * rank] = low_n
        branch_ref[...], second_ref[...], lows_ref[3 * rank : 4 * rank], lows_ref[4 * rank :] = feed_quarter(
            z_ref, gy_ref, wide, thin, pack_ref, rank, lows_in[rank:], low_n, act_ref, grad_ref, sums_ref
        )

    operands = [z, lows, table, cotangent, cot_side, pack] + dense
    specs = [KEEP, KEEP, placed_block((1, rank, features), of_mine(5))]
    specs += [placed_block((1, rows, features), lambda i, spot, *_: (spot[0], 0, 0))] + [KEEP] * 4
    outs = [
        shaped((tokens, features), bf16),
        shaped((tokens, features), f32),
        shaped((tokens, features), f32),
        shaped((5 * rank, tokens), f32),
        shaped((2 * rank, units), f32),
    ]
    scratch = [pltpu.VMEM((tokens, units), bf16)] * 2
    return call(body, (spot, pick, lengths), operands, specs, outs, [KEEP] * 5, scratch=scratch, limit=BIG)


def feed_near(z, gy, branch, second, lows, pack, dense):
    tokens, features = z.shape
    units = dense[0].shape[1]
    rank = lows.shape[0] // 5
    blocks = [slice(n, min(n + BLOCK, units)) for n in range(0, units, BLOCK)]

    def body(z_ref, gy_ref, branch_in, second_in, lows_in, pack_ref, wide_hbm, thin_hbm, branch_ref, second_ref, lows_ref, sums_ref, wide, thin, act_ref, grad_ref, sems):
        copies = {}
        for n, at in enumerate(blocks):
            copies[at.start] = (
                pltpu.make_async_copy(wide_hbm.at[:, at], wide.at[:, at], sems.at[0, n]),
                pltpu.make_async_copy(thin_hbm.at[at], thin.at[at], sems.at[1, n]),
            )
            for c in copies[at.start]:
                c.start()

        def ready(at):
            for c in copies[at.start]:
                c.wait()

        sums = feed_quarter(
            z_ref, gy_ref, wide, thin, pack_ref, rank, lows_in[rank : 2 * rank], lows_in[2 * rank : 3 * rank],
            act_ref, grad_ref, sums_ref, ready,
        )
        branch_ref[...] = branch_in[...] + sums[0]
        second_ref[...] = second_in[...] + sums[1]
        lows_ref[: 3 * rank] = lows_in[: 3 * rank]
        lows_ref[3 * rank : 4 * rank] = lows_in[3 * rank : 4 * rank] + sums[2]
        lows_ref[4 * rank :] = lows_in[4 * rank :] + sums[3]

    operands = [z, gy, branch, second, lows, pack] + dense
    outs = [shaped(branch.shape, f32), shaped(second.shape, f32), shaped(lows.shape, f32), shaped((2 * rank, units), f32)]
    scratch = [pltpu.VMEM(d.shape, bf16) for d in dense] + [pltpu.VMEM((tokens, units), bf16)] * 2
    scratch += [pltpu.SemaphoreType.DMA((2, len(blocks)))]
    return call(
        body, (), operands, [KEEP] * 6 + [in_hbm] * 2, outs, [KEEP] * 4, scratch=scratch, aliases={2: 0, 3: 1}, limit=BIG
    )


def far_copies(ins, wide, thin, sems):
    part = ins[0].shape[0]
    copies = []
    for n in range(len(ins) // 4):
        for q in range(2):
            k = 2 * n + q
            at = slice(k * part, (k + 1) * part)
            copies.append(pltpu.make_async_copy(ins[4 * n + q], wide.at[at], sems.at[2 * k]))
            copies.append(pltpu.make_async_copy(ins[4 * n + 2 + q], thin.at[at], sems.at[2 * k + 1]))
    for c in copies:
        c.start()
    return copies


def far_parts(parts, z_ref, gy_ref, copies, wide, thin, received_ref, far_side_ref, rank, base, low_w, low_n, act_ref, grad_ref, sums_ref):
    count = wide.shape[0] // (2 * len(parts))
    outer, inner = [], []
    for r in parts:
        lanes = slice(r * count, (r + 1) * count)
        outer += [received_ref[base + rank : base + 2 * rank, lanes], far_side_ref[rank : 2 * rank, lanes]]
        inner += [received_ref[base + 2 * rank : base + 3 * rank, lanes], far_side_ref[2 * rank : 3 * rank, lanes]]
    arrived = []

    def ready(end):
        while len(arrived) * count < min(end, wide.shape[0]):
            n = len(arrived)
            copies[2 * n].wait()
            copies[2 * n + 1].wait()
            arrived.append(n)

    *total, sums = feed_units(
        z_ref, gy_ref, wide, thin, jnp.concatenate(outer, axis=1), jnp.concatenate(inner, axis=1), low_w, low_n,
        act_ref, grad_ref, ready,
    )
    sums_ref[...] = sums
    return total


def far_scratch(parts, part, features, tokens):
    units = 2 * len(parts) * part
    return [pltpu.VMEM((units, features), bf16)] * 2 + [pltpu.VMEM((tokens, units), bf16)] * 2 + [
        pltpu.SemaphoreType.DMA((4 * len(parts),))
    ]


def feed_far(parts, z, gy, branch, second, lows, received, far_side, weights):
    tokens, features = z.shape
    part = weights[0].shape[0]
    rank = lows.shape[0] // 5
    base = received.shape[0] - 3 * rank
    count = len(weights)

    def body(z_ref, gy_ref, branch_in, second_in, lows_in, received_ref, far_side_ref, *refs):
        ins, (branch_ref, second_ref, lows_ref, sums_ref) = refs[:count], refs[count : count + 4]
        wide, thin, act_ref, grad_ref, sems = refs[count + 4 :]
        copies = far_copies(ins, wide, thin, sems)
        total = far_parts(
            parts, z_ref, gy_ref, copies, wide, thin, received_ref, far_side_ref, rank, base,
            lows_in[rank : 2 * rank], lows_in[2 * rank : 3 * rank], act_ref, grad_ref, sums_ref,
        )
        branch_ref[...] = branch_in[...] + total[0]
        second_ref[...] = second_in[...] + total[1]
        lows_ref[: 3 * rank] = lows_in[: 3 * rank]
        lows_ref[3 * rank : 4 * rank] = lows_in[3 * rank : 4 * rank] + total[2]
        lows_ref[4 * rank :] = lows_in[4 * rank :] + total[3]

    operands = [z, gy, branch, second, lows, received, far_side] + weights
    outs = [
        shaped(branch.shape, f32),
        shaped(second.shape, f32),
        shaped(lows.shape, f32),
        shaped((2 * rank, 2 * len(parts) * part), f32),
    ]
    return call(
        body, (), operands, [KEEP] * 7 + [in_hbm] * count, outs, [KEEP] * 4,
        scratch=far_scratch(parts, part, features, tokens), aliases={2: 0, 3: 1}, limit=BIG,
    )


def shares(array, core):
    half = array.shape[1] // 2
    low, high = array[:, :half], array[:, half:]
    return jnp.where(core == 0, low, high), jnp.where(core == 0, high, low)


def padded(array, count):
    return jnp.concatenate([array, jnp.zeros((array.shape[0], count - array.shape[1]), array.dtype)], axis=1)


def lanes_up(count):
    return (count + 127) // 128 * 128


def feed_close(parts, spot, pick, lengths, hidden, z, gy, branch, second, lows, near_sums, far_sums, contexts, outs_w, far, packs, tables, received, cotangent, cot_side, gain, weights):
    tokens, features = hidden.shape
    rows = tokens // 2
    width = contexts[0].shape[1]
    rank = tables[0].shape[1]
    pack, side, far_side = packs
    base = received.shape[0] - 3 * rank
    part = weights[0].shape[0]
    units = 4 * part
    heads = width // HEAD_DIM
    half = features // 2
    tail = lanes_up(width)
    total_lanes = 3 * half + 2 * (2 * units + tail)

    def body(spot_ref, pick_ref, length_ref, hidden_ref, z_ref, gy_ref, branch_in, second_in, lows_ref, near0, near1, far0, far3, c01, c23, wo0, wo1, far_ref, pack_ref, side_ref, far_side_ref, received_ref, oo, wi, no, ca, cb, gain_ref, *refs):
        hbm, (out_ref, outb_ref, gh_ref, gc_ref, delta_ref, keep_ref, give_ref) = refs[:8], refs[8:15]
        wide, thin, act_ref, grad_ref, sems, last, ga_ref = refs[15:]
        copies = far_copies(hbm, wide, thin, sems)
        low_w = lows_ref[rank : 2 * rank]
        low_n = lows_ref[2 * rank : 3 * rank]
        found = far_parts(
            parts, z_ref, gy_ref, copies, wide, thin, received_ref, far_side_ref, rank, base,
            low_w, low_n, act_ref, grad_ref, last,
        )
        branch = branch_in[...] + found[0]
        grad_second = second_in[...] + found[1]
        low_next = lows_ref[3 * rank : 4 * rank] + found[2]
        grad_low = lows_ref[4 * rank :] + found[3]
        mask = live_column(spot_ref, length_ref, rows, (0, 2)).astype(f32)
        branch = branch + tn(halves(low_next), twice(no[0]))
        grad_second = grad_second + tn(halves(grad_low), twice(wi[0]))
        hidden_now = hidden_ref[...]
        output = (hidden_now + mask * branch).astype(bf16)
        out_ref[0] = output[:rows]
        outb_ref[...] = output[rows:]
        _, unit, scaled = normalize(hidden_now, gain_ref[...], gain_ref[...])
        grad_in = jnp.concatenate([ca[0], cb[...]], axis=0).astype(f32)
        grad_hidden = grad_in + normalize_back(grad_second, unit, scaled, gain_ref[...])
        gh_ref[...] = grad_hidden
        ga_ref[...] = (mask * grad_hidden).astype(bf16)
        grad_low_o = nt(oo[0], ga_ref[...])
        low_o2 = halves(grad_low_o)
        inner_o = output_inner_rows(pack_ref, side_ref, received_ref, far_side_ref, rank, base, width)
        contexts_all = [c01[0], c01[1], c23[0], c23[1]]
        weights_all = [wo0, wo1, far_ref.at[0, 0], far_ref.at[1, 0]]
        inner_sums = []
        for i in range(4):
            grad = (nt(weights_all[i][...], ga_ref[...]) + tn(twice(inner_o[i]), low_o2)).astype(bf16)
            gc_ref[i] = grad
            product = grad.astype(f32) * contexts_all[i].astype(f32)
            for h in range(heads):
                delta_ref[heads * i + h] = jnp.sum(
                    product[h * HEAD_DIM : (h + 1) * HEAD_DIM], axis=0, keepdims=True
                )
            inner_sums.append(folded(nt(low_o2, contexts_all[i])))
        core = spot_ref[3] & 1
        quad = spot_ref[2]
        shared = (
            folded(nn(halves(grad_low), z_ref[...])),
            folded(nn(halves(lows_ref[:rank]), ga_ref[...])),
            folded(nn(halves(low_next), gy_ref[...])),
        )
        for n in range(3):
            keep_ref[:, n * half : (n + 1) * half], give_ref[:, n * half : (n + 1) * half] = shares(shared[n], core)
        quarters = []
        for near in (near0, near1):
            quarters.append((near[:rank], near[rank:]))
        for q in range(2):
            lanes = slice(q * part, (q + 1) * part)
            later = slice((2 + q) * part, (3 + q) * part)
            pieces = [far0[:, lanes], last[:, lanes], last[:, later], far3[:, lanes]]
            joined = shuffled(jnp.concatenate(pieces, axis=1), quad)
            quarters.append((joined[:rank], joined[rank:]))
        for i in range(4):
            ref = (keep_ref, give_ref)[i % 2]
            at = 3 * half + (i // 2) * (2 * units + tail)
            ref[:, at : at + units] = quarters[i][0]
            ref[:, at + units : at + 2 * units] = quarters[i][1]
            ref[:, at + 2 * units : at + 2 * units + tail] = padded(inner_sums[i], tail)

    operands = [hidden, z, gy, branch, second, lows] + near_sums + far_sums + contexts + outs_w
    specs = [whole(hidden.shape), KEEP, KEEP, KEEP, KEEP] + [whole(o.shape) for o in operands[5:]]
    operands += [far, pack, side, far_side, received] + tables
    specs += [placed_block((2, 1, width, features), lambda *_: (0, 3, 0, 0))]
    specs += [whole(p.shape) for p in packs] + [whole(received.shape)]
    specs += [placed_block((1, rank, features), of_mine(n)) for n in (3, 4, 5)]
    operands += [cotangent, cot_side, gain] + weights
    specs += [placed_block((1, rows, features), lambda i, spot, *_: (spot[0], 0, 0))]
    specs += [whole(cot_side.shape), whole(gain.shape)] + [remain] * 8
    outs = [
        shaped((2, rows, features), bf16),
        shaped((rows, features), bf16),
        shaped((tokens, features), f32),
        shaped((4, width, tokens), bf16),
        shaped((4 * heads, 1, tokens), f32),
        shaped((rank, total_lanes), f32),
        shaped((rank, total_lanes), f32),
    ]
    scratch = far_scratch(parts, part, features, tokens)
    scratch += [pltpu.VMEM((2 * rank, 4 * part), f32), pltpu.VMEM((tokens, features), bf16)]
    out_specs = [placed_block((1, rows, features), lambda i, spot, *_: (spot[0], 0, 0))] + [KEEP] * 6
    return call(body, (spot, pick, lengths), operands, specs, outs, out_specs, scratch=scratch, limit=BIG)


def gather_pair(quarters, low, factors, before=None):
    rank = low.shape[0] // 3
    width, tokens = quarters[0][0].shape
    tail = lanes_up(3 * width)
    extra = 0 if before is None else 1

    def body(*refs):
        groups = [refs[3 * i : 3 * i + 3] for i in range(2)]
        low_ref, *places = refs[6:9]
        g_ref, gl_ref, keep_ref, give_ref = refs[9 + extra :]
        lows = [halves(low_ref[n * rank : (n + 1) * rank]) for n in range(3)]
        for n in range(3):
            at = slice(n * rank, (n + 1) * rank)
            total = jnp.zeros((rank, tokens), f32) if before is None else refs[9][at]
            for i in range(2):
                q, own, other = groups[i][0], groups[i][1], groups[1 - i][2]
                if n == 0:
                    g = q[...]
                else:
                    g = (own[n - 1] + other[n - 1].astype(f32)).astype(bf16)
                g_ref[i, n] = g
                total = total + nn(places[i][:rank, n * width : (n + 1) * width], g)
                (keep_ref, give_ref)[i][:, n * width : (n + 1) * width] = folded(nt(lows[n], g))
            gl_ref[at] = total
        for ref in (keep_ref, give_ref):
            ref[:, 3 * width :] = jnp.zeros((rank, tail - 3 * width), f32)

    operands = [a for q in quarters for a in q] + [low] + list(factors) + ([] if before is None else [before])
    outs = [
        shaped((2, 3, width, tokens), bf16),
        shaped((3 * rank, tokens), f32),
        shaped((rank, tail), f32),
        shaped((rank, tail), f32),
    ]
    return call(body, (), operands, [KEEP] * len(operands), outs, [KEEP] * 4, weight=3)


def gather_inner(spot, gl, z, first, second):
    features = z.shape[1]
    rank = gl.shape[0] // 3
    half = features // 2
    tail = first[0].shape[1]

    def body(spot_ref, gl_ref, z_ref, a0, b0, a1, b1, keep_ref, give_ref):
        core = spot_ref[3] & 1
        for n in range(3):
            inner = folded(nn(halves(gl_ref[n * rank : (n + 1) * rank]), z_ref[...]))
            keep_ref[:, n * half : (n + 1) * half], give_ref[:, n * half : (n + 1) * half] = shares(inner, core)
        for ref, pieces in ((keep_ref, (a0, a1)), (give_ref, (b0, b1))):
            for i in range(2):
                ref[:, 3 * half + i * tail : 3 * half + (i + 1) * tail] = pieces[i][...]

    out = shaped((rank, 3 * half + 2 * tail), f32)
    operands = [gl, z] + list(first) + list(second)
    return call(body, (spot,), operands, [KEEP] * 6, [out, out], [KEEP] * 2, weight=2)


def settle(spot, pick, keep, moved, common, with_picks):
    rank, lanes = keep.shape
    own = (lanes - common) // 2
    extra = 128 if with_picks else 0

    def body(spot_ref, pick_ref, keep_ref, moved_ref, here_ref, there_ref):
        total = (keep_ref[...] + moved_ref[...]).astype(bf16)
        here_ref[:, : common + own] = total[:, : common + own]
        there_ref[:, :common] = total[:, :common]
        there_ref[:, common : common + own] = total[:, common + own :]
        if with_picks:
            iota = lax.broadcasted_iota(jnp.int32, (rank, 128), 1)
            line = jnp.zeros((rank, 128), f32)
            for n in range(6):
                line = jnp.where(iota == n, pick_ref[spot_ref[0], n].astype(f32), line)
            here_ref[:, common + own :] = line.astype(bf16)
            there_ref[:, common + own :] = line.astype(bf16)

    out = shaped((rank, common + own + extra), bf16)
    return call(body, (spot, pick), [keep, moved], [whole(keep.shape)] * 2, [out, out], [whole(out.shape)] * 2, weight=1)


def combine(spot, picks, arrays, groups, rows_of_table):
    per, rank = arrays[0].shape[:2]
    half = groups[0][1]

    def body(spot_ref, pick_ref, *refs):
        ins, outs = refs[: len(arrays)], refs[len(arrays) :]
        places = [outs[0].at[n] for n in range(3)] + list(outs[4:])
        for out in places:
            out[...] = jnp.zeros(out.shape, f32)
        for a, ref in enumerate(ins):
            for c in range(per):
                for (start, count, number), out in zip(groups, places):
                    row = pick_ref[a * per + c, number]
                    out[row] += ref[c, :, start : start + count].astype(f32)
        for n in range(3):
            outs[1 + n][...] = outs[0][n]

    outs = [shaped((3, rows_of_table, rank, half), f32)] + [shaped((rows_of_table, rank, 2 * half), f32)] * 3
    outs += [shaped((rows_of_table, rank, count), f32) for _, count, _ in groups[3:]]
    own = placed_block((rows_of_table, rank, half), lambda i, spot, pick: (0, 0, spot[3] & 1))
    specs = [KEEP] + [own] * 3 + [KEEP] * (len(groups) - 3)
    return call(body, (spot, picks), list(arrays), [KEEP] * len(arrays), outs, specs, weight=100)


def complete(spot, tables, moved):
    _, count, rank, half = moved.shape

    def body(spot_ref, moved_ref, *refs):
        for n in range(3):
            refs[3 + n][...] = moved_ref[n]

    out = shaped((count, rank, 2 * half), f32)
    theirs = placed_block((count, rank, half), lambda i, spot: (0, 0, 1 - (spot[3] & 1)))
    return call(
        body, (spot,), [moved] + list(tables), [KEEP] + [remain] * 3, [out] * 3, [theirs] * 3,
        aliases={2: 0, 3: 1, 4: 2}, weight=2)


def pair_up(spot, array, second):
    rows, features = second.shape

    def body(spot_ref, array_ref, second_ref, out_ref):
        out_ref[0] = second_ref[...].astype(array.dtype)

    out_spec = placed_block((1, rows, features), lambda i, spot: (spot[1], 0, 0))
    return call(
        body, (spot,), [array, second], [remain, KEEP], shaped(array.shape, array.dtype), out_spec, aliases={1: 0}, weight=1)


def pair_and_complete(spot, array, second, tables, moved):
    rows, features = second.shape
    _, count, rank, half = moved.shape

    def body(spot_ref, second_ref, moved_ref, *refs):
        refs[4][0] = second_ref[...].astype(array.dtype)
        for n in range(3):
            refs[5 + n][...] = moved_ref[n]

    table = shaped((count, rank, 2 * half), f32)
    theirs = placed_block((count, rank, half), lambda i, spot: (0, 0, 1 - (spot[3] & 1)))
    out_spec = placed_block((1, rows, features), lambda i, spot: (spot[1], 0, 0))
    return call(
        body, (spot,), [second, moved, array] + list(tables), [KEEP] * 2 + [remain] * 4,
        [shaped(array.shape, array.dtype)] + [table] * 3, [out_spec] + [theirs] * 3,
        aliases={3: 0, 4: 1, 5: 2, 6: 3}, weight=2,
    )


def join(groups):
    flat = [a for g in groups for a in g]
    outs = [shaped((sum(a.shape[0] for a in g),) + g[0].shape[1:], g[0].dtype) for g in groups]

    def body(*refs):
        at = 0
        for g, out in zip(groups, refs[len(flat) :]):
            start = 0
            for a in g:
                out[start : start + a.shape[0]] = refs[at][...]
                start += a.shape[0]
                at += 1

    return call(body, (), flat, [KEEP] * len(flat), outs, [KEEP] * len(outs), weight=1)


def finish(spot, pick, g01, g23, gl, inners, weights, far, states, grad_hidden, gain, block):
    features = gain.shape[1]
    rows = g01.shape[3] // 2
    width = g01.shape[2]
    rank = gl.shape[0] // 3
    at = slice(block * rows, (block + 1) * rows)

    def body(spot_ref, pick_ref, g01_ref, g23_ref, gl_ref, iq, ik, iv, *refs):
        ws, (far_ref, x_ref, gh_ref, gain_ref, grad_ref) = refs[:6], refs[6:]
        low = [halves(gl_ref[n * rank : (n + 1) * rank, at]) for n in range(3)]
        total = tn(
            jnp.concatenate(low, axis=0),
            jnp.concatenate([twice(iq[0]), twice(ik[0]), twice(iv[0])], axis=0),
        )
        for i in range(4):
            if i < 2:
                weight = jnp.concatenate([w[...] for w in ws[3 * i : 3 * i + 3]], axis=0)
            else:
                weight = far_ref[i - 2].reshape(3 * width, features)
            g_ref = (g01_ref, g23_ref)[i // 2]
            total = total + tn(g_ref[i % 2, :, :, at].reshape(3 * width, rows), weight)
        x = x_ref[0] if block == 0 else x_ref[...]
        _, unit, scaled = normalize(x.astype(f32), gain_ref[...], gain_ref[...])
        grad = gh_ref[at] + normalize_back(total, unit, scaled, gain_ref[...])
        if block == 0:
            grad_ref[0] = grad
        else:
            grad_ref[...] = grad.astype(bf16)

    operands = [g01, g23, gl] + inners + weights + [far, states, grad_hidden, gain]
    specs = [KEEP] * 3
    specs += [placed_block((1, rank, features), of_mine(n)) for n in range(3)]
    specs += [KEEP] * 6
    specs += [placed_block((2, 3, width, features), lambda *_: (0, 0, 0, 0))]
    if block == 0:
        specs += [placed_block((1, rows, features), lambda i, spot, *_: (spot[0], 0, 0))]
        out, out_spec = shaped((2, rows, features), f32), placed_block((1, rows, features), lambda i, spot, *_: (spot[0], 0, 0))
    else:
        specs += [placed_block((rows, features), lambda *_: (0, 0))]
        out, out_spec = shaped((rows, features), bf16), KEEP
    specs += [KEEP] * 2
    return call(body, (spot, pick), operands, specs, out, out_spec, weight=5)


def make_body(dp_size, tensor_size):
    def across(array):
        return swap(array, "tensor", 2, tensor_size)

    def beside(array):
        return swap(array, "tensor", 1, tensor_size)

    def along(array, bits):
        return swap(array, "dp", bits, dp_size)

    def body(
        inputs,
        cotangent,
        lengths,
        adapter_pick,
        first_gain,
        first_bias,
        query_weight,
        key_weight,
        value_weight,
        output_weight,
        second_gain,
        second_bias,
        widen_weight,
        narrow_weight,
        query_inner,
        query_outer,
        key_inner,
        key_outer,
        value_inner,
        value_outer,
        output_inner,
        output_outer,
        widen_inner,
        widen_outer,
        narrow_inner,
        narrow_outer,
    ):
        rows, features = inputs.shape[1:]
        place = lax.axis_index("tensor")
        quad = lax.axis_index("dp") & 3
        mine = place >> 1
        spot = jnp.stack([mine, 1 - mine, quad, place]).astype(jnp.int32)
        pick = adapter_pick

        def flip(array):
            return jnp.swapaxes(array, 1, 2)

        small = [query_outer, key_outer, value_outer, flip(output_inner), widen_outer, flip(narrow_inner)]
        inners = [flip(query_inner), flip(key_inner), flip(value_inner)]
        tables = [output_outer, flip(widen_inner), narrow_outer]
        gains = [v.reshape(1, -1) for v in (first_gain, first_bias, second_gain, second_bias)]
        heads = [query_weight.T, key_weight.T, value_weight.T, output_weight]
        dense = [widen_weight, narrow_weight]
        width = query_outer.shape[2]
        half = features // 2

        head_rows = heads[0].shape[0] // 4
        together = jnp.stack([w.reshape(4, head_rows, features) for w in heads], axis=1)
        part_heads = lax.dynamic_index_in_dim(together, quad, 0, keepdims=False)
        far0 = across(part_heads)
        send, pack = stage(after(spot, part_heads), pick, inputs, small)
        near_heads = [beside(w) for w in after(heads, part_heads)]
        received = across(after(send, near_heads[:2]))
        side = beside(pack)
        near_dense = [beside(after(dense[0], near_heads))]
        near_dense.append(beside(after(dense[1], near_dense[0])))
        part_wide, part_thin, part_last, cot_send = stage_dense(
            after(spot, pack), widen_weight, narrow_weight, cotangent
        )
        far1, far2 = along(far0, 1), along(far0, 2)
        wide0 = across(after(part_wide, far0))
        z, low, kv01 = project_near(
            spot, pick, inputs, after(received, part_wide, side, far0, near_dense), gains[0], gains[1], inners, pack,
            side, [heads[1], heads[2], near_heads[1], near_heads[2]],
        )
        kv01_side = beside(kv01)
        q01 = queries_near(after(z, kv01), low, pack, side, [heads[0], near_heads[0]])
        side0 = beside(after(far0, kv01))
        side1 = beside(after(far1, kv01, side0))
        far3, far4 = along(after(far2[:2], q01), 1), along(after(far1[2:], q01), 2)
        c01, total01 = attend(spot, lengths, q01, kv01, after(kv01_side, side1))
        side2 = beside(after(far2, c01, side1))
        far_side = beside(after(received[rows:], c01))
        side3, side4 = beside(after(far3, c01)), beside(after(far4, c01))
        wide1, wide2 = along(after(wide0, c01), 1), along(after(wide0, c01), 2)
        cot_side = across(after(cot_send, c01))
        far, kv23, q23 = project_far(
            spot, after(z, c01, wide0), low, received, far_side,
            [[far0, far1, far2, far3, far4], [side0, side1, side2, side3, side4]],
        )
        kv23_side = beside(kv23)
        thin0 = across(after(part_thin, kv23))
        c23, total23 = attend(spot, lengths, q23, kv23, kv23_side)
        packs = [pack, side, far_side]
        outs_w = [heads[3], near_heads[3]]
        hidden, z2, lows = feed_open(
            spot, pick, lengths, [c01, c23], outs_w, far, packs, tables, inputs, received, gains[2], gains[3]
        )
        wide3 = along(after(wide2, lows), 1)
        thin3 = across(after(part_last, lows))
        wide_sides = [beside(after(w, lows)) for w in (wide0, wide1, wide2)]
        gy, branch, second, lows, sums0 = feed_first(
            spot, pick, lengths, z2, lows, tables[2], cotangent, cot_side, pack, dense
        )
        thin1, thin2 = along(after(thin0, lows), 1), along(after(thin0, lows), 2)
        thin_sides = [beside(after(thin0, lows))]
        branch, second, lows, sums1 = feed_near(
            z2, gy, branch, second, after(lows, wide_sides), side, near_dense
        )
        wide_sides.append(beside(after(wide3, sums1)))
        branch, second, lows, sums2 = feed_far(
            (0,), z2, gy, branch, second, lows, received, far_side, [wide0, wide_sides[0], thin0, thin_sides[0]]
        )
        thin_sides += [beside(after(t, sums2)) for t in (thin1, thin2, thin3)]
        branch, second, lows, sums3 = feed_far(
            (3,), z2, gy, branch, second, lows, received, far_side, [wide3, wide_sides[3], thin3, thin_sides[3]]
        )
        output, outb, grad_hidden, grad_context, deltas, keep, give = feed_close(
            (1, 2), spot, pick, lengths, hidden, z2, gy, branch, second, lows, [sums0, sums1], [sums2, sums3],
            [c01, c23], outs_w, far, packs, tables, received, cotangent, cot_side, gains[2],
            [wide1, wide_sides[1], thin1, thin_sides[1], wide2, wide_sides[2], thin2, thin_sides[2]],
        )

        def first_turn(here, other, crossed):
            one, two = join([[here[None], crossed[0][None]], [other[None], crossed[1][None]]])
            return [(one, along(one, 1)), (two, along(two, 2))]

        def second_turn(turns):
            one, two = join(turns)
            return [one, along(one, 2), two, along(two, 1)]

        def whole_sum(table):
            bits = 8
            while bits < dp_size:
                table = table + along(table, bits)
                bits *= 2
            return table

        def back(number, q, kv, kv_side, totals):
            gq, own, other = attend_back(spot, lengths, q, kv, kv_side, grad_context, totals, deltas, number)
            return gq, own, other

        moved = beside(give)
        here, there = settle(spot, pick, keep, moved, 3 * half, True)
        other = across(there)
        out_side = across(outb)
        crossed = [along(here, 4)]
        quarters = [back(0, after(q01, here), kv01, kv01_side, total01)]
        quarters.append(back(1, after(q01, quarters[0][0]), kv01, kv01_side, total01))
        sides = [beside(after(quarters[0][2], quarters[1][0]))]
        crossed.append(along(after(other, quarters[1][0]), 4))
        quarters.append(back(2, after(q23, quarters[1][0], out_side), kv23, kv23_side, total23))
        sides.append(beside(after(quarters[1][2], quarters[2][0], sides[0])))
        turns = first_turn(here, other, after(crossed, quarters[2][0]))
        quarters.append(back(3, after(q23, quarters[2][0], turns[0][0]), kv23, kv23_side, total23))
        pieces = [(gq, own, sided) for (gq, own, _), sided in zip(quarters, sides)]
        g01, gl, *first = gather_pair(
            [pieces[0], (after(pieces[1][0], quarters[3][0]),) + pieces[1][1:]], after(low, turns), [pack, side]
        )
        early = second_turn(after(turns, g01))
        sides += [beside(after(q[2], g01)) for q in quarters[2:]]
        pieces += [(gq, own, sided) for (gq, own, _), sided in zip(quarters[2:], sides[2:])]
        far_factors = [received[rows:], far_side]
        output = pair_up(spot, output, after(out_side, g01))
        g23, gl, *second = gather_pair(pieces[2:], low, far_factors, after(gl, output))
        keep, give = gather_inner(spot, gl, z, first, second)
        moved = beside(give)
        here, there = settle(spot, pick, keep, moved, 3 * half, False)
        other = across(there)
        crossed = [along(here, 4)]
        crossed.append(along(other, 4))
        ends = (gl, inners, heads[:3] + near_heads[:3], far)
        gradb = finish(spot, pick, g01, after(g23, other), *ends, received, grad_hidden, gains[0], 1)
        grad_side = across(gradb)
        grad = finish(spot, pick, g01, after(g23, gradb, crossed), *ends, inputs, grad_hidden, gains[0], 0)
        turns = first_turn(here, other, after(crossed, gradb))
        early = after(early, gradb, turns[0][0])
        picks = jnp.concatenate([a[:, 0, -128:-122] for a in early]).astype(jnp.int32)
        adapters = query_inner.shape[0]
        units = widen_weight.shape[1]
        base = 3 * half
        early = combine(
            spot,
            after(picks, gradb),
            early,
            [
                (0, half, 4),
                (half, half, 3),
                (2 * half, half, 5),
                (base, units, 4),
                (base + units, units, 5),
                (base + 2 * units, width, 3),
            ],
            adapters,
        )
        early = [whole_sum(t) for t in early]
        late = second_turn(turns)
        input_grad, *early_shared = pair_and_complete(spot, grad, grad_side, early[1:4], beside(early[0]))
        late = combine(
            spot,
            after(picks, grad_side, grad),
            late,
            [(n * half, half, n) for n in range(3)] + [(base + n * width, width, n) for n in range(3)],
            adapters,
        )
        late = [whole_sum(t) for t in late]
        late_shared = complete(spot, late[1:4], beside(late[0]))
        return (
            output,
            input_grad,
            flip(late_shared[0]),
            late[4],
            flip(late_shared[1]),
            late[5],
            flip(late_shared[2]),
            late[6],
            flip(early[6]),
            early_shared[1],
            flip(early_shared[0]),
            early[4],
            flip(early[5]),
            early_shared[2],
        )

    return body


def solution(mesh):
    placed = (
        P("dp", "tensor", None),
        P("dp", "tensor", None),
        P("dp"),
        P("dp", None),
        P(),
        P(),
        P(None, "tensor"),
        P(None, "tensor"),
        P(None, "tensor"),
        P("tensor", None),
        P(),
        P(),
        P(None, "tensor"),
        P("tensor", None),
        P(),
        P(None, None, "tensor"),
        P(),
        P(None, None, "tensor"),
        P(),
        P(None, None, "tensor"),
        P(None, "tensor", None),
        P(),
        P(),
        P(None, None, "tensor"),
        P(None, "tensor", None),
        P(),
    )
    return jax.shard_map(
        make_body(mesh.shape["dp"], mesh.shape["tensor"]),
        mesh=mesh,
        in_specs=placed,
        out_specs=(
            P("dp", "tensor", None),
            P("dp", "tensor", None),
            P(),
            P(None, None, "tensor"),
            P(),
            P(None, None, "tensor"),
            P(),
            P(None, None, "tensor"),
            P(None, "tensor", None),
            P(),
            P(),
            P(None, None, "tensor"),
            P(None, "tensor", None),
            P(),
        ),
        check_vma=False,
    )
```
